32 devices in a mesh: rep: 8 (over z, x), ep: 4 (over y, core).
Axes of the slice: x: 2, y: 2, z: 4, core: 2. Of those that a mesh axis runs over, the one named last changes fastest.
Arguments:
- tokens: bfloat16 [25216, 512], P(('rep', 'ep')), may hold values from -6 to 6
- ln1_gain: float32 [512], replicated, may hold values from 0.5 to 1.5
- w_qkv: bfloat16 [512, 1536], replicated, may hold values from -0.25 to 0.25
- w_proj: bfloat16 [512, 512], replicated, may hold values from -1.5 to 1.5
- ln2_gain: float32 [512], replicated, may hold values from 0.5 to 1.5
- w_router: bfloat16 [512, 8], replicated, may hold values from -0.1796875 to 0.1796875
- w_in: bfloat16 [8, 512, 2048], P('ep'), may hold values from -0.25 to 0.25
- w_out: bfloat16 [8, 2048, 512], P('ep'), may hold values from -0.75 to 0.75
- noise: float32 [25216, 8], P(('rep', 'ep')), may hold values from -1.8 to 1.8
- choices: int32 [25216, 2], P(('rep', 'ep')), may hold values from 0 to 7, as said below
- slots: int32 [25216, 2], P(('rep', 'ep')), may hold values from 0 to 246, as said below
- cotangent: bfloat16 [25216, 512], P(('rep', 'ep')), may hold values from -6 to 6
Outputs:
- output: bfloat16 [25216, 512], P(('rep', 'ep'))
- input_grad: float32 [25216, 512], P(('rep', 'ep'))
- ln1_gain_grad: float32 [512], replicated
- w_qkv_grad: float32 [512, 1536], replicated
- w_proj_grad: float32 [512, 512], replicated
- ln2_gain_grad: float32 [512], replicated
- w_router_grad: float32 [512, 8], replicated
- w_in_grad: float32 [8, 512, 2048], P('ep', 'rep')
- w_out_grad: float32 [8, 2048, 512], P('ep', 'rep')
The draws below stay inside these ranges and needn't reach their ends.
Inputs may be any that keep to these rules, and one draw needn't show every extreme that they name: `choices`: the two experts of a row differ. Within each aligned block of 788 rows, slots[t, c] counts the pairs naming the same expert that come before (t, c), where all first choices (c = 0) in row order come before all second choices, capped at 246; a pair with slot 246 is dropped.
All inputs are finite; a program needn't handle non-finite values.
Results may differ from the reference program's by a relative error of at most 0.015.
Values may be sent and summed in bfloat16 or wider, within the bound.
A program may use at most 192 MiB of HBM per device.

```python
import jax
import jax.numpy as jnp
from jax import lax

D = 512
HEADS = 8
HEAD_DIM = 64
FF = 2048
SEQ = 197
EXPERTS = 8
IMG_DEV = 4
TOK_DEV = 788
CAP = 246
TOKENS = 25216
N_EP = 4
DEVICES = 32


def route_table(key):
    group_hot = jax.random.randint(jax.random.fold_in(key, 11), (DEVICES // N_EP,), 0, EXPERTS)
    hot_expert = jnp.repeat(group_hot, N_EP)
    block_keys = jax.random.split(jax.random.fold_in(key, 12), DEVICES)
    hot_count = CAP + TOK_DEV // 16
    labels = jnp.arange(EXPERTS, dtype=jnp.int32)

    def one_block(block_key, hot_one):
        first_key, second_key, third_key = jax.random.split(block_key, 3)
        shuffled = jax.random.permutation(first_key, TOK_DEV)
        others = (hot_one + 1 + jax.random.randint(second_key, (TOK_DEV,), 0, EXPERTS - 1)) % EXPERTS
        first_pick = jnp.where(shuffled < hot_count, hot_one, others).astype(jnp.int32)
        second_pick = ((first_pick + 1 + jax.random.randint(third_key, (TOK_DEV,), 0, EXPERTS - 1)) % EXPERTS).astype(jnp.int32)
        first_hits = (first_pick[:, None] == labels[None, :]).astype(jnp.int32)
        second_hits = (second_pick[:, None] == labels[None, :]).astype(jnp.int32)
        first_rank = jnp.cumsum(first_hits, 0) - first_hits
        second_rank = jnp.cumsum(second_hits, 0) - second_hits + jnp.sum(first_hits, 0)[None, :]
        first_slot = jnp.sum(first_rank * first_hits, 1)
        second_slot = jnp.sum(second_rank * second_hits, 1)
        route_picks = jnp.stack([first_pick, second_pick], 1).astype(jnp.int32)
        slot_values = jnp.minimum(jnp.stack([first_slot, second_slot], 1), CAP).astype(jnp.int32)
        return (route_picks, slot_values)
    route_picks, slot_values = jax.vmap(one_block)(block_keys, hot_expert)
    return (route_picks.reshape(TOKENS, 2), slot_values.reshape(TOKENS, 2))


def draw_choices(key, part):
    route_picks, slot_values = route_table(key)
    return route_picks


def draw_slots(key, part):
    route_picks, slot_values = route_table(key)
    return slot_values


def level_of(key, dims, cuts, smallest, high):
    loudness, own = 1.0, jax.random.fold_in(key, 6)
    for position, shards_of in cuts:
        draws = jnp.exp(jax.random.uniform(jax.random.fold_in(own, position), (shards_of,), jnp.float32, smallest / len(cuts), high / len(cuts)))
        loudness = loudness * jnp.repeat(draws, dims[position] // shards_of).reshape([-1 if axis == position else 1 for axis in range(len(dims))])
    return loudness


def centred(key, extent, deviation, bound, cuts=(), held_as=jnp.bfloat16):
    values = deviation * jax.random.normal(key, extent, jnp.float32)
    if cuts:
        values = values * level_of(key, extent, cuts, -0.22, 0.18)
    return jnp.clip(values, -bound, bound).astype(held_as)


def setup_inputs(seed: int = 0) -> dict:
    splits = jax.random.split(jax.random.key(seed), 13)
    return {
        "tokens": centred(splits[0], (TOKENS, D), 1.0, 6.0, ((0, 32),)),
        "ln1_gain": jnp.clip(1.0 + 0.1 * jax.random.normal(splits[1], (D,), jnp.float32), 0.5, 1.5),
        "w_qkv": centred(splits[2], (D, 3 * D), D ** -0.5, 0.25),
        "w_proj": centred(splits[3], (D, D), (D // 32) ** -0.5, 1.5),
        "ln2_gain": jnp.clip(1.0 + 0.1 * jax.random.normal(splits[4], (D,), jnp.float32), 0.5, 1.5),
        "w_router": centred(splits[5], (D, EXPERTS), 0.03, 0.1796875),
        "w_in": centred(splits[6], (EXPERTS, D, FF), D ** -0.5, 0.25, ((0, 4),)),
        "w_out": centred(splits[7], (EXPERTS, FF, D), (FF // 32) ** -0.5, 0.75, ((0, 4),)),
        "noise": centred(splits[8], (TOKENS, EXPERTS), 0.3, 1.8, ((0, 32),), jnp.float32),
        "choices": draw_choices(jax.random.fold_in(splits[12], 71), 0),
        "slots": draw_slots(jax.random.fold_in(splits[12], 71), 0),
        "cotangent": centred(splits[11], (TOKENS, D), 1.0, 6.0, ((0, 32),)),
    }


@jax.custom_vjp
def low(v):
    return lax.optimization_barrier(v.astype(jnp.bfloat16)).astype(jnp.float32)

@jax.custom_vjp
def low_back(v):
    return v

def low_keep(v):
    return (low(v), None)

def low_pass(kept, grad):
    return (grad,)

def back_keep(v):
    return (v, None)

def back_low(kept, grad):
    return (low(grad),)
low.defvjp(low_keep, low_pass)
low_back.defvjp(back_keep, back_low)
epsilon = 1e-06
highest = lax.Precision.HIGHEST

def layer_norm(source, gain_row):
    row_mean = lax.optimization_barrier(jnp.mean(source, -1, keepdims=True))
    centered = source - row_mean
    spread = lax.optimization_barrier(jnp.mean(centered * centered, -1, keepdims=True))
    return centered * lax.rsqrt(spread + epsilon) * gain_row

def block_forward(params, source, noise_rows, choice_rows, slot_rows):
    ln1_gain, w_qkv, w_proj, ln2_gain, w_router, w_in, w_out = params
    score_scale = HEAD_DIM ** (-0.5)
    normed = low(layer_norm(source, ln1_gain))
    projected = low_back(low(jnp.dot(normed, w_qkv, precision=highest)))
    queries = projected[:, :D].reshape(IMG_DEV, SEQ, HEADS, HEAD_DIM)
    keys_all = projected[:, D:2 * D].reshape(IMG_DEV, SEQ, HEADS, HEAD_DIM)
    values_all = projected[:, 2 * D:].reshape(IMG_DEV, SEQ, HEADS, HEAD_DIM)
    scores = low_back(jnp.einsum('ishd,ithd->ihst', queries, keys_all, precision=highest) * score_scale)
    attention = low(jax.nn.softmax(scores, -1))
    attended = jnp.einsum('ihst,ithd->ishd', attention, values_all, precision=highest).reshape(TOK_DEV, D)
    attended = low_back(low(attended))
    residual = source + low_back(jnp.dot(attended, w_proj, precision=highest))
    hidden = low(layer_norm(residual, ln2_gain))
    logits = low_back(jnp.dot(hidden, w_router, precision=highest)) + noise_rows
    gates = jax.nn.softmax(logits, -1)
    picked_gate = jnp.take_along_axis(gates, choice_rows, 1)
    kept_pair = slot_rows < CAP
    slot_index = jnp.where(kept_pair, choice_rows * CAP + slot_rows, EXPERTS * CAP).astype(jnp.int32)
    read_index = jnp.minimum(slot_index, EXPERTS * CAP - 1).astype(jnp.int32)
    spread_rows = jnp.broadcast_to(hidden[:, None, :], (TOK_DEV, 2, D)).reshape(TOK_DEV * 2, D)
    buffer = jnp.zeros((EXPERTS * CAP, D), jnp.float32).at[slot_index.reshape(-1)].set(spread_rows, mode='drop')
    buffer = low_back(buffer.reshape(EXPERTS, CAP, D))
    hidden_pre = low_back(jnp.einsum('ecd,edf->ecf', buffer, w_in, precision=highest))
    hidden_act = low(jax.nn.gelu(hidden_pre))
    expert_out = low_back(low(jnp.einsum('ecf,efd->ecd', hidden_act, w_out, precision=highest)))
    gathered = expert_out.reshape(EXPERTS * CAP, D)[read_index]
    pair_gate = picked_gate * kept_pair.astype(jnp.float32)
    return residual + lax.optimization_barrier(jnp.sum(pair_gate[..., None] * gathered, 1))

def forward(source, params, noise, choices, slots):

    def scan_step(state_none, pieces):
        block_source, block_noise, block_choice, block_slot = pieces
        return (state_none, jax.checkpoint(block_forward)(params, block_source, block_noise, block_choice, block_slot))
    pieces = (source.reshape(DEVICES, TOK_DEV, D), noise.reshape(DEVICES, TOK_DEV, EXPERTS), choices.reshape(DEVICES, TOK_DEV, 2), slots.reshape(DEVICES, TOK_DEV, 2))
    state_none, blocks = lax.scan(scan_step, None, pieces)
    return blocks.reshape(TOKENS, D)

def reference(tokens, ln1_gain, w_qkv, w_proj, ln2_gain, w_router, w_in, w_out, noise, choices, slots, cotangent):
    source = tokens.astype(jnp.float32)
    params = (ln1_gain.astype(jnp.float32), w_qkv.astype(jnp.float32), w_proj.astype(jnp.float32), ln2_gain.astype(jnp.float32), w_router.astype(jnp.float32), w_in.astype(jnp.float32), w_out.astype(jnp.float32))
    noise_f = noise.astype(jnp.float32)

    def wrapped(source_arg, params_arg):
        return forward(source_arg, params_arg, noise_f, choices, slots)
    result, pullback = jax.vjp(wrapped, source, params)
    input_grad, grads = pullback(cotangent.astype(jnp.float32))
    return (result.astype(jnp.bfloat16), input_grad, grads[0], grads[1], grads[2], grads[3], grads[4], grads[5], grads[6])
```

```python
import functools

import jax
import jax.numpy as jnp
from jax import lax
from jax.experimental import pallas as pl
from jax.experimental.pallas import tpu as pltpu
from jax.sharding import PartitionSpec as P

HEADS = 8
HEAD_DIM = 64
SEQ = 197
CAP = 246


epsilon = 1e-06


def layer_norm(source, gain_row):
    row_mean = jnp.mean(source, -1, keepdims=True)
    centered = source - row_mean
    spread = jnp.mean(centered * centered, -1, keepdims=True)
    return centered * lax.rsqrt(spread + epsilon) * gain_row


def expert_hidden(arrived, w_in):
    hidden_pre = jnp.einsum("jrd,jdf->jrf", arrived, w_in, preferred_element_type=jnp.float32)
    return (hidden_pre, jax.nn.gelu(hidden_pre).astype(jnp.bfloat16))


def local(
    tokens,
    ln1_gain,
    w_qkv,
    w_proj,
    ln2_gain,
    w_router,
    w_in,
    w_out,
    noise,
    choices,
    slots,
    cotangent,
):
    row_count, model_width = tokens.shape
    experts_all = w_router.shape[1]
    images = row_count // SEQ
    score_scale = HEAD_DIM ** (-0.5)
    source = tokens.astype(jnp.float32)
    normed, norm1_back = jax.vjp(layer_norm, source, ln1_gain)
    normed_low = normed.astype(jnp.bfloat16)
    projected = jnp.dot(normed_low, w_qkv, preferred_element_type=jnp.float32).astype(jnp.bfloat16)

    def heads_of(columns):
        return columns.reshape(images, SEQ, HEADS, HEAD_DIM)

    queries = heads_of(projected[:, :model_width])
    keys_all = heads_of(projected[:, model_width : 2 * model_width])
    values_all = heads_of(projected[:, 2 * model_width :])
    scores = (
        jnp.einsum("ishd,ithd->ihst", queries, keys_all, preferred_element_type=jnp.float32)
        * score_scale
    )
    logsum = jax.nn.logsumexp(scores, -1, keepdims=True)
    attention = jnp.exp(scores - logsum).astype(jnp.bfloat16)
    attended = jnp.einsum(
        "ihst,ithd->ishd", attention, values_all, preferred_element_type=jnp.float32
    )
    attended = attended.reshape(row_count, model_width).astype(jnp.bfloat16)
    residual = source + jnp.dot(attended, w_proj, preferred_element_type=jnp.float32)
    normed2, norm2_back = jax.vjp(layer_norm, residual, ln2_gain)
    hidden = normed2.astype(jnp.bfloat16)
    logits = jnp.dot(hidden, w_router, preferred_element_type=jnp.float32)

    def routing(logit_rows):
        return jnp.take_along_axis(jax.nn.softmax(logit_rows + noise, -1), choices, 1)

    picked_gate, routing_back = jax.vjp(routing, logits)
    kept_pair = slots < CAP
    kept_float = kept_pair.astype(jnp.float32)
    slot_index = jnp.where(kept_pair, choices * CAP + slots, experts_all * CAP)
    read_index = jnp.minimum(slot_index, experts_all * CAP - 1)
    pair_gate = picked_gate * kept_float

    def place(pair_rows):
        flat_rows = pair_rows.reshape(row_count * 2, model_width)
        filled = (
            jnp.zeros((experts_all * CAP, model_width), jnp.bfloat16)
            .at[slot_index.reshape(-1)]
            .set(flat_rows, mode="drop")
        )
        return filled.reshape(experts_all, CAP, model_width)

    hidden_pairs = jnp.broadcast_to(hidden[:, None, :], (row_count, 2, model_width))
    arrived = lax.all_to_all(place(hidden_pairs), "ep", split_axis=0, concat_axis=1, tiled=True)
    hidden_pre, hidden_act = expert_hidden(arrived, w_in)
    expert_out = jnp.einsum(
        "jrf,jfd->jrd", hidden_act, w_out, preferred_element_type=jnp.float32
    ).astype(jnp.bfloat16)
    returned = lax.all_to_all(expert_out, "ep", split_axis=1, concat_axis=0, tiled=True).reshape(
        experts_all * CAP, model_width
    )
    gathered = returned[read_index].astype(jnp.float32)
    output = residual + jnp.sum(pair_gate[..., None] * gathered, 1)
    upstream = cotangent.astype(jnp.float32)
    d_gate = jnp.sum(upstream[:, None, :] * gathered, -1) * kept_float
    d_pairs = (pair_gate[..., None] * upstream[:, None, :]).astype(jnp.bfloat16)
    grad_rows = lax.all_to_all(place(d_pairs), "ep", split_axis=0, concat_axis=1, tiled=True)
    again_rows, again_pre, again_act = (arrived, hidden_pre, hidden_act)
    d_act = jnp.einsum("jrd,jfd->jrf", grad_rows, w_out, preferred_element_type=jnp.float32)
    gelu_back = jax.vjp(jax.nn.gelu, again_pre)[1]
    d_pre = gelu_back(d_act)[0].astype(jnp.bfloat16)
    d_w_out = jnp.einsum("jrf,jrd->jfd", again_act, grad_rows, preferred_element_type=jnp.float32)
    d_w_in = jnp.einsum("jrd,jrf->jdf", again_rows, d_pre, preferred_element_type=jnp.float32)
    in_share, out_share = (
        lax.psum_scatter(d_w_in, "rep", scatter_dimension=1, tiled=True),
        lax.psum_scatter(d_w_out, "rep", scatter_dimension=1, tiled=True),
    )
    d_rows = jnp.einsum("jrf,jdf->jrd", d_pre, w_in, preferred_element_type=jnp.float32).astype(
        jnp.bfloat16
    )
    d_back = lax.all_to_all(d_rows, "ep", split_axis=1, concat_axis=0, tiled=True).reshape(
        experts_all * CAP, model_width
    )
    d_hidden = jnp.sum(d_back[read_index].astype(jnp.float32) * kept_float[..., None], 1)
    d_logits = routing_back(d_gate)[0].astype(jnp.bfloat16)
    d_w_router = jnp.einsum("td,te->de", hidden, d_logits, preferred_element_type=jnp.float32)
    d_hidden = d_hidden + jnp.einsum(
        "te,de->td", d_logits, w_router, preferred_element_type=jnp.float32
    )
    d_resid_part, d_gain2 = norm2_back(d_hidden)
    d_residual = upstream + d_resid_part
    d_branch = d_residual.astype(jnp.bfloat16)
    d_w_proj = jnp.einsum("td,te->de", attended, d_branch, preferred_element_type=jnp.float32)
    d_attended = jnp.einsum("te,de->td", d_branch, w_proj, preferred_element_type=jnp.float32)
    d_attended = heads_of(d_attended.astype(jnp.bfloat16))
    rescored = (
        jnp.einsum("ishd,ithd->ihst", queries, keys_all, preferred_element_type=jnp.float32)
        * score_scale
    )
    probability = jnp.exp(rescored - logsum)
    d_prob = jnp.einsum(
        "ishd,ithd->ihst", d_attended, values_all, preferred_element_type=jnp.float32
    )
    d_values = jnp.einsum(
        "ihst,ishd->ithd",
        probability.astype(jnp.bfloat16),
        d_attended,
        preferred_element_type=jnp.float32,
    )
    d_scores = (probability * (d_prob - jnp.sum(probability * d_prob, -1, keepdims=True))).astype(
        jnp.bfloat16
    )
    d_queries = (
        jnp.einsum("ihst,ithd->ishd", d_scores, keys_all, preferred_element_type=jnp.float32)
        * score_scale
    )
    d_keys = (
        jnp.einsum("ihst,ishd->ithd", d_scores, queries, preferred_element_type=jnp.float32)
        * score_scale
    )
    d_projected = jnp.concatenate(
        [
            d_queries.reshape(row_count, model_width),
            d_keys.reshape(row_count, model_width),
            d_values.reshape(row_count, model_width),
        ],
        1,
    ).astype(jnp.bfloat16)
    d_w_qkv = jnp.einsum("td,te->de", normed_low, d_projected, preferred_element_type=jnp.float32)
    d_normed = jnp.einsum("te,de->td", d_projected, w_qkv, preferred_element_type=jnp.float32)
    d_source_part, d_gain1 = norm1_back(d_normed)
    input_grad = d_residual + d_source_part
    dense_sums = lax.psum((d_gain1, d_w_qkv, d_w_proj, d_gain2, d_w_router), ("rep", "ep"))
    return (
        output.astype(jnp.bfloat16),
        input_grad,
        dense_sums[0],
        dense_sums[1],
        dense_sums[2],
        dense_sums[3],
        dense_sums[4],
        in_share,
        out_share,
    )


IMAGES = 4
PAD = 208
ROWS = IMAGES * PAD
WIDTH = 512
PAIRS = 4
SLOT_PAD = 256
PLACES = 4 * SLOT_PAD
CHUNK = 256
CHUNKS = 8
UNITS = 8
SHARE_IN = 64
MESH = pl.DeviceIdType.MESH
bf16 = jnp.bfloat16
f32 = jnp.float32


def dot(a, b):
    return jnp.dot(a, b, preferred_element_type=f32)


def dot_nt(a, b):
    return lax.dot_general(a, b, (((1,), (1,)), ((), ())), preferred_element_type=f32)


def dot_tn(a, b):
    return lax.dot_general(a, b, (((0,), (0,)), ((), ())), preferred_element_type=f32)


def normalized(source):
    centered = source - jnp.mean(source, -1, keepdims=True)
    scale = lax.rsqrt(jnp.mean(centered * centered, -1, keepdims=True) + epsilon)
    return centered * scale, scale


def norm_back(unit, scale, gain_row, grad):
    d_unit = grad * gain_row
    return scale * (
        d_unit
        - jnp.mean(d_unit, -1, keepdims=True)
        - unit * jnp.mean(d_unit * unit, -1, keepdims=True)
    )


def remote(src, dst, send, recv, device):
    return pltpu.make_async_remote_copy(
        src_ref=src, dst_ref=dst, send_sem=send, recv_sem=recv, device_id=device, device_id_type=MESH
    )


def block_kernel(
    tok, cot, gain1, gain2, wqkv, wproj, wrt, meta_in, w_in, w_out,
    out, ig, qkv_g, proj_g, small_g, win_g, wout_g,
    padf, tok_p, dy_own, hid_own, proj, att, resid, da_temp, gates, meta, hid_all, dy_all,
    buf_x, buf_g, buf_y, wi_buf, wo_buf, act_s, dpre_s, acc_o, acc_r,
    dwi, dwo, ri1, ri2, ri3, ro1, ro2, ro3,
    rret1, rret2, dgp, rdg1, rdg2, rg, sm, rsm,
    w_sem, o_sem, li_sem, lo_sem, ag_s, ag_r, m_s, m_r, p1_s, p1_r, p2_s, p2_r, q1_s, q1_r, q2_s, q2_r,
    di_s, di_r, do1_s, do1_r, do2_s, do2_r, do3_s, do3_r, ar_s, ar_r, sr_s, sr_r,
):
    rep = lax.axis_index("rep")
    ep = lax.axis_index("ep")
    core = lax.rem(ep, 2)
    yy = ep // 2
    bx = lax.rem(rep, 2)
    bz = lax.rem(rep // 2, 2)
    bw = rep // 4
    mate_e = ep + 1 - 2 * core
    mirror_e = ep + 2 - 4 * yy
    diag_e = mate_e + 2 - 4 * yy
    mate = (rep, mate_e)
    mirror = (rep, mirror_e)
    dev_x = (rep + 1 - 2 * bx, ep)
    dev_z = (rep + 2 - 4 * bz, ep)
    dev_w = (rep + 4 - 8 * bw, ep)

    barrier = pltpu.get_barrier_semaphore()
    for device in (mate, mirror, dev_x, dev_z, dev_w):
        pl.semaphore_signal(barrier, inc=1, device_id=device, device_id_type=MESH)
    pl.semaphore_wait(barrier, 5)

    def image_rows(i):
        return pl.ds(pl.multiple_of(i * PAD, 16), PAD)

    row_id = lax.broadcasted_iota(jnp.int32, (PAD, WIDTH), 0)

    def pad_rows(put):
        padf[784:800, :] = jnp.zeros((16, WIDTH), f32)
        padf[0:788, :] = out[...].astype(f32)
        for i in range(IMAGES):
            value = padf[SEQ * i : SEQ * i + PAD, :]
            put(i, jnp.where(row_id < SEQ, value, 0.0).astype(bf16))

    def put_tok(i, value):
        tok_p[i * PAD : (i + 1) * PAD, :] = value

    def put_dy(i, value):
        dy_own[i * PAD : (i + 1) * PAD, :] = value

    for source, put in ((cot, put_dy), (tok, put_tok)):
        fetch = pltpu.make_async_copy(source, out, o_sem.at[0])
        fetch.start()
        fetch.wait()
        pad_rows(put)

    stores = (dy_own, hid_own)
    gathered = (dy_all, hid_all)

    def gather_send(kind, i):
        rows = image_rows(i)
        for route, device in ((0, mate), (1, mirror)):
            remote(
                stores[kind].at[rows], gathered[kind].at[ep, rows],
                ag_s.at[kind, route, i], ag_r.at[kind, route, i], device,
            ).start()

    def gather_forward(kind, i):
        rows = image_rows(i)
        here = gathered[kind].at[mirror_e, rows]
        remote(here, here, ag_s.at[kind, 1, i], ag_r.at[kind, 1, i], mirror).wait_recv()
        remote(here, here, ag_s.at[kind, 2, i], ag_r.at[kind, 2, i], mate).start()

    def gather_finish(kind, i):
        rows = image_rows(i)
        for route, who in ((0, mate_e), (2, diag_e)):
            here = gathered[kind].at[who, rows]
            remote(here, here, ag_s.at[kind, route, i], ag_r.at[kind, route, i], mate).wait_recv()
        for route in range(3):
            here = stores[kind].at[rows]
            remote(here, here, ag_s.at[kind, route, i], ag_r.at[kind, route, i], mate).wait_send()

    def weights(step):
        el = step // CHUNKS
        start = pl.multiple_of(lax.rem(step, CHUNKS) * CHUNK, CHUNK)
        slot = lax.rem(step, 2)
        return (
            pltpu.make_async_copy(w_in.at[el, :, pl.ds(start, CHUNK)], wi_buf.at[slot], w_sem.at[0, slot]),
            pltpu.make_async_copy(w_out.at[el, pl.ds(start, CHUNK), :], wo_buf.at[slot], w_sem.at[1, slot]),
        )

    for copy in weights(0):
        copy.start()

    lane = lax.broadcasted_iota(jnp.int32, (1, 128), 1)
    masks = ((lane < HEAD_DIM).astype(f32).astype(bf16), (lane >= HEAD_DIM).astype(f32).astype(bf16))
    key_col = lax.broadcasted_iota(jnp.int32, (PAD, PAD), 1)
    score_scale = HEAD_DIM ** (-0.5)

    def softmax_of(queries, keys):
        scores = jnp.where(key_col < SEQ, dot_nt(queries, keys), -1e30)
        weight = jnp.exp(scores - jnp.max(scores, -1, keepdims=True))
        return weight / jnp.sum(weight, -1, keepdims=True)

    def columns(part, pair):
        start = part * WIDTH + pair * 128
        return slice(start, start + 128)

    def forward_image(i, carry):
        rows = image_rows(i)
        gather_send(0, i)
        source = tok_p[rows, :].astype(f32)
        unit, _ = normalized(source)
        normed = (unit * gain1[...]).astype(bf16)
        for part in range(3):
            cols = slice(part * WIDTH, (part + 1) * WIDTH)
            proj[rows, cols] = dot(normed, wqkv[:, cols]).astype(bf16)
        for pair in range(PAIRS):
            queries = proj[rows, columns(0, pair)] * jnp.array(score_scale, bf16)
            keys = proj[rows, columns(1, pair)]
            values = proj[rows, columns(2, pair)]
            total = None
            for mask in masks:
                attention = softmax_of(queries, keys * mask).astype(bf16)
                term = dot(attention, values * mask)
                total = term if total is None else total + term
            att[rows, columns(0, pair)] = total.astype(bf16)
        residual = source + dot(att[rows, :], wproj[...])
        resid[rows, :] = residual
        unit2, _ = normalized(residual)
        hid_own[rows, :] = (unit2 * gain2[...]).astype(bf16)
        gather_send(1, i)

        @pl.when(i >= 1)
        def _():
            gather_forward(0, i - 1)

        @pl.when(i >= 2)
        def _():
            gather_forward(1, i - 2)

        return carry

    lax.fori_loop(0, IMAGES, forward_image, 0)

    expert_id = lax.broadcasted_iota(jnp.int32, (8, ROWS), 0).astype(f32)

    def picks():
        return [(expert_id == meta_in[8 + c : 9 + c, :]).astype(f32) for c in range(2)]

    logits = dot_nt(wrt[...], hid_own[...]) + meta_in[0:8, :]
    gate_top = jnp.exp(logits - jnp.max(logits, 0, keepdims=True))
    gate_rows = gate_top / jnp.sum(gate_top, 0, keepdims=True)
    gates[...] = gate_rows
    meta[ep] = jnp.zeros((8, ROWS), f32)
    for c, hot in enumerate(picks()):
        slot = meta_in[10 + c : 11 + c, :]
        kept = slot < CAP
        chosen = meta_in[8 + c : 9 + c, :]
        meta[ep, c : c + 1, :] = jnp.where(kept, chosen * SLOT_PAD + slot, -1.0)
        meta[ep, 2 + c : 3 + c, :] = jnp.where(kept, jnp.sum(gate_rows * hot, 0, keepdims=True), 0.0)
    for route, device in ((0, mate), (1, mirror)):
        remote(meta.at[ep], meta.at[ep], m_s.at[route], m_r.at[route], device).start()
    dy_all[ep] = dy_own[...]
    hid_all[ep] = hid_own[...]
    gather_forward(0, 3)
    gather_forward(1, 2)
    gather_forward(1, 3)
    here = meta.at[mirror_e]
    remote(here, here, m_s.at[1], m_r.at[1], mirror).wait_recv()
    remote(here, here, m_s.at[2], m_r.at[2], mate).start()
    for kind in range(2):
        for i in range(IMAGES):
            gather_finish(kind, i)
    for route, who in ((0, mate_e), (2, diag_e)):
        remote(meta.at[who], meta.at[who], m_s.at[route], m_r.at[route], mate).wait_recv()
    for route in range(3):
        remote(meta.at[ep], meta.at[ep], m_s.at[route], m_r.at[route], mate).wait_send()

    slot_id = lax.broadcasted_iota(jnp.int32, (SLOT_PAD, ROWS), 0)

    def hits(s, el):
        first = (2 * ep + el) * SLOT_PAD
        place = (slot_id + first).astype(f32)
        return place == meta[s, 0:1, :], place == meta[s, 1:2, :]

    def hot_of(hit):
        return jnp.where(hit[0] | hit[1], 1.0, 0.0).astype(bf16)

    def slot_gate(s, hit):
        weight = jnp.where(hit[0], meta[s, 2:3, :], 0.0) + jnp.where(hit[1], meta[s, 3:4, :], 0.0)
        return jnp.sum(weight, -1, keepdims=True)

    def slot_rows(s, el):
        return pl.ds(pl.multiple_of(el * PLACES + s * SLOT_PAD, SLOT_PAD), SLOT_PAD)

    def place_source(s, carry):
        for el in range(2):
            hit = hits(s, el)
            hot = hot_of(hit)
            rows = slot_rows(s, el)
            buf_x[rows, :] = dot(hot, hid_all[s]).astype(bf16)
            placed = dot(hot, dy_all[s])
            buf_y[rows, :] = placed.astype(bf16)
            buf_g[rows, :] = (slot_gate(s, hit) * placed).astype(bf16)
        return carry

    lax.fori_loop(0, 4, place_source, 0)

    def unit_parts(u):
        el = u // 4
        j = lax.rem(u, 4)
        even = el * CHUNKS + 2 * j
        return el, j, even

    def copy_a1(u):
        el, j, even = unit_parts(u)
        return (
            remote(dwo.at[el, j // 2, lax.rem(j, 2), 1 - bx], ro1.at[u], do1_s.at[u], do1_r.at[u], dev_x),
            remote(dwi.at[even, :, :, 1 - bx], ri1.at[even], di_s.at[0, 0, u], di_r.at[0, 0, u], dev_x),
            remote(dwi.at[even + 1, :, 1 - bz, :], ri1.at[even + 1], di_s.at[1, 0, u], di_r.at[1, 0, u], dev_z),
        )

    def copy_a2(u):
        el, j, even = unit_parts(u)
        return (
            remote(dwi.at[even, :, 1 - bz, bx], ri2.at[even], di_s.at[0, 1, u], di_r.at[0, 1, u], dev_z),
            remote(dwi.at[even + 1, :, bz, 1 - bx], ri2.at[even + 1], di_s.at[1, 1, u], di_r.at[1, 1, u], dev_x),
        )

    def copy_o2(el, hi):
        return remote(
            dwo.at[el, hi, 1 - bz, bx], ro2.at[el, hi], do2_s.at[el, hi], do2_r.at[el, hi], dev_z
        )

    def copy_a3(u):
        el, j, even = unit_parts(u)
        return tuple(
            remote(
                dwi.at[even + odd, 1 - bw, bz, bx], ri3.at[even + odd],
                di_s.at[odd, 2, u], di_r.at[odd, 2, u], dev_w,
            )
            for odd in range(2)
        )

    def copy_o3(el):
        return remote(dwo.at[el, 1 - bw, bz, bx], ro3.at[el], do3_s.at[el], do3_r.at[el], dev_w)

    def leave_in(u):
        el, j, even = unit_parts(u)
        rows = pl.ds(pl.multiple_of(u * SHARE_IN, SHARE_IN), SHARE_IN)
        cols = pl.ds(pl.multiple_of(j * 2 * CHUNK, 2 * CHUNK), 2 * CHUNK)
        return pltpu.make_async_copy(acc_r.at[rows], win_g.at[el, :, cols], li_sem.at[u])

    def leave_out(el):
        rows = pl.ds(pl.multiple_of(WIDTH + el * CHUNK, CHUNK), CHUNK)
        return pltpu.make_async_copy(acc_r.at[rows], wout_g.at[el], lo_sem.at[el])

    def stage1(u):
        for copy in copy_a1(u):
            copy.start()

    def plus(a, b):
        return (a.astype(f32) + b.astype(f32)).astype(bf16)

    def stage2(u):
        el, j, even = unit_parts(u)
        for copy in copy_a1(u):
            copy.wait_recv()
        dwi[even, :, :, bx] = plus(dwi[even, :, :, bx], ri1[even])
        dwi[even + 1, :, bz] = plus(dwi[even + 1, :, bz], ri1[even + 1])
        for copy in copy_a2(u):
            copy.start()
        dwo[el, j // 2, lax.rem(j, 2), bx] = plus(dwo[el, j // 2, lax.rem(j, 2), bx], ro1[u])

        @pl.when(lax.rem(j, 2) == 1)
        def _():
            copy_o2(el, j // 2).start()

    def stage3(u):
        el, j, even = unit_parts(u)
        for copy in copy_a2(u):
            copy.wait_recv()
        for odd in range(2):
            dwi[even + odd, :, bz, bx] = plus(dwi[even + odd, :, bz, bx], ri2[even + odd])
        for copy in copy_a3(u):
            copy.start()

        @pl.when(lax.rem(j, 2) == 1)
        def _():
            hi = j // 2
            copy_o2(el, hi).wait_recv()
            dwo[el, hi, bz, bx] = plus(dwo[el, hi, bz, bx], ro2[el, hi])

        @pl.when(j == 3)
        def _():
            copy_o3(el).start()

    def stage4(u):
        el, j, even = unit_parts(u)
        for copy in copy_a3(u):
            copy.wait_recv()
        rows = pl.ds(pl.multiple_of(u * SHARE_IN, SHARE_IN), SHARE_IN)
        for odd in range(2):
            cols = slice(odd * CHUNK, (odd + 1) * CHUNK)
            acc_r[rows, cols] = dwi[even + odd, bw, bz, bx].astype(f32) + ri3[even + odd].astype(f32)
        leave_in(u).start()

        @pl.when(j == 3)
        def _():
            copy_o3(el).wait_recv()
            rows = pl.ds(pl.multiple_of(WIDTH + el * CHUNK, CHUNK), CHUNK)
            acc_r[rows, :] = dwo[el, bw, bz, bx].astype(f32) + ro3[el].astype(f32)
            leave_out(el).start()

    gelu_a = 0.7978845608028654
    gelu_b = gelu_a * 0.044715

    def expert_step(step, carry):
        el = step // CHUNKS
        k = lax.rem(step, CHUNKS)
        slot = lax.rem(step, 2)
        for copy in weights(step):
            copy.wait()

        @pl.when(step + 1 < 2 * CHUNKS)
        def _():
            for copy in weights(step + 1):
                copy.start()

        @pl.when(k == 0)
        def _():
            acc_o[...] = jnp.zeros((PLACES, WIDTH), f32)
            acc_r[...] = jnp.zeros((PLACES, WIDTH), f32)

        wi = wi_buf[slot]
        wo = wo_buf[slot]
        first = pl.multiple_of(el * PLACES, PLACES)
        for part in range(4):
            rows = slice(part * 256, (part + 1) * 256)
            far = pl.ds(pl.multiple_of(first + part * 256, 256), 256)
            pre = dot(buf_x[far, :], wi)
            square = pre * pre
            level = jnp.tanh(pre * (gelu_a + gelu_b * square))
            half = 0.5 + 0.5 * level
            act = (pre * half).astype(bf16)
            slope = half + (0.5 * pre) * (1.0 - level * level) * (gelu_a + 3.0 * gelu_b * square)
            d_act = dot_nt(buf_g[far, :], wo)
            d_pre = (d_act * slope).astype(bf16)
            act_s[rows, :] = act
            dpre_s[rows, :] = d_pre
            acc_o[rows, :] += dot(act, wo)
            acc_r[rows, :] += dot_nt(d_pre, wi)
        whole = pl.ds(first, PLACES)
        dwo[el, k // 4, lax.rem(k // 2, 2), lax.rem(k, 2)] = dot_tn(act_s[...], buf_g[whole, :]).astype(bf16)
        grad_in = dot_tn(buf_x[whole, :], dpre_s[...]).astype(bf16)
        dwi[step] = grad_in.reshape(2, 2, 2, SHARE_IN, CHUNK)

        @pl.when(lax.rem(step, 2) == 1)
        def _():
            u = step // 2
            stage1(u)

            @pl.when(jnp.logical_and(lax.rem(u, 2) == 1, u >= 3))
            def _():
                v = (u - 3) // 2
                stage2(v)

                @pl.when(v >= 1)
                def _():
                    stage3(v - 1)

        @pl.when(k == CHUNKS - 1)
        def _():
            buf_x[whole, :] = acc_o[...].astype(bf16)
            buf_g[whole, :] = acc_r[...].astype(bf16)

        return carry

    lax.fori_loop(0, 2 * CHUNKS, expert_step, 0)

    partial = (dy_all, hid_all)

    def ret_one(kind, which, who):
        return remote(partial[kind].at[who], rret1.at[kind, which], p1_s.at[kind, which], p1_r.at[kind, which], mate)

    def ret_two(kind, i):
        rows = image_rows(i)
        return remote(partial[kind].at[mirror_e, rows], rret2.at[kind, rows], p2_s.at[kind, i], p2_r.at[kind, i], mirror)

    def gate_one(which, who):
        return remote(dgp.at[who], rdg1.at[which], q1_s.at[which], q1_r.at[which], mate)

    def gate_two():
        return remote(dgp.at[mirror_e], rdg2, q2_s, q2_r, mirror)

    def return_source(index, carry):
        flip_y = 1 - index // 2
        flip_c = 1 - lax.rem(index, 2)
        s = 2 * (yy + flip_y - 2 * flip_y * yy) + core + flip_c - 2 * flip_c * core
        gate_total = [None, None]
        turned = (act_s, dpre_s)
        for el in range(2):
            hit = hits(s, el)
            rows = slot_rows(s, el)
            turned[el][0:ROWS, :] = hot_of(hit).T
            result = buf_x[rows, :].astype(f32)
            d_slot = jnp.sum(result * buf_y[rows, :].astype(f32), -1, keepdims=True)
            buf_x[rows, :] = (slot_gate(s, hit) * result).astype(bf16)
            for c in range(2):
                term = jnp.sum(jnp.where(hit[c], d_slot, 0.0), 0, keepdims=True)
                gate_total[c] = term if el == 0 else gate_total[c] + term
        for target, source in ((dy_all, buf_g), (hid_all, buf_x)):
            for i in range(IMAGES):
                rows = slice(i * PAD, (i + 1) * PAD)
                value = dot(act_s[rows, :], source[slot_rows(s, 0), :]) + dot(dpre_s[rows, :], source[slot_rows(s, 1), :])
                target[s, rows, :] = value.astype(bf16)
        dgp[s] = jnp.zeros((8, ROWS), f32)
        for c in range(2):
            dgp[s, c : c + 1, :] = gate_total[c]

        @pl.when(index == 0)
        def _():
            gate_one(1, diag_e).start()
            ret_one(0, 1, diag_e).start()
            ret_one(1, 1, diag_e).start()

        @pl.when(index == 1)
        def _():
            gate_one(1, diag_e).wait_recv()
            dgp[mirror_e] = dgp[mirror_e] + rdg1[1]
            gate_two().start()
            for kind in range(2):
                ret_one(kind, 1, diag_e).wait_recv()
                for i in range(IMAGES):
                    rows = slice(i * PAD, (i + 1) * PAD)
                    partial[kind][mirror_e, rows, :] = plus(partial[kind][mirror_e, rows, :], rret1[kind, 1, rows, :])
                    ret_two(kind, i).start()

        @pl.when(index == 2)
        def _():
            gate_one(0, mate_e).start()
            ret_one(0, 0, mate_e).start()
            ret_one(1, 0, mate_e).start()

        return carry

    lax.fori_loop(0, 4, return_source, 0)

    gate_one(0, mate_e).wait_recv()
    gate_two().wait_recv()
    d_gate = dgp[ep] + rdg1[0] + rdg2[...]
    spread = None
    for c, hot in enumerate(picks()):
        term = hot * jnp.where(meta_in[10 + c : 11 + c, :] < CAP, d_gate[c : c + 1, :], 0.0)
        spread = term if spread is None else spread + term
    gate_rows = gates[...]
    d_logits = (gate_rows * (spread - jnp.sum(gate_rows * spread, 0, keepdims=True))).astype(bf16)
    padf[...] = dot_tn(d_logits, wrt[...])
    sm[0, 0:8, :] = jnp.zeros((8, WIDTH), f32)
    sm[0, 8:16, :] = dot(d_logits, hid_own[...])
    for kind in range(2):
        ret_one(kind, 0, mate_e).wait_recv()

    def backward_image(i, carry):
        rows = image_rows(i)
        ret_two(0, i).wait_recv()
        d_hidden = (
            padf[rows, :]
            + dy_all[ep, rows, :].astype(f32)
            + rret1[0, 0, rows, :].astype(f32)
            + rret2[0, rows, :].astype(f32)
        )
        unit2, scale2 = normalized(resid[rows, :])
        sm[0, 1:2, :] += jnp.sum(d_hidden * unit2, 0, keepdims=True)
        d_residual = dy_own[rows, :].astype(f32) + norm_back(unit2, scale2, gain2[...], d_hidden)
        padf[rows, :] = d_residual
        d_branch = d_residual.astype(bf16)
        hid_own[rows, :] = d_branch
        da_temp[...] = dot_nt(d_branch, wproj[...]).astype(bf16)
        for pair in range(PAIRS):
            queries = proj[rows, columns(0, pair)] * jnp.array(score_scale, bf16)
            keys = proj[rows, columns(1, pair)]
            values = proj[rows, columns(2, pair)]
            d_att = da_temp[:, columns(0, pair)]
            d_q = d_k = d_v = None
            for mask in masks:
                own_keys = keys * mask
                chance = softmax_of(queries, own_keys)
                d_chance = dot_nt(d_att, values * mask)
                both = chance * d_chance
                d_scores = (both - chance * jnp.sum(both, -1, keepdims=True)).astype(bf16)
                t_q = dot(d_scores, own_keys)
                t_k = dot_tn(d_scores, queries * mask)
                t_v = dot_tn(chance.astype(bf16), d_att * mask)
                d_q = t_q if d_q is None else d_q + t_q
                d_k = t_k if d_k is None else d_k + t_k
                d_v = t_v if d_v is None else d_v + t_v
            proj[rows, columns(0, pair)] = (d_q * score_scale).astype(bf16)
            proj[rows, columns(1, pair)] = d_k.astype(bf16)
            proj[rows, columns(2, pair)] = d_v.astype(bf16)
        d_normed = dot_nt(proj[rows, :], wqkv[...])
        unit, scale = normalized(tok_p[rows, :].astype(f32))
        sm[0, 0:1, :] += jnp.sum(d_normed * unit, 0, keepdims=True)
        padf[rows, :] += norm_back(unit, scale, gain1[...], d_normed)
        tok_p[rows, :] = (unit * gain1[...]).astype(bf16)
        stage2(3 + i)
        stage3(2 + i)
        stage4(i)
        return carry

    lax.fori_loop(0, IMAGES, backward_image, 0)

    for part in range(3):
        for half in range(2):
            cols = slice(part * WIDTH + half * 256, part * WIDTH + (half + 1) * 256)
            buf_x[part * WIDTH : (part + 1) * WIDTH, half * 256 : (half + 1) * 256] = dot_tn(
                tok_p[...], proj[:, cols]
            ).astype(bf16)
    for kind in range(2):
        for which, who in ((1, diag_e), (0, mate_e)):
            ret_one(kind, which, who).wait_send()
    for half in range(2):
        cols = slice(half * 256, (half + 1) * 256)
        buf_x[3 * WIDTH : 4 * WIDTH, cols] = dot_tn(att[...], hid_own[:, cols]).astype(bf16)

    levels = ((core, mate), (yy, mirror), (bx, dev_x), (bz, dev_z), (bw, dev_w))

    def region(bits, size):
        start = 0
        for level, bit in enumerate(bits):
            start = start + bit * (1024 >> level)
        return pl.ds(pl.multiple_of(start, size), size)

    held = []
    offset = 0
    late = [
        lambda: (stage2(7), stage3(6)),
        lambda: (stage3(7), stage4(4)),
        lambda: (stage4(5),),
        lambda: (stage4(6),),
        lambda: (stage4(7),),
    ]
    for level, (bit, device) in enumerate(levels):
        size = 1024 >> level
        away = region(held + [1 - bit], size)
        keep = region(held + [bit], size)
        land = rg.at[offset : offset + size]
        copy = remote(buf_x.at[away], land, ar_s.at[level], ar_r.at[level], device)
        copy.start()
        little = remote(sm.at[level], rsm.at[level], sr_s.at[level], sr_r.at[level], device)
        little.start()
        late[level]()
        copy.wait_recv()
        target = buf_x if level < 4 else buf_g
        target[keep, :] = plus(buf_x[keep, :], rg[offset : offset + size, :])
        little.wait_recv()
        sm[level + 1] = sm[level] + rsm[level]
        copy.wait_send()
        little.wait_send()
        held.append(bit)
        offset += size
    small_g[...] = sm[5]

    for level in range(4, -1, -1):
        bit, device = levels[level]
        size = 1024 >> level
        mine = region(held, size)
        other = region(held[:level] + [1 - bit], size)
        send = remote(buf_g.at[mine], buf_g.at[mine], ar_s.at[5 + level], ar_r.at[5 + level], device)
        send.start()
        if level == 4:
            for i in range(IMAGES):
                rows = slice(i * PAD, (i + 1) * PAD)
                ret_two(1, i).wait_recv()
                value = (
                    resid[rows, :]
                    + hid_all[ep, rows, :].astype(f32)
                    + rret1[1, 0, rows, :].astype(f32)
                    + rret2[1, rows, :].astype(f32)
                )
                acc_o[SEQ * i : SEQ * i + SEQ, :] = value[0:SEQ, :]
                ig[SEQ * i : SEQ * i + SEQ, :] = padf[i * PAD : i * PAD + SEQ, :]
            out[...] = acc_o[0:788, :].astype(bf16)
        remote(buf_g.at[other], buf_g.at[other], ar_s.at[5 + level], ar_r.at[5 + level], device).wait_recv()
        send.wait_send()
        held.pop()

    for u in range(UNITS):
        leave_in(u).wait()
    for el in range(2):
        leave_out(el).wait()
    for part in range(4):
        rows = slice((part % 2) * WIDTH, (part % 2 + 1) * WIDTH)
        target = qkv_g.at[:, part * WIDTH : (part + 1) * WIDTH] if part < 3 else proj_g
        if part >= 2:
            pltpu.make_async_copy(acc_r.at[rows], target, o_sem.at[part % 2]).wait()
        acc_r[rows, :] = buf_g[part * WIDTH : (part + 1) * WIDTH, :].astype(f32)
        pltpu.make_async_copy(acc_r.at[rows], target, o_sem.at[part % 2]).start()
    for kind in range(2):
        for i in range(IMAGES):
            ret_two(kind, i).wait_send()
    gate_one(1, diag_e).wait_send()
    gate_one(0, mate_e).wait_send()
    gate_two().wait_send()

    def drain(u, carry):
        for copy in copy_a1(u) + copy_a2(u) + copy_a3(u):
            copy.wait_send()
        return carry

    lax.fori_loop(0, UNITS, drain, 0)
    for el in range(2):
        for hi in range(2):
            copy_o2(el, hi).wait_send()
        copy_o3(el).wait_send()
    for part in range(2):
        rows = slice(part * WIDTH, (part + 1) * WIDTH)
        pltpu.make_async_copy(acc_r.at[rows], proj_g, o_sem.at[part]).wait()


def fused(
    tokens, ln1_gain, w_qkv, w_proj, ln2_gain, w_router, w_in, w_out, noise, choices, slots, cotangent
):
    table = jnp.concatenate([noise, choices.astype(f32), slots.astype(f32)], 1).reshape(IMAGES, SEQ, 12)
    filler = jnp.concatenate([jnp.zeros((8,), f32), -jnp.ones((2,), f32), jnp.full((2,), CAP, f32)])
    filler = jnp.broadcast_to(filler, (IMAGES, PAD - SEQ, 12))
    meta_in = jnp.concatenate([table, filler], 1).reshape(ROWS, 12).T
    vmem = pl.BlockSpec(memory_space=pltpu.VMEM)
    anywhere = pl.BlockSpec(memory_space=pl.ANY)
    dma = pltpu.SemaphoreType.DMA
    v = pltpu.VMEM
    rows = (ROWS, WIDTH)
    scratch = [
        v(rows, f32), v(rows, bf16), v(rows, bf16), v(rows, bf16), v((ROWS, 3 * WIDTH), bf16), v(rows, bf16),
        v(rows, f32), v((PAD, WIDTH), bf16), v((8, ROWS), f32), v((4, 8, ROWS), f32),
        v((4, *rows), bf16), v((4, *rows), bf16),
        v((2 * PLACES, WIDTH), bf16), v((2 * PLACES, WIDTH), bf16), v((2 * PLACES, WIDTH), bf16),
        v((2, WIDTH, CHUNK), bf16), v((2, CHUNK, WIDTH), bf16),
        v((PLACES, CHUNK), bf16), v((PLACES, CHUNK), bf16), v((PLACES, WIDTH), f32), v((PLACES, WIDTH), f32),
        v((2 * CHUNKS, 2, 2, 2, SHARE_IN, CHUNK), bf16), v((2, 2, 2, 2, CHUNK, WIDTH), bf16),
        v((2 * CHUNKS, 2, 2, SHARE_IN, CHUNK), bf16), v((2 * CHUNKS, 2, SHARE_IN, CHUNK), bf16),
        v((2 * CHUNKS, SHARE_IN, CHUNK), bf16),
        v((UNITS, CHUNK, WIDTH), bf16), v((2, 2, CHUNK, WIDTH), bf16), v((2, CHUNK, WIDTH), bf16),
        v((2, 2, *rows), bf16), v((2, *rows), bf16),
        v((4, 8, ROWS), f32), v((2, 8, ROWS), f32), v((8, ROWS), f32),
        v((1984, WIDTH), bf16), v((6, 16, WIDTH), f32), v((5, 16, WIDTH), f32),
        dma((2, 2)), dma((2,)), dma((UNITS,)), dma((2,)), dma((2, 3, IMAGES)), dma((2, 3, IMAGES)), dma((3,)), dma((3,)),
        dma((2, 2)), dma((2, 2)), dma((2, IMAGES)), dma((2, IMAGES)), dma((2,)), dma((2,)), dma, dma,
        dma((2, 3, UNITS)), dma((2, 3, UNITS)), dma((UNITS,)), dma((UNITS,)),
        dma((2, 2)), dma((2, 2)), dma((2,)), dma((2,)), dma((10,)), dma((10,)), dma((5,)), dma((5,)),
    ]
    results = pl.pallas_call(
        block_kernel,
        out_shape=(
            jax.ShapeDtypeStruct((788, WIDTH), bf16),
            jax.ShapeDtypeStruct((788, WIDTH), f32),
            jax.ShapeDtypeStruct((WIDTH, 3 * WIDTH), f32),
            jax.ShapeDtypeStruct((WIDTH, WIDTH), f32),
            jax.ShapeDtypeStruct((16, WIDTH), f32),
            jax.ShapeDtypeStruct((2, SHARE_IN, CHUNK * CHUNKS), f32),
            jax.ShapeDtypeStruct((2, CHUNK, WIDTH), f32),
        ),
        in_specs=[anywhere] * 2 + [vmem] * 6 + [anywhere] * 2,
        out_specs=(vmem, vmem, anywhere, anywhere, vmem, anywhere, anywhere),
        scratch_shapes=scratch,
        compiler_params=pltpu.CompilerParams(
            collective_id=0, has_side_effects=True, vmem_limit_bytes=61 << 20
        ),
        name="block",
    )(
        tokens, cotangent, ln1_gain[None, :], ln2_gain[None, :], w_qkv, w_proj, w_router.T, meta_in, w_in, w_out
    )
    out, input_grad, qkv_grad, proj_grad, small, in_share, out_share = results
    return (
        out, input_grad, small[0], qkv_grad, proj_grad, small[1], small[8:16].T, in_share, out_share
    )


def solution(mesh):
    in_specs = (
        P(("rep", "ep"), None),
        P(),
        P(),
        P(),
        P(),
        P(),
        P("ep", None, None),
        P("ep", None, None),
        P(("rep", "ep"), None),
        P(("rep", "ep"), None),
        P(("rep", "ep"), None),
        P(("rep", "ep"), None),
    )
    out_specs = (
        P(("rep", "ep"), None),
        P(("rep", "ep"), None),
        P(),
        P(),
        P(),
        P(),
        P(),
        P("ep", "rep", None),
        P("ep", "rep", None),
    )
    whole = fused if dict(mesh.shape) == {"rep": 8, "ep": 4} else local
    return jax.shard_map(whole, mesh=mesh, in_specs=in_specs, out_specs=out_specs, check_vma=False)
```

```python
import functools

import jax
import jax.numpy as jnp
from jax import lax
from jax.experimental import pallas as pl
from jax.experimental.pallas import tpu as pltpu
from jax.sharding import PartitionSpec as P

HEADS = 8
HEAD_DIM = 64
SEQ = 197
CAP = 246


epsilon = 1e-06


def layer_norm(source, gain_row):
    row_mean = jnp.mean(source, -1, keepdims=True)
    centered = source - row_mean
    spread = jnp.mean(centered * centered, -1, keepdims=True)
    return centered * lax.rsqrt(spread + epsilon) * gain_row


def expert_hidden(arrived, w_in):
    hidden_pre = jnp.einsum("jrd,jdf->jrf", arrived, w_in, preferred_element_type=jnp.float32)
    return (hidden_pre, jax.nn.gelu(hidden_pre).astype(jnp.bfloat16))


def local(
    tokens,
    ln1_gain,
    w_qkv,
    w_proj,
    ln2_gain,
    w_router,
    w_in,
    w_out,
    noise,
    choices,
    slots,
    cotangent,
):
    row_count, model_width = tokens.shape
    experts_all = w_router.shape[1]
    images = row_count // SEQ
    score_scale = HEAD_DIM ** (-0.5)
    source = tokens.astype(jnp.float32)
    normed, norm1_back = jax.vjp(layer_norm, source, ln1_gain)
    normed_low = normed.astype(jnp.bfloat16)
    projected = jnp.dot(normed_low, w_qkv, preferred_element_type=jnp.float32).astype(jnp.bfloat16)

    def heads_of(columns):
        return columns.reshape(images, SEQ, HEADS, HEAD_DIM)

    queries = heads_of(projected[:, :model_width])
    keys_all = heads_of(projected[:, model_width : 2 * model_width])
    values_all = heads_of(projected[:, 2 * model_width :])
    scores = (
        jnp.einsum("ishd,ithd->ihst", queries, keys_all, preferred_element_type=jnp.float32)
        * score_scale
    )
    logsum = jax.nn.logsumexp(scores, -1, keepdims=True)
    attention = jnp.exp(scores - logsum).astype(jnp.bfloat16)
    attended = jnp.einsum(
        "ihst,ithd->ishd", attention, values_all, preferred_element_type=jnp.float32
    )
    attended = attended.reshape(row_count, model_width).astype(jnp.bfloat16)
    residual = source + jnp.dot(attended, w_proj, preferred_element_type=jnp.float32)
    normed2, norm2_back = jax.vjp(layer_norm, residual, ln2_gain)
    hidden = normed2.astype(jnp.bfloat16)
    logits = jnp.dot(hidden, w_router, preferred_element_type=jnp.float32)

    def routing(logit_rows):
        return jnp.take_along_axis(jax.nn.softmax(logit_rows + noise, -1), choices, 1)

    picked_gate, routing_back = jax.vjp(routing, logits)
    kept_pair = slots < CAP
    kept_float = kept_pair.astype(jnp.float32)
    slot_index = jnp.where(kept_pair, choices * CAP + slots, experts_all * CAP)
    read_index = jnp.minimum(slot_index, experts_all * CAP - 1)
    pair_gate = picked_gate * kept_float

    def place(pair_rows):
        flat_rows = pair_rows.reshape(row_count * 2, model_width)
        filled = (
            jnp.zeros((experts_all * CAP, model_width), jnp.bfloat16)
            .at[slot_index.reshape(-1)]
            .set(flat_rows, mode="drop")
        )
        return filled.reshape(experts_all, CAP, model_width)

    hidden_pairs = jnp.broadcast_to(hidden[:, None, :], (row_count, 2, model_width))
    arrived = lax.all_to_all(place(hidden_pairs), "ep", split_axis=0, concat_axis=1, tiled=True)
    hidden_pre, hidden_act = expert_hidden(arrived, w_in)
    expert_out = jnp.einsum(
        "jrf,jfd->jrd", hidden_act, w_out, preferred_element_type=jnp.float32
    ).astype(jnp.bfloat16)
    returned = lax.all_to_all(expert_out, "ep", split_axis=1, concat_axis=0, tiled=True).reshape(
        experts_all * CAP, model_width
    )
    gathered = returned[read_index].astype(jnp.float32)
    output = residual + jnp.sum(pair_gate[..., None] * gathered, 1)
    upstream = cotangent.astype(jnp.float32)
    d_gate = jnp.sum(upstream[:, None, :] * gathered, -1) * kept_float
    d_pairs = (pair_gate[..., None] * upstream[:, None, :]).astype(jnp.bfloat16)
    grad_rows = lax.all_to_all(place(d_pairs), "ep", split_axis=0, concat_axis=1, tiled=True)
    again_rows, again_pre, again_act = (arrived, hidden_pre, hidden_act)
    d_act = jnp.einsum("jrd,jfd->jrf", grad_rows, w_out, preferred_element_type=jnp.float32)
    gelu_back = jax.vjp(jax.nn.gelu, again_pre)[1]
    d_pre = gelu_back(d_act)[0].astype(jnp.bfloat16)
    d_w_out = jnp.einsum("jrf,jrd->jfd", again_act, grad_rows, preferred_element_type=jnp.float32)
    d_w_in = jnp.einsum("jrd,jrf->jdf", again_rows, d_pre, preferred_element_type=jnp.float32)
    in_share, out_share = (
        lax.psum_scatter(d_w_in, "rep", scatter_dimension=1, tiled=True),
        lax.psum_scatter(d_w_out, "rep", scatter_dimension=1, tiled=True),
    )
    d_rows = jnp.einsum("jrf,jdf->jrd", d_pre, w_in, preferred_element_type=jnp.float32).astype(
        jnp.bfloat16
    )
    d_back = lax.all_to_all(d_rows, "ep", split_axis=1, concat_axis=0, tiled=True).reshape(
        experts_all * CAP, model_width
    )
    d_hidden = jnp.sum(d_back[read_index].astype(jnp.float32) * kept_float[..., None], 1)
    d_logits = routing_back(d_gate)[0].astype(jnp.bfloat16)
    d_w_router = jnp.einsum("td,te->de", hidden, d_logits, preferred_element_type=jnp.float32)
    d_hidden = d_hidden + jnp.einsum(
        "te,de->td", d_logits, w_router, preferred_element_type=jnp.float32
    )
    d_resid_part, d_gain2 = norm2_back(d_hidden)
    d_residual = upstream + d_resid_part
    d_branch = d_residual.astype(jnp.bfloat16)
    d_w_proj = jnp.einsum("td,te->de", attended, d_branch, preferred_element_type=jnp.float32)
    d_attended = jnp.einsum("te,de->td", d_branch, w_proj, preferred_element_type=jnp.float32)
    d_attended = heads_of(d_attended.astype(jnp.bfloat16))
    rescored = (
        jnp.einsum("ishd,ithd->ihst", queries, keys_all, preferred_element_type=jnp.float32)
        * score_scale
    )
    probability = jnp.exp(rescored - logsum)
    d_prob = jnp.einsum(
        "ishd,ithd->ihst", d_attended, values_all, preferred_element_type=jnp.float32
    )
    d_values = jnp.einsum(
        "ihst,ishd->ithd",
        probability.astype(jnp.bfloat16),
        d_attended,
        preferred_element_type=jnp.float32,
    )
    d_scores = (probability * (d_prob - jnp.sum(probability * d_prob, -1, keepdims=True))).astype(
        jnp.bfloat16
    )
    d_queries = (
        jnp.einsum("ihst,ithd->ishd", d_scores, keys_all, preferred_element_type=jnp.float32)
        * score_scale
    )
    d_keys = (
        jnp.einsum("ihst,ishd->ithd", d_scores, queries, preferred_element_type=jnp.float32)
        * score_scale
    )
    d_projected = jnp.concatenate(
        [
            d_queries.reshape(row_count, model_width),
            d_keys.reshape(row_count, model_width),
            d_values.reshape(row_count, model_width),
        ],
        1,
    ).astype(jnp.bfloat16)
    d_w_qkv = jnp.einsum("td,te->de", normed_low, d_projected, preferred_element_type=jnp.float32)
    d_normed = jnp.einsum("te,de->td", d_projected, w_qkv, preferred_element_type=jnp.float32)
    d_source_part, d_gain1 = norm1_back(d_normed)
    input_grad = d_residual + d_source_part
    dense_sums = lax.psum((d_gain1, d_w_qkv, d_w_proj, d_gain2, d_w_router), ("rep", "ep"))
    return (
        output.astype(jnp.bfloat16),
        input_grad,
        dense_sums[0],
        dense_sums[1],
        dense_sums[2],
        dense_sums[3],
        dense_sums[4],
        in_share,
        out_share,
    )


IMAGES = 4
PAD = 208
ROWS = IMAGES * PAD
WIDTH = 512
PAIRS = 4
SLOT_PAD = 256
PLACES = 4 * SLOT_PAD
CHUNK = 256
CHUNKS = 8
WIDE = 2 * CHUNK
STEPS = CHUNKS // 2
UNITS = 8
SHARE_IN = 64
PARTS = 2
MESH = pl.DeviceIdType.MESH
bf16 = jnp.bfloat16
f32 = jnp.float32


def dot(a, b):
    return jnp.dot(a, b, preferred_element_type=f32)


def dot_nt(a, b):
    return lax.dot_general(a, b, (((1,), (1,)), ((), ())), preferred_element_type=f32)


def dot_tn(a, b):
    return lax.dot_general(a, b, (((0,), (0,)), ((), ())), preferred_element_type=f32)


def normalized(source):
    centered = source - jnp.mean(source, -1, keepdims=True)
    scale = lax.rsqrt(jnp.mean(centered * centered, -1, keepdims=True) + epsilon)
    return centered * scale, scale


def norm_back(unit, scale, gain_row, grad):
    d_unit = grad * gain_row
    return scale * (
        d_unit
        - jnp.mean(d_unit, -1, keepdims=True)
        - unit * jnp.mean(d_unit * unit, -1, keepdims=True)
    )


def remote(src, dst, send, recv, device):
    return pltpu.make_async_remote_copy(
        src_ref=src, dst_ref=dst, send_sem=send, recv_sem=recv, device_id=device, device_id_type=MESH
    )


def block_kernel(
    tok, cot, gain1, gain2, w_qkv, w_proj, wrt, noise, choices, slots, w_in, w_out,
    out_g, ig_g, dense_g, small_g, win_a, win_b, wout_a, wout_b,
    wqkv, wproj, table, meta_in, out, ig, padf, tok_p, dy_own, hid_own, proj, att, resid, da_temp, gates, meta, hid_all, dy_all,
    buf_x, buf_g, buf_y, wi_buf, wo_buf, act_s, dpre_s, acc, turned_x,
    dwi, dwo, ri1, ri2, ri3, ro1, ro2, ro3,
    rret1, rret2, dgp, rdg1, rdg2, rg_c, rg_y, rg_d, rg_w, sm, rsm,
    f_sem, w_sem, o_sem, li_sem, lo_sem, ag_s, ag_r, near_r, far_r, m_s, m_r, p1_s, p1_r, p2_s, p2_r, q1_s, q1_r, q2_s, q2_r,
    rs_s, di_r, i3_r, do1_r, do2_r, do3_r, ar_s, ar_r, ad_s, ad_r, sr_s, sr_r,
):
    rep = lax.axis_index("rep")
    ep = lax.axis_index("ep")
    core = lax.rem(ep, 2)
    yy = ep // 2
    bx = lax.rem(rep, 2)
    bz = lax.rem(rep // 2, 2)
    bw = rep // 4
    mate_e = ep + 1 - 2 * core
    mirror_e = ep + 2 - 4 * yy
    diag_e = mate_e + 2 - 4 * yy
    mate = (rep, mate_e)
    mirror = (rep, mirror_e)
    dev_x = (rep + 1 - 2 * bx, ep)
    dev_z = (rep + 2 - 4 * bz, ep)
    dev_w = (rep + 4 - 8 * bw, ep)

    barrier = pltpu.get_barrier_semaphore()
    dev_xz = (rep + 1 - 2 * bx + 2 - 4 * bz, ep)
    for device in (mate, mirror, dev_x, dev_z, dev_xz, dev_w):
        pl.semaphore_signal(barrier, inc=1, device_id=device, device_id_type=MESH)
    fetches = [
        pltpu.make_async_copy(a, b, f_sem.at[n])
        for n, (a, b) in enumerate(((cot, out), (w_qkv, wqkv), (w_proj, wproj), (tok, out)))
    ]
    for fetch in fetches[:3]:
        fetch.start()

    def image_rows(i):
        return pl.ds(pl.multiple_of(i * PAD, 16), PAD)

    row_id = lax.broadcasted_iota(jnp.int32, (PAD, WIDTH), 0)

    def pad_rows(put):
        padf[784:800, :] = jnp.zeros((16, WIDTH), f32)
        padf[0:788, :] = out[...].astype(f32)
        for i in range(IMAGES):
            value = padf[SEQ * i : SEQ * i + PAD, :]
            put(i, jnp.where(row_id < SEQ, value, 0.0).astype(bf16))

    def put_tok(i, value):
        tok_p[i * PAD : (i + 1) * PAD, :] = value

    def put_dy(i, value):
        dy_own[i * PAD : (i + 1) * PAD, :] = value

    table[...] = jnp.zeros((16, 896), f32)
    table[0:8, 0:788] = noise[...]
    table[8:10, 0:788] = choices[...].astype(f32)
    table[10:12, 0:788] = slots[...].astype(f32)
    lanes = lax.broadcasted_iota(jnp.int32, (16, 896), 1)
    kinds = lax.broadcasted_iota(jnp.int32, (16, 896), 0)
    spaced = jnp.where(kinds < 8, 0.0, jnp.where(kinds < 10, -1.0, float(CAP)))
    flat = table[...]
    for i in range(IMAGES):
        shifted = flat if i == 0 else pltpu.roll(flat, i * (PAD - SEQ), 1)
        spaced = jnp.where((lanes >= i * PAD) & (lanes < i * PAD + SEQ), shifted, spaced)
    meta_in[...] = spaced[:, 0:ROWS]
    fetches[0].wait()
    pad_rows(put_dy)
    fetches[3].start()
    fetches[3].wait()
    pad_rows(put_tok)
    pl.semaphore_wait(barrier, 6)

    stores = (dy_own, hid_own)
    gathered = (dy_all, hid_all)

    def gather_send(kind, i):
        rows = image_rows(i)
        for route, device in ((0, mate), (1, mirror)):
            remote(
                stores[kind].at[rows], gathered[kind].at[ep, rows],
                ag_s.at[kind], near_r.at[kind] if route == 0 else ag_r.at[kind, i], device,
            ).start()

    def gather_forward(kind, i):
        rows = image_rows(i)
        here = gathered[kind].at[mirror_e, rows]
        remote(here, here, ag_s.at[kind], ag_r.at[kind, i], mirror).wait_recv()
        remote(here, here, ag_s.at[kind], far_r.at[kind], mate).start()

    def gather_near(kind):
        here = gathered[kind].at[mate_e]
        remote(here, here, ag_s.at[kind], near_r.at[kind], mate).wait_recv()

    def gather_far(kind):
        here = gathered[kind].at[diag_e]
        remote(here, here, ag_s.at[kind], far_r.at[kind], mate).wait_recv()
        here = gathered[kind].at[0:3]
        remote(here, here, ag_s.at[kind], far_r.at[kind], mate).wait_send()

    def sent(like, semaphore):
        remote(like, like, semaphore, q2_r, mate).wait_send()

    def weights(step):
        el = lax.rem(step // STEPS, 2)
        start = pl.multiple_of(lax.rem(step, STEPS) * WIDE, WIDE)
        slot = lax.rem(step, 2)
        return (
            pltpu.make_async_copy(w_in.at[el, :, pl.ds(start, WIDE)], wi_buf.at[slot], w_sem.at[0, slot]),
            pltpu.make_async_copy(w_out.at[el, pl.ds(start, WIDE), :], wo_buf.at[slot], w_sem.at[1, slot]),
        )

    for copy in weights(0):
        copy.start()

    fetches[1].wait()
    fetches[2].wait()
    lane = lax.broadcasted_iota(jnp.int32, (1, 128), 1)
    masks = ((lane < HEAD_DIM).astype(f32).astype(bf16), (lane >= HEAD_DIM).astype(f32).astype(bf16))
    key_col = lax.broadcasted_iota(jnp.int32, (PAD, PAD), 1)
    score_scale = HEAD_DIM ** (-0.5)

    def softmax_of(queries, keys):
        scores = jnp.where(key_col < SEQ, dot_nt(queries, keys), -1e30)
        weight = jnp.exp(scores - jnp.max(scores, -1, keepdims=True))
        return weight / jnp.sum(weight, -1, keepdims=True)

    def columns(part, pair):
        start = part * WIDTH + pair * 128
        return slice(start, start + 128)

    def forward_image(i, carry):
        rows = image_rows(i)
        gather_send(0, i)
        source = tok_p[rows, :].astype(f32)
        unit, _ = normalized(source)
        normed = (unit * gain1[...]).astype(bf16)
        for part in range(3):
            cols = slice(part * WIDTH, (part + 1) * WIDTH)
            proj[rows, cols] = dot(normed, wqkv[:, cols]).astype(bf16)
        for pair in range(PAIRS):
            queries = proj[rows, columns(0, pair)] * jnp.array(score_scale, bf16)
            keys = proj[rows, columns(1, pair)]
            values = proj[rows, columns(2, pair)]
            total = None
            for mask in masks:
                attention = softmax_of(queries, keys * mask).astype(bf16)
                term = dot(attention, values * mask)
                total = term if total is None else total + term
            att[rows, columns(0, pair)] = total.astype(bf16)
        residual = source + dot(att[rows, :], wproj[...])
        resid[rows, :] = residual
        unit2, _ = normalized(residual)
        hid_own[rows, :] = (unit2 * gain2[...]).astype(bf16)
        gather_send(1, i)

        return carry

    lax.fori_loop(0, IMAGES, forward_image, 0)

    expert_id = lax.broadcasted_iota(jnp.int32, (8, ROWS), 0).astype(f32)

    def picks():
        return [(expert_id == meta_in[8 + c : 9 + c, :]).astype(f32) for c in range(2)]

    logits = dot_nt(wrt[...], hid_own[...]) + meta_in[0:8, :]
    gate_top = jnp.exp(logits - jnp.max(logits, 0, keepdims=True))
    gate_rows = gate_top / jnp.sum(gate_top, 0, keepdims=True)
    gates[...] = gate_rows
    meta[ep] = jnp.zeros((8, ROWS), f32)
    for c, hot in enumerate(picks()):
        slot = meta_in[10 + c : 11 + c, :]
        kept = slot < CAP
        chosen = meta_in[8 + c : 9 + c, :]
        meta[ep, c : c + 1, :] = jnp.where(kept, chosen * SLOT_PAD + slot, -1.0)
        meta[ep, 2 + c : 3 + c, :] = jnp.where(kept, jnp.sum(gate_rows * hot, 0, keepdims=True), 0.0)
    for route, device in ((0, mate), (1, mirror)):
        remote(meta.at[ep], meta.at[ep], m_s.at[route], m_r.at[route], device).start()
    dy_all[ep] = dy_own[...]
    hid_all[ep] = hid_own[...]
    gather_forward(0, 0)
    for kind in range(2):
        gather_near(kind)
    remote(meta.at[mate_e], meta.at[mate_e], m_s.at[0], m_r.at[0], mate).wait_recv()

    slot_id = lax.broadcasted_iota(jnp.int32, (SLOT_PAD, ROWS), 0)

    def hits(s, el):
        first = (2 * ep + el) * SLOT_PAD
        place = (slot_id + first).astype(f32)
        return place == meta[s, 0:1, :], place == meta[s, 1:2, :]

    def hot_of(hit):
        return jnp.where(hit[0] | hit[1], 1.0, 0.0).astype(bf16)

    def slot_gate(s, hit):
        weight = jnp.where(hit[0], meta[s, 2:3, :], 0.0) + jnp.where(hit[1], meta[s, 3:4, :], 0.0)
        return jnp.sum(weight, -1, keepdims=True)

    sources = ((ep, mate_e), (mirror_e, diag_e))

    def slot_rows(pass_id, el, index):
        start = pass_id * PLACES + el * 2 * SLOT_PAD + index * SLOT_PAD
        return pl.ds(pl.multiple_of(start, SLOT_PAD), SLOT_PAD)

    def place_sources(pass_id):
        first, second = sources[pass_id]

        def place_source(index, carry):
            s = first + index * (second - first)
            for el in range(2):
                hit = hits(s, el)
                hot = hot_of(hit)
                rows = slot_rows(pass_id, el, index)
                buf_x[rows, :] = dot(hot, hid_all[s]).astype(bf16)
                placed = dot(hot, dy_all[s])
                buf_y[rows, :] = placed.astype(bf16)
                buf_g[rows, :] = (slot_gate(s, hit) * placed).astype(bf16)
            return carry

        lax.fori_loop(0, 2, place_source, 0)

    place_sources(0)

    def unit_parts(u):
        el = u // 4
        j = u % 4
        even = el * CHUNKS + 2 * j
        return el, j, even

    def copy_o1(u):
        el, j, even = unit_parts(u)
        return remote(dwo.at[el, j // 2, j % 2, 1 - bx], ro1.at[u], rs_s.at[5], do1_r.at[u], dev_x)

    def copy_o2(el, hi):
        return remote(
            dwo.at[el, hi, 1 - bz, bx], ro2.at[el, hi], rs_s.at[6], do2_r.at[el, hi], dev_z
        )

    def copy_o3(el, part):
        rows = slice(part * 64, (part + 1) * 64)
        return remote(
            dwo.at[el, 1 - bw, bz, bx, rows], ro3.at[el, rows], rs_s.at[7], do3_r.at[el], dev_w
        )

    def copy_e1(u):
        el, j, even = unit_parts(u)
        return remote(dwi.at[even, :, :, 1 - bx], ri1.at[even], rs_s.at[0], di_r.at[0, u], dev_x)

    def copy_e2(u):
        el, j, even = unit_parts(u)
        return remote(dwi.at[even, :, 1 - bz, bx], ri2.at[even], rs_s.at[1], di_r.at[1, u], dev_z)

    def copy_d1(u):
        el, j, even = unit_parts(u)
        return remote(dwi.at[even + 1, :, 1 - bz, :], ri1.at[even + 1], rs_s.at[2], di_r.at[2, u], dev_z)

    def copy_d2(u):
        el, j, even = unit_parts(u)
        return remote(dwi.at[even + 1, :, bz, 1 - bx], ri2.at[even + 1], rs_s.at[3], di_r.at[3, u], dev_x)

    def copy_i3(u, odd):
        el, j, even = unit_parts(u)
        return remote(
            dwi.at[even + odd, 1 - bw, bz, bx], ri3.at[even + odd],
            rs_s.at[4], i3_r.at[odd, el], dev_w,
        )

    def leave_in(u, odd):
        el, j, even = unit_parts(u)
        cols = slice((2 * j + odd) * CHUNK, (2 * j + odd + 1) * CHUNK)
        return [
            pltpu.make_async_copy(dwi.at[even + odd, bw, bz, bx], win_a.at[el, :, cols], li_sem.at[0]),
            pltpu.make_async_copy(ri3.at[even + odd], win_b.at[el, :, cols], li_sem.at[1]),
        ]

    def leave_out(el):
        return [
            pltpu.make_async_copy(dwo.at[el, bw, bz, bx], wout_a.at[el], lo_sem.at[0]),
            pltpu.make_async_copy(ro3.at[el], wout_b.at[el], lo_sem.at[1]),
        ]

    def plus(a, b):
        return (a.astype(f32) + b.astype(f32)).astype(bf16)

    def send_o(u):
        copy_o1(u).start()

    def send_e(u):
        copy_e1(u).start()

    def send_d(u):
        copy_d1(u).start()

    def took_o1(u):
        el, j, even = unit_parts(u)
        copy_o1(u).wait_recv()
        if u + 3 < UNITS:
            send_o(u + 3)
        dwo[el, j // 2, j % 2, bx] = plus(dwo[el, j // 2, j % 2, bx], ro1[u])
        if j % 2 == 1:
            copy_o2(el, j // 2).start()

    def took_o2(el, hi):
        copy_o2(el, hi).wait_recv()
        dwo[el, hi, bz, bx] = plus(dwo[el, hi, bz, bx], ro2[el, hi])

    def took_o3(el):
        remote(ro3.at[el], ro3.at[el], rs_s.at[7], do3_r.at[el], dev_w).wait_recv()
        for copy in leave_out(el):
            copy.start()

    def took_e1(u):
        el, j, even = unit_parts(u)
        copy_e1(u).wait_recv()
        dwi[even, :, :, bx] = plus(dwi[even, :, :, bx], ri1[even])
        copy_e2(u).start()

    def took_e2(u):
        el, j, even = unit_parts(u)
        copy_e2(u).wait_recv()
        dwi[even, :, bz, bx] = plus(dwi[even, :, bz, bx], ri2[even])
        copy_i3(u, 0).start()

    def took_d1(u):
        el, j, even = unit_parts(u)
        copy_d1(u).wait_recv()
        dwi[even + 1, :, bz] = plus(dwi[even + 1, :, bz], ri1[even + 1])
        copy_d2(u).start()

    def took_d2(u):
        el, j, even = unit_parts(u)
        copy_d2(u).wait_recv()
        dwi[even + 1, :, bz, bx] = plus(dwi[even + 1, :, bz, bx], ri2[even + 1])
        copy_i3(u, 1).start()

    def took_i3(el, odd):
        group = ri3.at[0:4]
        remote(group, group, rs_s.at[4], i3_r.at[odd, el], dev_w).wait_recv()
        for j in range(4):
            for copy in leave_in(4 * el + j, odd):
                copy.start()

    moves = {
        "O": send_o, "E": send_e, "D": send_d, "o": took_o1, "e": took_e1, "d": took_d1,
        "f": took_e2, "c": took_d2,
        "p": lambda n: took_o2(n // 2, n % 2), "q": took_o3, "r": lambda n: copy_o3(n // 4, n % 4).start(),
        "g": lambda n: took_i3(n, 0), "h": lambda n: took_i3(n, 1),
    }

    def go(*words):
        for word in words:
            moves[word[:-1]](int(word[-1]))

    gelu_a = 0.7978845608028654
    gelu_b = gelu_a * 0.044715

    half_places = 2 * SLOT_PAD

    def expert_pass(pass_id, extra):
        def expert_step(step, carry):
            turn = pass_id * 2 * STEPS + step
            el = step // STEPS
            k = lax.rem(step, STEPS)
            slot = lax.rem(step, 2)
            first = pl.multiple_of(pass_id * PLACES + el * half_places, half_places)
            whole = pl.ds(first, half_places)
            for copy in weights(turn):
                copy.wait()

            @pl.when(turn + 1 < 4 * STEPS)
            def _():
                for copy in weights(turn + 1):
                    copy.start()

            @pl.when(k == 0)
            def _():
                acc[...] = jnp.zeros((PLACES, WIDTH), f32)
                turned_x[...] = buf_x[whole, :].T

            wi = wi_buf[slot]
            wo = wo_buf[slot]
            for part in range(PARTS):
                size = half_places // PARTS
                rows = slice(part * size, (part + 1) * size)
                rows_r = slice(half_places + part * size, half_places + (part + 1) * size)
                far = pl.ds(pl.multiple_of(first + part * size, size), size)
                pre = dot(buf_x[far, :], wi)
                square = pre * pre
                level = jnp.tanh(pre * (gelu_a + gelu_b * square))
                half = 0.5 + 0.5 * level
                act = (pre * half).astype(bf16)
                slope = half + (0.5 * pre) * (1.0 - level * level) * (gelu_a + 3.0 * gelu_b * square)
                d_act = dot_nt(buf_g[far, :], wo)
                d_pre = (d_act * slope).astype(bf16)
                act_s[rows, :] = act
                dpre_s[rows, :] = d_pre
                acc[rows, :] += dot(act, wo)
                acc[rows_r, :] += dot_nt(d_pre, wi)
            for odd in range(2):
                cols = slice(odd * CHUNK, (odd + 1) * CHUNK)
                grad_out = dot_tn(act_s[0:half_places, cols], buf_g[whole, :])
                grad_in = dot(turned_x[...], dpre_s[0:half_places, cols]).reshape(2, 2, 2, SHARE_IN, CHUNK)
                out_at = (el, k // 2, lax.rem(k, 2), odd)
                in_at = 2 * step + odd
                if pass_id == 1:
                    grad_out = grad_out + dwo[out_at].astype(f32)
                    grad_in = grad_in + dwi[in_at].astype(f32)
                dwo[out_at] = grad_out.astype(bf16)
                dwi[in_at] = grad_in.astype(bf16)
            for when, what in extra:

                @pl.when(step == when)
                def _(what=what):
                    what()

            @pl.when(k == STEPS - 1)
            def _():
                buf_x[whole, :] = acc[0:half_places, :].astype(bf16)
                buf_g[whole, :] = acc[half_places:, :].astype(bf16)

            return carry

        lax.fori_loop(0, 2 * STEPS, expert_step, 0)

    expert_pass(
        0,
        [
            (0, lambda: gather_forward(1, 0)),
            (2, lambda: gather_forward(0, 1)),
            (4, lambda: gather_forward(1, 1)),
            (6, lambda: gather_forward(0, 2)),
        ],
    )

    partial = (dy_all, hid_all)

    def ret_one(kind, which, who):
        return remote(partial[kind].at[who], rret1.at[kind, which], p1_s, p1_r.at[kind, which], mate)

    def ret_two(kind, i):
        rows = image_rows(i)
        return remote(partial[kind].at[mirror_e, rows], rret2.at[kind, rows], p2_s, p2_r.at[kind, i], mirror)

    def gate_one(which, who):
        return remote(dgp.at[who], rdg1.at[which], q1_s, q1_r.at[which], mate)

    def gate_two():
        return remote(dgp.at[mirror_e], rdg2, q2_s, q2_r, mirror)

    def return_source(pass_id, index):
        s = sources[pass_id][index]
        gate_total = [None, None]
        turned = (act_s, dpre_s)
        for el in range(2):
            hit = hits(s, el)
            rows = slot_rows(pass_id, el, index)
            turned[el][:, 0:CHUNK] = hot_of(hit).T
            result = buf_x[rows, :].astype(f32)
            d_slot = jnp.sum(result * buf_y[rows, :].astype(f32), -1, keepdims=True)
            buf_x[rows, :] = (slot_gate(s, hit) * result).astype(bf16)
            for c in range(2):
                term = jnp.sum(jnp.where(hit[c], d_slot, 0.0), 0, keepdims=True)
                gate_total[c] = term if el == 0 else gate_total[c] + term
        dgp[s] = jnp.zeros((8, ROWS), f32)
        for c in range(2):
            dgp[s, c : c + 1, :] = gate_total[c]

        def rows_of_image(i, carry):
            rows = image_rows(i)
            for target, source in ((dy_all, buf_g), (hid_all, buf_x)):
                value = dot(act_s[rows, 0:CHUNK], source[slot_rows(pass_id, 0, index), :])
                value = value + dot(dpre_s[rows, 0:CHUNK], source[slot_rows(pass_id, 1, index), :])
                target[s, rows, :] = value.astype(bf16)
            return carry

        lax.fori_loop(0, IMAGES, rows_of_image, 0)

    gather_forward(1, 2)
    return_source(0, 1)
    gate_one(0, mate_e).start()
    ret_one(0, 0, mate_e).start()
    ret_one(1, 0, mate_e).start()
    gather_forward(0, 3)
    return_source(0, 0)
    gather_forward(1, 3)
    here = meta.at[mirror_e]
    remote(here, here, m_s.at[1], m_r.at[1], mirror).wait_recv()
    remote(here, here, m_s.at[2], m_r.at[2], mate).start()
    for kind in range(2):
        gather_far(kind)
    remote(meta.at[diag_e], meta.at[diag_e], m_s.at[2], m_r.at[2], mate).wait_recv()
    for route in range(3):
        remote(meta.at[ep], meta.at[ep], m_s.at[route], m_r.at[route], mate).wait_send()
    place_sources(1)
    expert_pass(
        1,
        [
            (0, lambda: go("O0", "D0")),
            (1, lambda: go("O1", "D1")),
            (2, lambda: go("O2", "D2")),
            (3, lambda: go("D3")),
            (4, lambda: go("D4", "d0", "o0")),
            (5, lambda: go("D5", "d1")),
            (6, lambda: go("D6", "d2")),
            (7, lambda: go("D7", "o1")),
        ],
    )
    return_source(1, 1)
    gate_one(1, diag_e).start()
    ret_one(0, 1, diag_e).start()
    ret_one(1, 1, diag_e).start()
    go("d3", "c0", "o2")
    return_source(1, 0)
    gate_one(1, diag_e).wait_recv()
    dgp[mirror_e] = dgp[mirror_e] + rdg1[1]
    gate_two().start()

    def cross(kind, i):
        rows = slice(i * PAD, (i + 1) * PAD)
        partial[kind][mirror_e, rows, :] = plus(partial[kind][mirror_e, rows, :], rret1[kind, 1, rows, :])
        ret_two(kind, i).start()

    ret_one(0, 1, diag_e).wait_recv()
    for i in range(IMAGES):
        cross(0, i)
    go("d4", "d5", "o3")

    gate_one(0, mate_e).wait_recv()
    gate_two().wait_recv()
    d_gate = dgp[ep] + rdg1[0] + rdg2[...]
    spread = None
    for c, hot in enumerate(picks()):
        term = hot * jnp.where(meta_in[10 + c : 11 + c, :] < CAP, d_gate[c : c + 1, :], 0.0)
        spread = term if spread is None else spread + term
    gate_rows = gates[...]
    d_logits = (gate_rows * (spread - jnp.sum(gate_rows * spread, 0, keepdims=True))).astype(bf16)
    padf[...] = dot_tn(d_logits, wrt[...])
    sm[0, 0:8, :] = jnp.zeros((8, WIDTH), f32)
    sm[0, 8:16, :] = dot(d_logits, hid_own[...])
    for kind in range(2):
        ret_one(kind, 0, mate_e).wait_recv()

    def backward_image(i, carry):
        rows = image_rows(i)
        ret_two(0, i).wait_recv()
        d_hidden = (
            padf[rows, :]
            + dy_all[ep, rows, :].astype(f32)
            + rret1[0, 0, rows, :].astype(f32)
            + rret2[0, rows, :].astype(f32)
        )
        unit2, scale2 = normalized(resid[rows, :])
        sm[0, 1:2, :] += jnp.sum(d_hidden * unit2, 0, keepdims=True)
        d_residual = dy_own[rows, :].astype(f32) + norm_back(unit2, scale2, gain2[...], d_hidden)
        padf[rows, :] = d_residual
        d_branch = d_residual.astype(bf16)
        hid_own[rows, :] = d_branch
        da_temp[...] = dot_nt(d_branch, wproj[...]).astype(bf16)
        for pair in range(PAIRS):
            queries = proj[rows, columns(0, pair)] * jnp.array(score_scale, bf16)
            keys = proj[rows, columns(1, pair)]
            values = proj[rows, columns(2, pair)]
            d_att = da_temp[:, columns(0, pair)]
            d_q = d_k = d_v = None
            for mask in masks:
                own_keys = keys * mask
                chance = softmax_of(queries, own_keys)
                d_chance = dot_nt(d_att, values * mask)
                both = chance * d_chance
                d_scores = (both - chance * jnp.sum(both, -1, keepdims=True)).astype(bf16)
                t_q = dot(d_scores, own_keys)
                t_k = dot_tn(d_scores, queries * mask)
                t_v = dot_tn(chance.astype(bf16), d_att * mask)
                d_q = t_q if d_q is None else d_q + t_q
                d_k = t_k if d_k is None else d_k + t_k
                d_v = t_v if d_v is None else d_v + t_v
            proj[rows, columns(0, pair)] = (d_q * score_scale).astype(bf16)
            proj[rows, columns(1, pair)] = d_k.astype(bf16)
            proj[rows, columns(2, pair)] = d_v.astype(bf16)
        d_normed = dot_nt(proj[rows, :], wqkv[...])
        unit, scale = normalized(tok_p[rows, :].astype(f32))
        sm[0, 0:1, :] += jnp.sum(d_normed * unit, 0, keepdims=True)
        padf[rows, :] += norm_back(unit, scale, gain1[...], d_normed)
        tok_p[rows, :] = (unit * gain1[...]).astype(bf16)
        for when, what in (
            (0, lambda: (go("c1", "d6", "d7", "c2", "p0", "o4"),)),
            (1, lambda: (go("c3", "p1", "r0", "r1", "r2", "r3"), ret_one(1, 1, diag_e).wait_recv(), cross(1, 0),)),
            (2, lambda: (go("o5", "c4", "E0"), cross(1, 1),)),
            (3, lambda: (go("c5", "E1"),)),
        ):

            @pl.when(i == when)
            def _(what=what):
                what()

        return carry

    lax.fori_loop(0, IMAGES, backward_image, 0)

    for part in range(3):
        for half in range(2):
            cols = slice(part * WIDTH + half * 256, part * WIDTH + (half + 1) * 256)
            buf_x[part * WIDTH : (part + 1) * WIDTH, half * 256 : (half + 1) * 256] = dot_tn(
                tok_p[...], proj[:, cols]
            ).astype(bf16)
    for half in range(2):
        cols = slice(half * 256, (half + 1) * 256)
        buf_x[3 * WIDTH : 4 * WIDTH, cols] = dot_tn(att[...], hid_own[:, cols]).astype(bf16)

    plane = ((1 - bx, bz, dev_x), (bx, 1 - bz, dev_z), (1 - bx, 1 - bz, dev_xz))

    def half_at(chunk, bit):
        return pl.ds(pl.multiple_of(chunk * WIDTH + bit * 256, 256), 256)

    def quarter_at(chunk, bit):
        return pl.ds(pl.multiple_of(chunk * WIDTH + core * 256 + bit * 128, 128), 128)

    def plane_at(chunk, x, z):
        return pl.ds(pl.multiple_of(chunk * WIDTH + core * 256 + yy * 128 + z * 64 + x * 32, 32), 32)

    def piece_at(chunk, bit):
        start = chunk * WIDTH + core * 256 + yy * 128 + bz * 64 + bx * 32 + bit * 16
        return pl.ds(pl.multiple_of(start, 16), 16)

    def sum_core(chunk):
        return remote(buf_x.at[half_at(chunk, 1 - core)], rg_c.at[chunk], ar_s.at[0], ar_r.at[chunk, 0], mate)

    def sum_y(chunk):
        return remote(buf_x.at[quarter_at(chunk, 1 - yy)], rg_y.at[chunk], ar_s.at[1], ar_r.at[chunk, 1], mirror)

    def sum_plane(chunk):
        return [
            remote(buf_x.at[plane_at(chunk, x, z)], rg_d.at[chunk, n], ad_s.at[0], ad_r.at[chunk, 0], device)
            for n, (x, z, device) in enumerate(plane)
        ]

    def sum_w(chunk):
        return remote(buf_x.at[piece_at(chunk, 1 - bw)], rg_w.at[chunk], ar_s.at[2], ar_r.at[chunk, 2], dev_w)

    def spread_w(chunk, bit):
        here = buf_g.at[piece_at(chunk, bit)]
        return remote(here, here, ar_s.at[3], ar_r.at[chunk, 3], dev_w)

    def spread_plane(chunk):
        copies = []
        here = buf_g.at[plane_at(chunk, bx, bz)]
        for _, _, device in plane:
            copies.append(remote(here, here, ad_s.at[1], ad_r.at[chunk, 1], device))
        return copies

    def spread_y(chunk, bit):
        here = buf_g.at[quarter_at(chunk, bit)]
        return remote(here, here, ar_s.at[4], ar_r.at[chunk, 4], mirror)

    def spread_core(chunk, bit):
        here = buf_g.at[half_at(chunk, bit)]
        return remote(here, here, ar_s.at[5], ar_r.at[chunk, 5], mate)

    def dense_out(chunk):
        rows = slice(chunk * WIDTH, (chunk + 1) * WIDTH)
        return pltpu.make_async_copy(buf_g.at[rows], dense_g.at[rows], o_sem.at[chunk])

    def do_c(chunk):
        sum_core(chunk).wait_recv()
        keep = half_at(chunk, core)
        buf_x[keep, :] = plus(buf_x[keep, :], rg_c[chunk])
        sum_y(chunk).start()

    def do_y(chunk):
        sum_y(chunk).wait_recv()
        keep = quarter_at(chunk, yy)
        buf_x[keep, :] = plus(buf_x[keep, :], rg_y[chunk])
        for copy in sum_plane(chunk):
            copy.start()

    def do_plane(chunk):
        remote(rg_d.at[chunk], rg_d.at[chunk], ad_s.at[0], ad_r.at[chunk, 0], dev_x).wait_recv()
        keep = plane_at(chunk, bx, bz)
        total = buf_x[keep, :].astype(f32)
        for n in range(3):
            total = total + rg_d[chunk, n].astype(f32)
        buf_x[keep, :] = total.astype(bf16)
        sum_w(chunk).start()

    def do_w(chunk):
        sum_w(chunk).wait_recv()
        keep = piece_at(chunk, bw)
        buf_g[keep, :] = plus(buf_x[keep, :], rg_w[chunk])
        spread_w(chunk, bw).start()

    def do_aw(chunk):
        spread_w(chunk, 1 - bw).wait_recv()
        for copy in spread_plane(chunk):
            copy.start()

    def do_aplane(chunk):
        remote(rg_d.at[chunk], rg_d.at[chunk], ad_s.at[1], ad_r.at[chunk, 1], dev_x).wait_recv()
        spread_y(chunk, yy).start()

    def do_ay(chunk):
        spread_y(chunk, 1 - yy).wait_recv()
        spread_core(chunk, core).start()

    def do_ac(chunk):
        spread_core(chunk, 1 - core).wait_recv()
        dense_out(chunk).start()

    little_way = (mate, mirror, dev_x, dev_z, dev_w)

    def little_copy(level):
        return remote(sm.at[level], rsm.at[level], sr_s, sr_r.at[level], little_way[level])

    def little(level):
        little_copy(level).wait_recv()
        sm[level + 1] = sm[level] + rsm[level]
        if level < 4:
            little_copy(level + 1).start()

    def unpad_grad():
        for i in range(IMAGES):
            ig[SEQ * i : SEQ * i + SEQ, :] = padf[i * PAD : i * PAD + SEQ, :]

    def finish_rows():
        sent(rret1, p1_s)
        sent(rret2, p2_s)
        sent(rdg1, q1_s)
        sent(rdg2, q2_s)
        for n, like in enumerate((ri1.at[0:8], ri2.at[0:8], ri1.at[0:8], ri2.at[0:8])):
            sent(like, rs_s.at[n])
        sent(ro1, rs_s.at[5])
        sent(ro2, rs_s.at[6])
        sent(rsm, sr_s)
        for n, like in enumerate((rg_c, rg_y, rg_w, rg_w)):
            sent(like, ar_s.at[n])
        for n in range(2):
            sent(rg_d, ad_s.at[n])
        for i in range(IMAGES):
            rows = slice(i * PAD, (i + 1) * PAD)
            ret_two(1, i).wait_recv()
            value = (
                resid[rows, :]
                + hid_all[ep, rows, :].astype(f32)
                + rret1[1, 0, rows, :].astype(f32)
                + rret2[1, rows, :].astype(f32)
            )
            acc[SEQ * i : SEQ * i + SEQ, :] = value[0:SEQ, :]
        out[...] = acc[0:788, :].astype(bf16)

    for chunk in range(4):
        sum_core(chunk).start()
    little_copy(0).start()
    unpad_grad()
    pltpu.make_async_copy(ig, ig_g, f_sem.at[0]).start()
    moves.update({
        "Y": do_y, "P": do_plane, "W": do_w, "A": do_aw, "B": do_aplane, "G": do_ay, "C": do_ac,
        "S": do_c, "L": little, "X": lambda n: cross(1, n),
    })
    go("S0", "S1", "S2", "S3", "o6", "E2", "L0", "c6", "h0", "Y0", "E3", "p2", "Y1", "E4")
    go("o7", "c7", "Y2", "e0", "P0", "e1", "E5", "Y3", "X2", "P1", "W0", "e2", "E6", "f0")
    go("p3", "r4", "P2", "W1", "A0", "X3", "L1", "e3", "E7", "f1", "r5", "P3", "W2", "A1")
    go("B0", "e4", "f2", "r6", "q0", "W3", "A2", "B1", "L2", "e5", "f3", "r7", "h1", "G0")
    go("A3", "B2", "e6", "f4", "C0", "L3", "B3", "G1", "g0", "e7", "f5", "C1", "G2", "f6")
    go("C2", "L4", "f7", "G3", "C3")
    finish_rows()
    pltpu.make_async_copy(out, out_g, f_sem.at[1]).start()
    go("q1", "g1")
    small_g[...] = sm[5]
    pltpu.make_async_copy(ig, ig_g, f_sem.at[0]).wait()
    pltpu.make_async_copy(out, out_g, f_sem.at[1]).wait()

    sent(ri3, rs_s.at[4])
    sent(ro3, rs_s.at[7])
    sent(rg_y, ar_s.at[4])
    sent(rg_c, ar_s.at[5])
    for chunk in range(4):
        dense_out(chunk).wait()
    for n in range(2):
        pltpu.make_async_copy(ri3, ri3, li_sem.at[n]).wait()
        pltpu.make_async_copy(ro3, ro3, lo_sem.at[n]).wait()


def finish_kernel(
    out_in, ig_in, dense_in, small_in, win_a, win_b, wout_a, wout_b,
    out, ig, gain1_g, qkv_g, proj_g, gain2_g, router_g, win_g, wout_g,
    dense, small, in_a, in_b, out_a, out_b, qkv, projected, in_sum, out_sum, rows_f, rows_b, sems, leave,
):
    parts = [slice(part * WIDTH, (part + 1) * WIDTH) for part in range(4)]
    pairs = [(small_in, small)] + [(dense_in.at[rows], dense.at[rows]) for rows in parts]
    pairs += [(win_a, in_a), (win_b, in_b), (wout_a, out_a), (wout_b, out_b), (ig_in, rows_f), (out_in, rows_b)]
    fetch = [pltpu.make_async_copy(a, b, sems.at[n]) for n, (a, b) in enumerate(pairs)]
    for copy in fetch:
        copy.start()
    put = [
        pltpu.make_async_copy(a, b, leave.at[n])
        for n, (a, b) in enumerate(
            ((in_sum, win_g), (out_sum, wout_g), (projected, proj_g), (rows_f, ig), (rows_b, out))
        )
    ]
    fetch[0].wait()
    gain1_g[...] = small[0, :]
    gain2_g[...] = small[1, :]
    router_g[...] = small[8:16, :]
    for part, rows in enumerate(parts[:3]):
        fetch[1 + part].wait()
        qkv[:, rows] = dense[rows, :].astype(f32)
        pltpu.make_async_copy(qkv.at[:, rows], qkv_g.at[:, rows], leave.at[6 + part]).start()
    fetch[4].wait()
    projected[...] = dense[3 * WIDTH :, :].astype(f32)
    put[2].start()
    fetch[5].wait()
    fetch[6].wait()
    in_sum[...] = in_a[...].astype(f32) + in_b[...].astype(f32)
    put[0].start()
    fetch[7].wait()
    fetch[8].wait()
    out_sum[...] = out_a[...].astype(f32) + out_b[...].astype(f32)
    put[1].start()
    fetch[9].wait()
    put[3].start()
    fetch[10].wait()
    put[4].start()
    for part, rows in enumerate(parts[:3]):
        pltpu.make_async_copy(qkv.at[:, rows], qkv_g.at[:, rows], leave.at[6 + part]).wait()
    for copy in put:
        copy.wait()


def fused(
    tokens, ln1_gain, w_qkv, w_proj, ln2_gain, w_router, w_in, w_out, noise, choices, slots, cotangent
):
    vmem = pl.BlockSpec(memory_space=pltpu.VMEM)
    anywhere = pl.BlockSpec(memory_space=pl.ANY)
    dma = pltpu.SemaphoreType.DMA
    v = pltpu.VMEM
    rows = (ROWS, WIDTH)
    scratch = [
        v((WIDTH, 3 * WIDTH), bf16), v((WIDTH, WIDTH), bf16), v((16, 896), f32), v((16, ROWS), f32),
        v((788, WIDTH), bf16), v((788, WIDTH), f32),
        v(rows, f32), v(rows, bf16), v(rows, bf16), v(rows, bf16), v((ROWS, 3 * WIDTH), bf16), v(rows, bf16),
        v(rows, f32), v((PAD, WIDTH), bf16), v((8, ROWS), f32), v((4, 8, ROWS), f32),
        v((4, *rows), bf16), v((4, *rows), bf16),
        v((2 * PLACES, WIDTH), bf16), v((2 * PLACES, WIDTH), bf16), v((2 * PLACES, WIDTH), bf16),
        v((2, WIDTH, WIDE), bf16), v((2, WIDE, WIDTH), bf16),
        v((ROWS, WIDE), bf16), v((ROWS, WIDE), bf16), v((PLACES, WIDTH), f32), v((WIDTH, 2 * SLOT_PAD), bf16),
        v((2 * CHUNKS, 2, 2, 2, SHARE_IN, CHUNK), bf16), v((2, 2, 2, 2, CHUNK, WIDTH), bf16),
        v((2 * CHUNKS, 2, 2, SHARE_IN, CHUNK), bf16), v((2 * CHUNKS, 2, SHARE_IN, CHUNK), bf16),
        v((2 * CHUNKS, SHARE_IN, CHUNK), bf16),
        v((UNITS, CHUNK, WIDTH), bf16), v((2, 2, CHUNK, WIDTH), bf16), v((2, CHUNK, WIDTH), bf16),
        v((2, 2, *rows), bf16), v((2, *rows), bf16),
        v((4, 8, ROWS), f32), v((2, 8, ROWS), f32), v((8, ROWS), f32),
        v((4, 256, WIDTH), bf16), v((4, 128, WIDTH), bf16), v((4, 3, 32, WIDTH), bf16), v((4, 16, WIDTH), bf16), v((6, 16, WIDTH), f32), v((5, 16, WIDTH), f32),
        dma((4,)), dma((2, 2)), dma((4,)), dma((2,)), dma((2,)),
        dma((2,)), dma((2, IMAGES)), dma((2,)), dma((2,)), dma((3,)), dma((3,)),
        dma, dma((2, 2)), dma, dma((2, IMAGES)), dma, dma((2,)), dma, dma,
        dma((8,)), dma((4, UNITS)), dma((2, 2)), dma((UNITS,)), dma((2, 2)), dma((2,)),
        dma((6,)), dma((4, 6)), dma((2,)), dma((4, 2)), dma, dma((5,)),
    ]
    share_in = jax.ShapeDtypeStruct((2, SHARE_IN, CHUNK * CHUNKS), bf16)
    share_out = jax.ShapeDtypeStruct((2, CHUNK, WIDTH), bf16)
    results = pl.pallas_call(
        block_kernel,
        out_shape=(
            jax.ShapeDtypeStruct((788, WIDTH), bf16),
            jax.ShapeDtypeStruct((788, WIDTH), f32),
            jax.ShapeDtypeStruct((4 * WIDTH, WIDTH), bf16),
            jax.ShapeDtypeStruct((16, WIDTH), f32),
            share_in, share_in, share_out, share_out,
        ),
        in_specs=[anywhere] * 2 + [vmem] * 2 + [anywhere] * 2 + [vmem] * 4 + [anywhere] * 2,
        out_specs=(anywhere, anywhere, anywhere, vmem) + (anywhere,) * 4,
        scratch_shapes=scratch,
        compiler_params=pltpu.CompilerParams(
            collective_id=0, has_side_effects=True, vmem_limit_bytes=61 << 20
        ),
        name="block",
    )(
        tokens, cotangent, ln1_gain[None, :], ln2_gain[None, :], w_qkv, w_proj, w_router.T,
        noise.T, choices.T, slots.T, w_in, w_out
    )
    ended = pl.pallas_call(
        finish_kernel,
        out_shape=(
            jax.ShapeDtypeStruct((788, WIDTH), bf16),
            jax.ShapeDtypeStruct((788, WIDTH), f32),
            jax.ShapeDtypeStruct((WIDTH,), f32),
            jax.ShapeDtypeStruct((WIDTH, 3 * WIDTH), f32),
            jax.ShapeDtypeStruct((WIDTH, WIDTH), f32),
            jax.ShapeDtypeStruct((WIDTH,), f32),
            jax.ShapeDtypeStruct((8, WIDTH), f32),
            jax.ShapeDtypeStruct((2, SHARE_IN, CHUNK * CHUNKS), f32),
            jax.ShapeDtypeStruct((2, CHUNK, WIDTH), f32),
        ),
        in_specs=[anywhere] * 8,
        out_specs=(anywhere, anywhere, vmem, anywhere, anywhere, vmem, vmem, anywhere, anywhere),
        scratch_shapes=[
            v((4 * WIDTH, WIDTH), bf16), v((16, WIDTH), f32),
            v((2, SHARE_IN, CHUNK * CHUNKS), bf16), v((2, SHARE_IN, CHUNK * CHUNKS), bf16),
            v((2, CHUNK, WIDTH), bf16), v((2, CHUNK, WIDTH), bf16),
            v((WIDTH, 3 * WIDTH), f32), v((WIDTH, WIDTH), f32),
            v((2, SHARE_IN, CHUNK * CHUNKS), f32), v((2, CHUNK, WIDTH), f32),
            v((788, WIDTH), f32), v((788, WIDTH), bf16), dma((11,)), dma((9,)),
        ],
        compiler_params=pltpu.CompilerParams(vmem_limit_bytes=60 << 20),
        name="finish",
    )(*results)
    return (*ended[:6], ended[6].T, *ended[7:])


def solution(mesh):
    in_specs = (
        P(("rep", "ep"), None),
        P(),
        P(),
        P(),
        P(),
        P(),
        P("ep", None, None),
        P("ep", None, None),
        P(("rep", "ep"), None),
        P(("rep", "ep"), None),
        P(("rep", "ep"), None),
        P(("rep", "ep"), None),
    )
    out_specs = (
        P(("rep", "ep"), None),
        P(("rep", "ep"), None),
        P(),
        P(),
        P(),
        P(),
        P(),
        P("ep", "rep", None),
        P("ep", "rep", None),
    )
    whole = fused if dict(mesh.shape) == {"rep": 8, "ep": 4} else local
    return jax.shard_map(whole, mesh=mesh, in_specs=in_specs, out_specs=out_specs, check_vma=False)
```

```python
import functools

import jax
import jax.numpy as jnp
from jax import lax
from jax.experimental import pallas as pl
from jax.experimental.pallas import tpu as pltpu
from jax.sharding import PartitionSpec as P

HEADS = 8
HEAD_DIM = 64
SEQ = 197
CAP = 246


epsilon = 1e-06


def layer_norm(source, gain_row):
    row_mean = jnp.mean(source, -1, keepdims=True)
    centered = source - row_mean
    spread = jnp.mean(centered * centered, -1, keepdims=True)
    return centered * lax.rsqrt(spread + epsilon) * gain_row


def expert_hidden(arrived, w_in):
    hidden_pre = jnp.einsum("jrd,jdf->jrf", arrived, w_in, preferred_element_type=jnp.float32)
    return (hidden_pre, jax.nn.gelu(hidden_pre).astype(jnp.bfloat16))


def local(
    tokens,
    ln1_gain,
    w_qkv,
    w_proj,
    ln2_gain,
    w_router,
    w_in,
    w_out,
    noise,
    choices,
    slots,
    cotangent,
):
    row_count, model_width = tokens.shape
    experts_all = w_router.shape[1]
    images = row_count // SEQ
    score_scale = HEAD_DIM ** (-0.5)
    source = tokens.astype(jnp.float32)
    normed, norm1_back = jax.vjp(layer_norm, source, ln1_gain)
    normed_low = normed.astype(jnp.bfloat16)
    projected = jnp.dot(normed_low, w_qkv, preferred_element_type=jnp.float32).astype(jnp.bfloat16)

    def heads_of(columns):
        return columns.reshape(images, SEQ, HEADS, HEAD_DIM)

    queries = heads_of(projected[:, :model_width])
    keys_all = heads_of(projected[:, model_width : 2 * model_width])
    values_all = heads_of(projected[:, 2 * model_width :])
    scores = (
        jnp.einsum("ishd,ithd->ihst", queries, keys_all, preferred_element_type=jnp.float32)
        * score_scale
    )
    logsum = jax.nn.logsumexp(scores, -1, keepdims=True)
    attention = jnp.exp(scores - logsum).astype(jnp.bfloat16)
    attended = jnp.einsum(
        "ihst,ithd->ishd", attention, values_all, preferred_element_type=jnp.float32
    )
    attended = attended.reshape(row_count, model_width).astype(jnp.bfloat16)
    residual = source + jnp.dot(attended, w_proj, preferred_element_type=jnp.float32)
    normed2, norm2_back = jax.vjp(layer_norm, residual, ln2_gain)
    hidden = normed2.astype(jnp.bfloat16)
    logits = jnp.dot(hidden, w_router, preferred_element_type=jnp.float32)

    def routing(logit_rows):
        return jnp.take_along_axis(jax.nn.softmax(logit_rows + noise, -1), choices, 1)

    picked_gate, routing_back = jax.vjp(routing, logits)
    kept_pair = slots < CAP
    kept_float = kept_pair.astype(jnp.float32)
    slot_index = jnp.where(kept_pair, choices * CAP + slots, experts_all * CAP)
    read_index = jnp.minimum(slot_index, experts_all * CAP - 1)
    pair_gate = picked_gate * kept_float

    def place(pair_rows):
        flat_rows = pair_rows.reshape(row_count * 2, model_width)
        filled = (
            jnp.zeros((experts_all * CAP, model_width), jnp.bfloat16)
            .at[slot_index.reshape(-1)]
            .set(flat_rows, mode="drop")
        )
        return filled.reshape(experts_all, CAP, model_width)

    hidden_pairs = jnp.broadcast_to(hidden[:, None, :], (row_count, 2, model_width))
    arrived = lax.all_to_all(place(hidden_pairs), "ep", split_axis=0, concat_axis=1, tiled=True)
    hidden_pre, hidden_act = expert_hidden(arrived, w_in)
    expert_out = jnp.einsum(
        "jrf,jfd->jrd", hidden_act, w_out, preferred_element_type=jnp.float32
    ).astype(jnp.bfloat16)
    returned = lax.all_to_all(expert_out, "ep", split_axis=1, concat_axis=0, tiled=True).reshape(
        experts_all * CAP, model_width
    )
    gathered = returned[read_index].astype(jnp.float32)
    output = residual + jnp.sum(pair_gate[..., None] * gathered, 1)
    upstream = cotangent.astype(jnp.float32)
    d_gate = jnp.sum(upstream[:, None, :] * gathered, -1) * kept_float
    d_pairs = (pair_gate[..., None] * upstream[:, None, :]).astype(jnp.bfloat16)
    grad_rows = lax.all_to_all(place(d_pairs), "ep", split_axis=0, concat_axis=1, tiled=True)
    again_rows, again_pre, again_act = (arrived, hidden_pre, hidden_act)
    d_act = jnp.einsum("jrd,jfd->jrf", grad_rows, w_out, preferred_element_type=jnp.float32)
    gelu_back = jax.vjp(jax.nn.gelu, again_pre)[1]
    d_pre = gelu_back(d_act)[0].astype(jnp.bfloat16)
    d_w_out = jnp.einsum("jrf,jrd->jfd", again_act, grad_rows, preferred_element_type=jnp.float32)
    d_w_in = jnp.einsum("jrd,jrf->jdf", again_rows, d_pre, preferred_element_type=jnp.float32)
    in_share, out_share = (
        lax.psum_scatter(d_w_in, "rep", scatter_dimension=1, tiled=True),
        lax.psum_scatter(d_w_out, "rep", scatter_dimension=1, tiled=True),
    )
    d_rows = jnp.einsum("jrf,jdf->jrd", d_pre, w_in, preferred_element_type=jnp.float32).astype(
        jnp.bfloat16
    )
    d_back = lax.all_to_all(d_rows, "ep", split_axis=1, concat_axis=0, tiled=True).reshape(
        experts_all * CAP, model_width
    )
    d_hidden = jnp.sum(d_back[read_index].astype(jnp.float32) * kept_float[..., None], 1)
    d_logits = routing_back(d_gate)[0].astype(jnp.bfloat16)
    d_w_router = jnp.einsum("td,te->de", hidden, d_logits, preferred_element_type=jnp.float32)
    d_hidden = d_hidden + jnp.einsum(
        "te,de->td", d_logits, w_router, preferred_element_type=jnp.float32
    )
    d_resid_part, d_gain2 = norm2_back(d_hidden)
    d_residual = upstream + d_resid_part
    d_branch = d_residual.astype(jnp.bfloat16)
    d_w_proj = jnp.einsum("td,te->de", attended, d_branch, preferred_element_type=jnp.float32)
    d_attended = jnp.einsum("te,de->td", d_branch, w_proj, preferred_element_type=jnp.float32)
    d_attended = heads_of(d_attended.astype(jnp.bfloat16))
    rescored = (
        jnp.einsum("ishd,ithd->ihst", queries, keys_all, preferred_element_type=jnp.float32)
        * score_scale
    )
    probability = jnp.exp(rescored - logsum)
    d_prob = jnp.einsum(
        "ishd,ithd->ihst", d_attended, values_all, preferred_element_type=jnp.float32
    )
    d_values = jnp.einsum(
        "ihst,ishd->ithd",
        probability.astype(jnp.bfloat16),
        d_attended,
        preferred_element_type=jnp.float32,
    )
    d_scores = (probability * (d_prob - jnp.sum(probability * d_prob, -1, keepdims=True))).astype(
        jnp.bfloat16
    )
    d_queries = (
        jnp.einsum("ihst,ithd->ishd", d_scores, keys_all, preferred_element_type=jnp.float32)
        * score_scale
    )
    d_keys = (
        jnp.einsum("ihst,ishd->ithd", d_scores, queries, preferred_element_type=jnp.float32)
        * score_scale
    )
    d_projected = jnp.concatenate(
        [
            d_queries.reshape(row_count, model_width),
            d_keys.reshape(row_count, model_width),
            d_values.reshape(row_count, model_width),
        ],
        1,
    ).astype(jnp.bfloat16)
    d_w_qkv = jnp.einsum("td,te->de", normed_low, d_projected, preferred_element_type=jnp.float32)
    d_normed = jnp.einsum("te,de->td", d_projected, w_qkv, preferred_element_type=jnp.float32)
    d_source_part, d_gain1 = norm1_back(d_normed)
    input_grad = d_residual + d_source_part
    dense_sums = lax.psum((d_gain1, d_w_qkv, d_w_proj, d_gain2, d_w_router), ("rep", "ep"))
    return (
        output.astype(jnp.bfloat16),
        input_grad,
        dense_sums[0],
        dense_sums[1],
        dense_sums[2],
        dense_sums[3],
        dense_sums[4],
        in_share,
        out_share,
    )


IMAGES = 4
PAD = 208
ROWS = IMAGES * PAD
WIDTH = 512
PAIRS = 4
SLOT_PAD = 256
PLACES = 4 * SLOT_PAD
CHUNK = 256
CHUNKS = 8
WIDE = 2 * CHUNK
STEPS = CHUNKS // 2
UNITS = 8
SHARE_IN = 64
PARTS = 2
MESH = pl.DeviceIdType.MESH
bf16 = jnp.bfloat16
f32 = jnp.float32


def dot(a, b):
    return jnp.dot(a, b, preferred_element_type=f32)


def dot_nt(a, b):
    return lax.dot_general(a, b, (((1,), (1,)), ((), ())), preferred_element_type=f32)


def dot_tn(a, b):
    return lax.dot_general(a, b, (((0,), (0,)), ((), ())), preferred_element_type=f32)


def normalized(source):
    centered = source - jnp.mean(source, -1, keepdims=True)
    scale = lax.rsqrt(jnp.mean(centered * centered, -1, keepdims=True) + epsilon)
    return centered * scale, scale


def norm_back(unit, scale, gain_row, grad):
    d_unit = grad * gain_row
    return scale * (
        d_unit
        - jnp.mean(d_unit, -1, keepdims=True)
        - unit * jnp.mean(d_unit * unit, -1, keepdims=True)
    )


def remote(src, dst, send, recv, device):
    return pltpu.make_async_remote_copy(
        src_ref=src, dst_ref=dst, send_sem=send, recv_sem=recv, device_id=device, device_id_type=MESH
    )


def block_kernel(
    tok, cot, gain1, gain2, w_qkv, w_proj, wrt, noise, choices, slots, w_in, w_out,
    out_g, ig_g, dense_g, small_g, win_a, win_b, wout_a, wout_b,
    wqkv, wproj, table, meta_in, out, ig, padf, tok_p, dy_own, hid_own, proj, att, resid, da_temp, gates, meta, hid_all, dy_all,
    buf_x, buf_g, buf_y, wi_buf, wo_buf, act_s, dpre_s, acc, turned_x,
    dwi, dwo, ri1, ri2, ri3, ro1, ro2, ro3,
    rret1, rret2, dgp, rdg1, rdg2, rg_c, rg_y, rg_d, rg_w, sm, rsm,
    f_sem, w_sem, o_sem, li_sem, lo_sem, ag_s, ag_r, near_r, far_r, m_s, m_r, p1_s, p1_r, p2_s, p2_r, q1_s, q1_r, q2_s, q2_r,
    rs_s, di_r, i3_r, do1_r, do2_r, do3_r, ar_s, ar_r, ad_s, ad_r, sr_s, sr_r,
):
    rep = lax.axis_index("rep")
    ep = lax.axis_index("ep")
    core = lax.rem(ep, 2)
    yy = ep // 2
    bx = lax.rem(rep, 2)
    bz = lax.rem(rep // 2, 2)
    bw = rep // 4
    mate_e = ep + 1 - 2 * core
    mirror_e = ep + 2 - 4 * yy
    diag_e = mate_e + 2 - 4 * yy
    mate = (rep, mate_e)
    mirror = (rep, mirror_e)
    dev_x = (rep + 1 - 2 * bx, ep)
    dev_z = (rep + 2 - 4 * bz, ep)
    dev_w = (rep + 4 - 8 * bw, ep)

    barrier = pltpu.get_barrier_semaphore()
    dev_xz = (rep + 1 - 2 * bx + 2 - 4 * bz, ep)
    for device in (mate, mirror, dev_x, dev_z, dev_xz, dev_w):
        pl.semaphore_signal(barrier, inc=1, device_id=device, device_id_type=MESH)
    fetches = [
        pltpu.make_async_copy(a, b, f_sem.at[n])
        for n, (a, b) in enumerate(((cot, out), (w_qkv, wqkv), (w_proj, wproj), (tok, out)))
    ]
    for fetch in fetches[:3]:
        fetch.start()

    def image_rows(i):
        return pl.ds(pl.multiple_of(i * PAD, 16), PAD)

    row_id = lax.broadcasted_iota(jnp.int32, (PAD, WIDTH), 0)

    def pad_rows(put):
        padf[784:800, :] = jnp.zeros((16, WIDTH), f32)
        padf[0:788, :] = out[...].astype(f32)
        for i in range(IMAGES):
            value = padf[SEQ * i : SEQ * i + PAD, :]
            put(i, jnp.where(row_id < SEQ, value, 0.0).astype(bf16))

    def put_tok(i, value):
        tok_p[i * PAD : (i + 1) * PAD, :] = value

    def put_dy(i, value):
        dy_own[i * PAD : (i + 1) * PAD, :] = value

    fetches[0].wait()
    pad_rows(put_dy)
    fetches[3].start()
    pl.semaphore_wait(barrier, 6)

    stores = (dy_own, hid_own)
    gathered = (dy_all, hid_all)

    def gather_send(kind, i):
        rows = image_rows(i)
        for route, device in ((0, mate), (1, mirror)):
            remote(
                stores[kind].at[rows], gathered[kind].at[ep, rows],
                ag_s.at[kind], near_r.at[kind] if route == 0 else ag_r.at[kind, i], device,
            ).start()

    def gather_forward(kind, i):
        rows = image_rows(i)
        here = gathered[kind].at[mirror_e, rows]
        remote(here, here, ag_s.at[kind], ag_r.at[kind, i], mirror).wait_recv()
        remote(here, here, ag_s.at[kind], far_r.at[kind], mate).start()

    def gather_near(kind):
        here = gathered[kind].at[mate_e]
        remote(here, here, ag_s.at[kind], near_r.at[kind], mate).wait_recv()

    def gather_far(kind):
        here = gathered[kind].at[diag_e]
        remote(here, here, ag_s.at[kind], far_r.at[kind], mate).wait_recv()
        here = gathered[kind].at[0:3]
        remote(here, here, ag_s.at[kind], far_r.at[kind], mate).wait_send()

    def sent(like, semaphore):
        remote(like, like, semaphore, q2_r, mate).wait_send()

    for i in range(IMAGES):
        gather_send(0, i)
    table[...] = jnp.zeros((16, 896), f32)
    table[0:8, 0:788] = noise[...]
    table[8:10, 0:788] = choices[...].astype(f32)
    table[10:12, 0:788] = slots[...].astype(f32)
    lanes = lax.broadcasted_iota(jnp.int32, (16, 896), 1)
    kinds = lax.broadcasted_iota(jnp.int32, (16, 896), 0)
    spaced = jnp.where(kinds < 8, 0.0, jnp.where(kinds < 10, -1.0, float(CAP)))
    flat = table[...]
    for i in range(IMAGES):
        shifted = flat if i == 0 else pltpu.roll(flat, i * (PAD - SEQ), 1)
        spaced = jnp.where((lanes >= i * PAD) & (lanes < i * PAD + SEQ), shifted, spaced)
    meta_in[...] = spaced[:, 0:ROWS]
    fetches[3].wait()
    pad_rows(put_tok)

    def weights(step):
        el = lax.rem(step // STEPS, 2)
        start = pl.multiple_of(lax.rem(step, STEPS) * WIDE, WIDE)
        slot = lax.rem(step, 2)
        return (
            pltpu.make_async_copy(w_in.at[el, :, pl.ds(start, WIDE)], wi_buf.at[slot], w_sem.at[0, slot]),
            pltpu.make_async_copy(w_out.at[el, pl.ds(start, WIDE), :], wo_buf.at[slot], w_sem.at[1, slot]),
        )

    for copy in weights(0):
        copy.start()

    fetches[1].wait()
    fetches[2].wait()
    lane = lax.broadcasted_iota(jnp.int32, (1, 128), 1)
    masks = ((lane < HEAD_DIM).astype(f32).astype(bf16), (lane >= HEAD_DIM).astype(f32).astype(bf16))
    key_col = lax.broadcasted_iota(jnp.int32, (PAD, PAD), 1)
    score_scale = HEAD_DIM ** (-0.5)

    def softmax_of(queries, keys):
        scores = jnp.where(key_col < SEQ, dot_nt(queries, keys), -1e30)
        weight = jnp.exp(scores - jnp.max(scores, -1, keepdims=True))
        return weight / jnp.sum(weight, -1, keepdims=True)

    def columns(part, pair):
        start = part * WIDTH + pair * 128
        return slice(start, start + 128)

    def forward_image(i, carry):
        rows = image_rows(i)
        source = tok_p[rows, :].astype(f32)
        unit, _ = normalized(source)
        normed = (unit * gain1[...]).astype(bf16)
        for part in range(3):
            cols = slice(part * WIDTH, (part + 1) * WIDTH)
            proj[rows, cols] = dot(normed, wqkv[:, cols]).astype(bf16)
        for pair in range(PAIRS):
            queries = proj[rows, columns(0, pair)] * jnp.array(score_scale, bf16)
            keys = proj[rows, columns(1, pair)]
            values = proj[rows, columns(2, pair)]
            total = None
            for mask in masks:
                attention = softmax_of(queries, keys * mask).astype(bf16)
                term = dot(attention, values * mask)
                total = term if total is None else total + term
            att[rows, columns(0, pair)] = total.astype(bf16)
        residual = source + dot(att[rows, :], wproj[...])
        resid[rows, :] = residual
        unit2, _ = normalized(residual)
        hid_own[rows, :] = (unit2 * gain2[...]).astype(bf16)
        gather_send(1, i)

        return carry

    lax.fori_loop(0, IMAGES, forward_image, 0)

    expert_id = lax.broadcasted_iota(jnp.int32, (8, ROWS), 0).astype(f32)

    def picks():
        return [(expert_id == meta_in[8 + c : 9 + c, :]).astype(f32) for c in range(2)]

    logits = dot_nt(wrt[...], hid_own[...]) + meta_in[0:8, :]
    gate_top = jnp.exp(logits - jnp.max(logits, 0, keepdims=True))
    gate_rows = gate_top / jnp.sum(gate_top, 0, keepdims=True)
    gates[...] = gate_rows
    meta[ep] = jnp.zeros((8, ROWS), f32)
    for c, hot in enumerate(picks()):
        slot = meta_in[10 + c : 11 + c, :]
        kept = slot < CAP
        chosen = meta_in[8 + c : 9 + c, :]
        meta[ep, c : c + 1, :] = jnp.where(kept, chosen * SLOT_PAD + slot, -1.0)
        meta[ep, 2 + c : 3 + c, :] = jnp.where(kept, jnp.sum(gate_rows * hot, 0, keepdims=True), 0.0)
    for route, device in ((0, mate), (1, mirror)):
        remote(meta.at[ep], meta.at[ep], m_s.at[route], m_r.at[route], device).start()
    dy_all[ep] = dy_own[...]
    hid_all[ep] = hid_own[...]
    gather_forward(0, 0)
    for kind in range(2):
        gather_near(kind)
    remote(meta.at[mate_e], meta.at[mate_e], m_s.at[0], m_r.at[0], mate).wait_recv()

    slot_id = lax.broadcasted_iota(jnp.int32, (SLOT_PAD, ROWS), 0)

    def hits(s, el):
        first = (2 * ep + el) * SLOT_PAD
        place = (slot_id + first).astype(f32)
        return place == meta[s, 0:1, :], place == meta[s, 1:2, :]

    def hot_of(hit):
        return jnp.where(hit[0] | hit[1], 1.0, 0.0).astype(bf16)

    def slot_gate(s, hit):
        weight = jnp.where(hit[0], meta[s, 2:3, :], 0.0) + jnp.where(hit[1], meta[s, 3:4, :], 0.0)
        return jnp.sum(weight, -1, keepdims=True)

    sources = ((ep, mate_e), (mirror_e, diag_e))

    def slot_rows(pass_id, el, index):
        start = pass_id * PLACES + el * 2 * SLOT_PAD + index * SLOT_PAD
        return pl.ds(pl.multiple_of(start, SLOT_PAD), SLOT_PAD)

    def place_sources(pass_id):
        first, second = sources[pass_id]

        def place_source(index, carry):
            s = first + index * (second - first)
            for el in range(2):
                hit = hits(s, el)
                hot = hot_of(hit)
                rows = slot_rows(pass_id, el, index)
                buf_x[rows, :] = dot(hot, hid_all[s]).astype(bf16)
                placed = dot(hot, dy_all[s])
                buf_y[rows, :] = placed.astype(bf16)
                buf_g[rows, :] = (slot_gate(s, hit) * placed).astype(bf16)
            return carry

        lax.fori_loop(0, 2, place_source, 0)

    place_sources(0)

    def unit_parts(u):
        el = u // 4
        j = u % 4
        even = el * CHUNKS + 2 * j
        return el, j, even

    def copy_o1(u):
        el, j, even = unit_parts(u)
        return remote(dwo.at[el, j // 2, j % 2, 1 - bx], ro1.at[u], rs_s.at[5], do1_r.at[u], dev_x)

    def copy_o2(el, hi):
        return remote(
            dwo.at[el, hi, 1 - bz, bx], ro2.at[el, hi], rs_s.at[6], do2_r.at[el, hi], dev_z
        )

    def copy_o3(el, part):
        rows = slice(part * 64, (part + 1) * 64)
        return remote(
            dwo.at[el, 1 - bw, bz, bx, rows], ro3.at[el, rows], rs_s.at[7], do3_r.at[el], dev_w
        )

    def copy_e1(u):
        el, j, even = unit_parts(u)
        return remote(dwi.at[even, :, :, 1 - bx], ri1.at[even], rs_s.at[0], di_r.at[0, u], dev_x)

    def copy_e2(u):
        el, j, even = unit_parts(u)
        return remote(dwi.at[even, :, 1 - bz, bx], ri2.at[even], rs_s.at[1], di_r.at[1, u], dev_z)

    def copy_d1(u):
        el, j, even = unit_parts(u)
        return remote(dwi.at[even + 1, :, 1 - bz, :], ri1.at[even + 1], rs_s.at[2], di_r.at[2, u], dev_z)

    def copy_d2(u):
        el, j, even = unit_parts(u)
        return remote(dwi.at[even + 1, :, bz, 1 - bx], ri2.at[even + 1], rs_s.at[3], di_r.at[3, u], dev_x)

    def copy_i3(u, odd):
        el, j, even = unit_parts(u)
        return remote(
            dwi.at[even + odd, 1 - bw, bz, bx], ri3.at[even + odd],
            rs_s.at[4], i3_r.at[odd, el], dev_w,
        )

    def leave_in(u, odd):
        el, j, even = unit_parts(u)
        cols = slice((2 * j + odd) * CHUNK, (2 * j + odd + 1) * CHUNK)
        return [
            pltpu.make_async_copy(dwi.at[even + odd, bw, bz, bx], win_a.at[el, :, cols], li_sem.at[0]),
            pltpu.make_async_copy(ri3.at[even + odd], win_b.at[el, :, cols], li_sem.at[1]),
        ]

    def leave_out(el):
        return [
            pltpu.make_async_copy(dwo.at[el, bw, bz, bx], wout_a.at[el], lo_sem.at[0]),
            pltpu.make_async_copy(ro3.at[el], wout_b.at[el], lo_sem.at[1]),
        ]

    def plus(a, b):
        return (a.astype(f32) + b.astype(f32)).astype(bf16)

    def send_o(u):
        copy_o1(u).start()

    def send_e(u):
        copy_e1(u).start()

    def send_d(u):
        copy_d1(u).start()

    def took_o1(u):
        el, j, even = unit_parts(u)
        copy_o1(u).wait_recv()
        if u + 3 < UNITS:
            send_o(u + 3)
        dwo[el, j // 2, j % 2, bx] = plus(dwo[el, j // 2, j % 2, bx], ro1[u])
        if j % 2 == 1:
            copy_o2(el, j // 2).start()

    def took_o2(el, hi):
        copy_o2(el, hi).wait_recv()
        dwo[el, hi, bz, bx] = plus(dwo[el, hi, bz, bx], ro2[el, hi])

    def took_o3(el):
        remote(ro3.at[el], ro3.at[el], rs_s.at[7], do3_r.at[el], dev_w).wait_recv()
        for copy in leave_out(el):
            copy.start()

    def took_e1(u):
        el, j, even = unit_parts(u)
        copy_e1(u).wait_recv()
        dwi[even, :, :, bx] = plus(dwi[even, :, :, bx], ri1[even])
        copy_e2(u).start()

    def took_e2(u):
        el, j, even = unit_parts(u)
        copy_e2(u).wait_recv()
        dwi[even, :, bz, bx] = plus(dwi[even, :, bz, bx], ri2[even])
        copy_i3(u, 0).start()

    def took_d1(u):
        el, j, even = unit_parts(u)
        copy_d1(u).wait_recv()
        dwi[even + 1, :, bz] = plus(dwi[even + 1, :, bz], ri1[even + 1])

    def took_d2(u):
        el, j, even = unit_parts(u)
        copy_d2(u).wait_recv()
        dwi[even + 1, :, bz, bx] = plus(dwi[even + 1, :, bz, bx], ri2[even + 1])
        copy_i3(u, 1).start()

    def took_i3(el, odd):
        group = ri3.at[0:4]
        remote(group, group, rs_s.at[4], i3_r.at[odd, el], dev_w).wait_recv()
        for j in range(4):
            for copy in leave_in(4 * el + j, odd):
                copy.start()

    moves = {
        "O": send_o, "E": send_e, "D": send_d, "o": took_o1, "e": took_e1, "d": took_d1,
        "f": took_e2, "c": took_d2, "K": lambda n: copy_d2(n).start(),
        "p": lambda n: took_o2(n // 2, n % 2), "q": took_o3, "r": lambda n: copy_o3(n // 4, n % 4).start(),
        "g": lambda n: took_i3(n, 0), "h": lambda n: took_i3(n, 1),
    }

    def go(*words):
        for word in words:
            moves[word[:-1]](int(word[-1]))

    gelu_a = 0.7978845608028654
    gelu_b = gelu_a * 0.044715

    half_places = 2 * SLOT_PAD

    def expert_pass(pass_id, extra):
        def expert_step(step, carry):
            turn = pass_id * 2 * STEPS + step
            el = step // STEPS
            k = lax.rem(step, STEPS)
            slot = lax.rem(step, 2)
            first = pl.multiple_of(pass_id * PLACES + el * half_places, half_places)
            whole = pl.ds(first, half_places)
            for copy in weights(turn):
                copy.wait()

            @pl.when(turn + 1 < 4 * STEPS)
            def _():
                for copy in weights(turn + 1):
                    copy.start()

            @pl.when(k == 0)
            def _():
                acc[...] = jnp.zeros((PLACES, WIDTH), f32)
                turned_x[...] = buf_x[whole, :].T

            wi = wi_buf[slot]
            wo = wo_buf[slot]
            for part in range(PARTS):
                size = half_places // PARTS
                rows = slice(part * size, (part + 1) * size)
                rows_r = slice(half_places + part * size, half_places + (part + 1) * size)
                far = pl.ds(pl.multiple_of(first + part * size, size), size)
                pre = dot(buf_x[far, :], wi)
                square = pre * pre
                level = jnp.tanh(pre * (gelu_a + gelu_b * square))
                half = 0.5 + 0.5 * level
                act = (pre * half).astype(bf16)
                slope = half + (0.5 * pre) * (1.0 - level * level) * (gelu_a + 3.0 * gelu_b * square)
                d_act = dot_nt(buf_g[far, :], wo)
                d_pre = (d_act * slope).astype(bf16)
                act_s[rows, :] = act
                dpre_s[rows, :] = d_pre
                acc[rows, :] += dot(act, wo)
                acc[rows_r, :] += dot_nt(d_pre, wi)
            for odd in range(2):
                cols = slice(odd * CHUNK, (odd + 1) * CHUNK)
                grad_out = dot_tn(act_s[0:half_places, cols], buf_g[whole, :])
                grad_in = dot(turned_x[...], dpre_s[0:half_places, cols]).reshape(2, 2, 2, SHARE_IN, CHUNK)
                out_at = (el, k // 2, lax.rem(k, 2), odd)
                in_at = 2 * step + odd
                if pass_id == 1:
                    grad_out = grad_out + dwo[out_at].astype(f32)
                    grad_in = grad_in + dwi[in_at].astype(f32)
                dwo[out_at] = grad_out.astype(bf16)
                dwi[in_at] = grad_in.astype(bf16)
            for when, what in extra:

                @pl.when(step == when)
                def _(what=what):
                    what()

            @pl.when(k == STEPS - 1)
            def _():
                buf_x[whole, :] = acc[0:half_places, :].astype(bf16)
                buf_g[whole, :] = acc[half_places:, :].astype(bf16)

            return carry

        lax.fori_loop(0, 2 * STEPS, expert_step, 0)

    expert_pass(
        0,
        [
            (0, lambda: gather_forward(0, 1)),
            (2, lambda: gather_forward(0, 2)),
            (4, lambda: gather_forward(0, 3)),
            (5, lambda: gather_forward(1, 0)),
            (7, lambda: gather_forward(1, 1)),
        ],
    )

    partial = (dy_all, hid_all)

    def ret_one(kind, which, who):
        return remote(partial[kind].at[who], rret1.at[kind, which], p1_s, p1_r.at[kind, which], mate)

    def ret_two(kind, i):
        rows = image_rows(i)
        return remote(partial[kind].at[mirror_e, rows], rret2.at[kind, rows], p2_s, p2_r.at[kind, i], mirror)

    def gate_one(which, who):
        return remote(dgp.at[who], rdg1.at[which], q1_s, q1_r.at[which], mate)

    def gate_two():
        return remote(dgp.at[mirror_e], rdg2, q2_s, q2_r, mirror)

    turned = (act_s, dpre_s)

    def turn(pass_id, index):
        cols = slice(index * CHUNK, (index + 1) * CHUNK)
        for el in range(2):
            turned[el][:, cols] = hot_of(hits(sources[pass_id][index], el)).T

    def to_rows(pass_id, index, source, target):
        cols = slice(index * CHUNK, (index + 1) * CHUNK)
        s = sources[pass_id][index]

        def rows_of_image(i, carry):
            rows = image_rows(i)
            value = dot(act_s[rows, cols], source[slot_rows(pass_id, 0, index), :])
            value = value + dot(dpre_s[rows, cols], source[slot_rows(pass_id, 1, index), :])
            target[s, rows, :] = value.astype(bf16)
            return carry

        lax.fori_loop(0, IMAGES, rows_of_image, 0)

    def return_source(pass_id, index):
        s = sources[pass_id][index]
        turn(pass_id, index)
        gate_total = [None, None]
        for el in range(2):
            hit = hits(s, el)
            rows = slot_rows(pass_id, el, index)
            result = buf_x[rows, :].astype(f32)
            d_slot = jnp.sum(result * buf_y[rows, :].astype(f32), -1, keepdims=True)
            buf_x[rows, :] = (slot_gate(s, hit) * result).astype(bf16)
            for c in range(2):
                term = jnp.sum(jnp.where(hit[c], d_slot, 0.0), 0, keepdims=True)
                gate_total[c] = term if el == 0 else gate_total[c] + term
        dgp[s] = jnp.zeros((8, ROWS), f32)
        for c in range(2):
            dgp[s, c : c + 1, :] = gate_total[c]
        to_rows(pass_id, index, buf_g, dy_all)

    return_source(0, 1)
    gate_one(0, mate_e).start()
    ret_one(0, 0, mate_e).start()
    gather_forward(1, 2)
    return_source(0, 0)
    gather_forward(1, 3)
    here = meta.at[mirror_e]
    remote(here, here, m_s.at[1], m_r.at[1], mirror).wait_recv()
    remote(here, here, m_s.at[2], m_r.at[2], mate).start()
    for kind in range(2):
        gather_far(kind)
    remote(meta.at[diag_e], meta.at[diag_e], m_s.at[2], m_r.at[2], mate).wait_recv()
    for route in range(3):
        remote(meta.at[ep], meta.at[ep], m_s.at[route], m_r.at[route], mate).wait_send()
    place_sources(1)
    expert_pass(
        1,
        [
            (0, lambda: go("O0", "D0")),
            (1, lambda: go("O1", "D1")),
            (2, lambda: go("O2", "D2")),
            (3, lambda: go("D3")),
            (4, lambda: go("D4", "o0")),
            (5, lambda: go("D5")),
            (6, lambda: go("D6", "o1")),
            (7, lambda: go("D7")),
        ],
    )
    return_source(1, 1)
    gate_one(1, diag_e).start()
    ret_one(0, 1, diag_e).start()
    go("d0", "d1", "o2")
    return_source(1, 0)
    gate_one(1, diag_e).wait_recv()
    dgp[mirror_e] = dgp[mirror_e] + rdg1[1]
    gate_two().start()

    def cross(kind, i):
        rows = slice(i * PAD, (i + 1) * PAD)
        partial[kind][mirror_e, rows, :] = plus(partial[kind][mirror_e, rows, :], rret1[kind, 1, rows, :])
        ret_two(kind, i).start()

    ret_one(0, 1, diag_e).wait_recv()
    for i in range(IMAGES):
        cross(0, i)
    to_rows(1, 1, buf_x, hid_all)
    ret_one(1, 1, diag_e).start()
    turn(0, 1)
    to_rows(0, 1, buf_x, hid_all)
    ret_one(1, 0, mate_e).start()
    to_rows(1, 0, buf_x, hid_all)
    turn(0, 0)
    to_rows(0, 0, buf_x, hid_all)
    go("d2", "d3", "o3", "K0")

    gate_one(0, mate_e).wait_recv()
    gate_two().wait_recv()
    d_gate = dgp[ep] + rdg1[0] + rdg2[...]
    spread = None
    for c, hot in enumerate(picks()):
        term = hot * jnp.where(meta_in[10 + c : 11 + c, :] < CAP, d_gate[c : c + 1, :], 0.0)
        spread = term if spread is None else spread + term
    gate_rows = gates[...]
    d_logits = (gate_rows * (spread - jnp.sum(gate_rows * spread, 0, keepdims=True))).astype(bf16)
    padf[...] = dot_tn(d_logits, wrt[...])
    sm[0, 0:8, :] = jnp.zeros((8, WIDTH), f32)
    sm[0, 8:16, :] = dot(d_logits, hid_own[...])
    for kind in range(2):
        ret_one(kind, 0, mate_e).wait_recv()

    def backward_image(i, carry):
        rows = image_rows(i)
        ret_two(0, i).wait_recv()
        d_hidden = (
            padf[rows, :]
            + dy_all[ep, rows, :].astype(f32)
            + rret1[0, 0, rows, :].astype(f32)
            + rret2[0, rows, :].astype(f32)
        )
        unit2, scale2 = normalized(resid[rows, :])
        sm[0, 1:2, :] += jnp.sum(d_hidden * unit2, 0, keepdims=True)
        d_residual = dy_own[rows, :].astype(f32) + norm_back(unit2, scale2, gain2[...], d_hidden)
        padf[rows, :] = d_residual
        d_branch = d_residual.astype(bf16)
        hid_own[rows, :] = d_branch
        da_temp[...] = dot_nt(d_branch, wproj[...]).astype(bf16)
        for pair in range(PAIRS):
            queries = proj[rows, columns(0, pair)] * jnp.array(score_scale, bf16)
            keys = proj[rows, columns(1, pair)]
            values = proj[rows, columns(2, pair)]
            d_att = da_temp[:, columns(0, pair)]
            d_q = d_k = d_v = None
            for mask in masks:
                own_keys = keys * mask
                chance = softmax_of(queries, own_keys)
                d_chance = dot_nt(d_att, values * mask)
                both = chance * d_chance
                d_scores = (both - chance * jnp.sum(both, -1, keepdims=True)).astype(bf16)
                t_q = dot(d_scores, own_keys)
                t_k = dot_tn(d_scores, queries * mask)
                t_v = dot_tn(chance.astype(bf16), d_att * mask)
                d_q = t_q if d_q is None else d_q + t_q
                d_k = t_k if d_k is None else d_k + t_k
                d_v = t_v if d_v is None else d_v + t_v
            proj[rows, columns(0, pair)] = (d_q * score_scale).astype(bf16)
            proj[rows, columns(1, pair)] = d_k.astype(bf16)
            proj[rows, columns(2, pair)] = d_v.astype(bf16)
        d_normed = dot_nt(proj[rows, :], wqkv[...])
        unit, scale = normalized(tok_p[rows, :].astype(f32))
        sm[0, 0:1, :] += jnp.sum(d_normed * unit, 0, keepdims=True)
        padf[rows, :] += norm_back(unit, scale, gain1[...], d_normed)
        tok_p[rows, :] = (unit * gain1[...]).astype(bf16)
        for when, what in (
            (0, lambda: (go("d4", "d5", "d6", "d7", "o4", "p0", "K1"),)),
            (1, lambda: (go("o5", "p1", "r0", "r1", "r2", "r3", "E0"), ret_one(1, 1, diag_e).wait_recv(), cross(1, 0), go("K2"),)),
            (2, lambda: (go("o6", "E1"), cross(1, 1), cross(1, 2), go("K3"),)),
            (3, lambda: (go("c0", "E2"),)),
        ):

            @pl.when(i == when)
            def _(what=what):
                what()

        return carry

    lax.fori_loop(0, IMAGES, backward_image, 0)

    for part in range(3):
        for half in range(2):
            cols = slice(part * WIDTH + half * 256, part * WIDTH + (half + 1) * 256)
            buf_x[part * WIDTH : (part + 1) * WIDTH, half * 256 : (half + 1) * 256] = dot_tn(
                tok_p[...], proj[:, cols]
            ).astype(bf16)
    for half in range(2):
        cols = slice(half * 256, (half + 1) * 256)
        buf_x[3 * WIDTH : 4 * WIDTH, cols] = dot_tn(att[...], hid_own[:, cols]).astype(bf16)

    plane = ((1 - bx, bz, dev_x), (bx, 1 - bz, dev_z), (1 - bx, 1 - bz, dev_xz))

    def half_at(chunk, bit):
        return pl.ds(pl.multiple_of(chunk * WIDTH + bit * 256, 256), 256)

    def quarter_at(chunk, bit):
        return pl.ds(pl.multiple_of(chunk * WIDTH + core * 256 + bit * 128, 128), 128)

    def plane_at(chunk, x, z):
        return pl.ds(pl.multiple_of(chunk * WIDTH + core * 256 + yy * 128 + z * 64 + x * 32, 32), 32)

    def piece_at(chunk, bit):
        start = chunk * WIDTH + core * 256 + yy * 128 + bz * 64 + bx * 32 + bit * 16
        return pl.ds(pl.multiple_of(start, 16), 16)

    def sum_core(chunk):
        return remote(buf_x.at[half_at(chunk, 1 - core)], rg_c.at[chunk], ar_s.at[0], ar_r.at[chunk, 0], mate)

    def sum_y(chunk):
        return remote(buf_x.at[quarter_at(chunk, 1 - yy)], rg_y.at[chunk], ar_s.at[1], ar_r.at[chunk, 1], mirror)

    def sum_plane(chunk):
        return [
            remote(buf_x.at[plane_at(chunk, x, z)], rg_d.at[chunk, n], ad_s.at[0], ad_r.at[chunk, 0], device)
            for n, (x, z, device) in enumerate(plane)
        ]

    def sum_w(chunk):
        return remote(buf_x.at[piece_at(chunk, 1 - bw)], rg_w.at[chunk], ar_s.at[2], ar_r.at[chunk, 2], dev_w)

    def spread_w(chunk, bit):
        here = buf_g.at[piece_at(chunk, bit)]
        return remote(here, here, ar_s.at[3], ar_r.at[chunk, 3], dev_w)

    def spread_plane(chunk):
        copies = []
        here = buf_g.at[plane_at(chunk, bx, bz)]
        for _, _, device in plane:
            copies.append(remote(here, here, ad_s.at[1], ad_r.at[chunk, 1], device))
        return copies

    def spread_y(chunk, bit):
        here = buf_g.at[quarter_at(chunk, bit)]
        return remote(here, here, ar_s.at[4], ar_r.at[chunk, 4], mirror)

    def spread_core(chunk, bit):
        here = buf_g.at[half_at(chunk, bit)]
        return remote(here, here, ar_s.at[5], ar_r.at[chunk, 5], mate)

    def dense_out(chunk):
        rows = slice(chunk * WIDTH, (chunk + 1) * WIDTH)
        return pltpu.make_async_copy(buf_g.at[rows], dense_g.at[rows], o_sem.at[chunk])

    def do_c(chunk):
        sum_core(chunk).wait_recv()
        keep = half_at(chunk, core)
        buf_x[keep, :] = plus(buf_x[keep, :], rg_c[chunk])
        sum_y(chunk).start()

    def do_y(chunk):
        sum_y(chunk).wait_recv()
        keep = quarter_at(chunk, yy)
        buf_x[keep, :] = plus(buf_x[keep, :], rg_y[chunk])
        for copy in sum_plane(chunk):
            copy.start()

    def do_plane(chunk):
        remote(rg_d.at[chunk], rg_d.at[chunk], ad_s.at[0], ad_r.at[chunk, 0], dev_x).wait_recv()
        keep = plane_at(chunk, bx, bz)
        total = buf_x[keep, :].astype(f32)
        for n in range(3):
            total = total + rg_d[chunk, n].astype(f32)
        buf_x[keep, :] = total.astype(bf16)
        sum_w(chunk).start()

    def do_w(chunk):
        sum_w(chunk).wait_recv()
        keep = piece_at(chunk, bw)
        buf_g[keep, :] = plus(buf_x[keep, :], rg_w[chunk])
        spread_w(chunk, bw).start()

    def do_aw(chunk):
        spread_w(chunk, 1 - bw).wait_recv()
        for copy in spread_plane(chunk):
            copy.start()

    def do_aplane(chunk):
        remote(rg_d.at[chunk], rg_d.at[chunk], ad_s.at[1], ad_r.at[chunk, 1], dev_x).wait_recv()
        spread_y(chunk, yy).start()

    def do_ay(chunk):
        spread_y(chunk, 1 - yy).wait_recv()
        spread_core(chunk, core).start()

    def do_ac(chunk):
        spread_core(chunk, 1 - core).wait_recv()
        dense_out(chunk).start()

    little_way = (mate, mirror, dev_x, dev_z, dev_w)

    def little_copy(level):
        return remote(sm.at[level], rsm.at[level], sr_s, sr_r.at[level], little_way[level])

    def little(level):
        little_copy(level).wait_recv()
        sm[level + 1] = sm[level] + rsm[level]
        if level < 4:
            little_copy(level + 1).start()

    def unpad_grad():
        for i in range(IMAGES):
            ig[SEQ * i : SEQ * i + SEQ, :] = padf[i * PAD : i * PAD + SEQ, :]

    def finish_rows():
        sent(rret1, p1_s)
        sent(rret2, p2_s)
        sent(rdg1, q1_s)
        sent(rdg2, q2_s)
        for n, like in enumerate((ri1.at[0:8], ri2.at[0:8], ri1.at[0:8], ri2.at[0:8])):
            sent(like, rs_s.at[n])
        sent(ro1, rs_s.at[5])
        sent(ro2, rs_s.at[6])
        sent(rsm, sr_s)
        for n, like in enumerate((rg_c, rg_y, rg_w, rg_w)):
            sent(like, ar_s.at[n])
        for n in range(2):
            sent(rg_d, ad_s.at[n])
        for i in range(IMAGES):
            rows = slice(i * PAD, (i + 1) * PAD)
            ret_two(1, i).wait_recv()
            value = (
                resid[rows, :]
                + hid_all[ep, rows, :].astype(f32)
                + rret1[1, 0, rows, :].astype(f32)
                + rret2[1, rows, :].astype(f32)
            )
            acc[SEQ * i : SEQ * i + SEQ, :] = value[0:SEQ, :]
        out[...] = acc[0:788, :].astype(bf16)

    for chunk in range(4):
        sum_core(chunk).start()
    little_copy(0).start()
    unpad_grad()
    pltpu.make_async_copy(ig, ig_g, f_sem.at[0]).start()
    moves.update({
        "Y": do_y, "P": do_plane, "W": do_w, "A": do_aw, "B": do_aplane, "G": do_ay, "C": do_ac,
        "S": do_c, "L": little, "X": lambda n: cross(1, n),
    })
    go("S0", "S1", "S2", "S3", "o7", "c1", "L0", "p2", "e0", "E3", "Y0", "e1", "Y1", "p3")
    go("r4", "P0", "e2", "E4", "f0", "c2", "Y2", "L1", "P1", "W0", "f1", "Y3", "r5", "P2")
    go("W1", "A0", "e3", "E5", "L2", "f2", "P3", "W2", "A1", "X3", "e4", "E6", "B0", "W3")
    go("A2", "L3", "r6", "e5", "E7", "f3", "c3", "K4", "A3", "B1", "G0", "e6", "K5", "r7")
    go("f4", "L4", "c4", "B2", "G1", "C0", "e7", "K6", "f5", "c5", "h0", "K7", "f6", "g0")
    go("B3", "C1", "G2", "f7", "c6", "C2", "G3", "c7", "C3")
    finish_rows()
    pltpu.make_async_copy(out, out_g, f_sem.at[1]).start()
    go("q0", "q1", "g1", "h1")
    small_g[...] = sm[5]
    pltpu.make_async_copy(ig, ig_g, f_sem.at[0]).wait()
    pltpu.make_async_copy(out, out_g, f_sem.at[1]).wait()

    sent(ri3, rs_s.at[4])
    sent(ro3, rs_s.at[7])
    sent(rg_y, ar_s.at[4])
    sent(rg_c, ar_s.at[5])
    for chunk in range(4):
        dense_out(chunk).wait()
    for n in range(2):
        pltpu.make_async_copy(ri3, ri3, li_sem.at[n]).wait()
        pltpu.make_async_copy(ro3, ro3, lo_sem.at[n]).wait()


def finish_kernel(
    out_in, ig_in, dense_in, small_in, win_a, win_b, wout_a, wout_b,
    out, ig, gain1_g, qkv_g, proj_g, gain2_g, router_g, win_g, wout_g,
    dense, small, in_a, in_b, out_a, out_b, qkv, projected, in_sum, out_sum, rows_f, rows_b, sems, leave,
):
    parts = [slice(part * WIDTH, (part + 1) * WIDTH) for part in range(4)]
    pairs = [(small_in, small)] + [(dense_in.at[rows], dense.at[rows]) for rows in parts]
    pairs += [(win_a, in_a), (win_b, in_b), (wout_a, out_a), (wout_b, out_b), (ig_in, rows_f), (out_in, rows_b)]
    fetch = [pltpu.make_async_copy(a, b, sems.at[n]) for n, (a, b) in enumerate(pairs)]
    for copy in fetch:
        copy.start()
    put = [
        pltpu.make_async_copy(a, b, leave.at[n])
        for n, (a, b) in enumerate(
            (
                (in_sum, win_g), (out_sum, wout_g), (projected, proj_g), (rows_f, ig), (rows_b, out), (qkv, qkv_g),
            )
        )
    ]
    fetch[0].wait()
    gain1_g[...] = small[0, :]
    gain2_g[...] = small[1, :]
    router_g[...] = small[8:16, :]
    for part, rows in enumerate(parts[:3]):
        fetch[1 + part].wait()
        qkv[:, rows] = dense[rows, :].astype(f32)
    put[5].start()
    fetch[4].wait()
    projected[...] = dense[3 * WIDTH :, :].astype(f32)
    put[2].start()
    fetch[5].wait()
    fetch[6].wait()
    in_sum[...] = in_a[...].astype(f32) + in_b[...].astype(f32)
    put[0].start()
    fetch[7].wait()
    fetch[8].wait()
    out_sum[...] = out_a[...].astype(f32) + out_b[...].astype(f32)
    put[1].start()
    fetch[9].wait()
    put[3].start()
    fetch[10].wait()
    put[4].start()
    for copy in put:
        copy.wait()


def fused(
    tokens, ln1_gain, w_qkv, w_proj, ln2_gain, w_router, w_in, w_out, noise, choices, slots, cotangent
):
    vmem = pl.BlockSpec(memory_space=pltpu.VMEM)
    anywhere = pl.BlockSpec(memory_space=pl.ANY)
    dma = pltpu.SemaphoreType.DMA
    v = pltpu.VMEM
    rows = (ROWS, WIDTH)
    scratch = [
        v((WIDTH, 3 * WIDTH), bf16), v((WIDTH, WIDTH), bf16), v((16, 896), f32), v((16, ROWS), f32),
        v((788, WIDTH), bf16), v((788, WIDTH), f32),
        v(rows, f32), v(rows, bf16), v(rows, bf16), v(rows, bf16), v((ROWS, 3 * WIDTH), bf16), v(rows, bf16),
        v(rows, f32), v((PAD, WIDTH), bf16), v((8, ROWS), f32), v((4, 8, ROWS), f32),
        v((4, *rows), bf16), v((4, *rows), bf16),
        v((2 * PLACES, WIDTH), bf16), v((2 * PLACES, WIDTH), bf16), v((2 * PLACES, WIDTH), bf16),
        v((2, WIDTH, WIDE), bf16), v((2, WIDE, WIDTH), bf16),
        v((ROWS, WIDE), bf16), v((ROWS, WIDE), bf16), v((PLACES, WIDTH), f32), v((WIDTH, 2 * SLOT_PAD), bf16),
        v((2 * CHUNKS, 2, 2, 2, SHARE_IN, CHUNK), bf16), v((2, 2, 2, 2, CHUNK, WIDTH), bf16),
        v((2 * CHUNKS, 2, 2, SHARE_IN, CHUNK), bf16), v((2 * CHUNKS, 2, SHARE_IN, CHUNK), bf16),
        v((2 * CHUNKS, SHARE_IN, CHUNK), bf16),
        v((UNITS, CHUNK, WIDTH), bf16), v((2, 2, CHUNK, WIDTH), bf16), v((2, CHUNK, WIDTH), bf16),
        v((2, 2, *rows), bf16), v((2, *rows), bf16),
        v((4, 8, ROWS), f32), v((2, 8, ROWS), f32), v((8, ROWS), f32),
        v((4, 256, WIDTH), bf16), v((4, 128, WIDTH), bf16), v((4, 3, 32, WIDTH), bf16), v((4, 16, WIDTH), bf16), v((6, 16, WIDTH), f32), v((5, 16, WIDTH), f32),
        dma((4,)), dma((2, 2)), dma((4,)), dma((2,)), dma((2,)),
        dma((2,)), dma((2, IMAGES)), dma((2,)), dma((2,)), dma((3,)), dma((3,)),
        dma, dma((2, 2)), dma, dma((2, IMAGES)), dma, dma((2,)), dma, dma,
        dma((8,)), dma((4, UNITS)), dma((2, 2)), dma((UNITS,)), dma((2, 2)), dma((2,)),
        dma((6,)), dma((4, 6)), dma((2,)), dma((4, 2)), dma, dma((5,)),
    ]
    share_in = jax.ShapeDtypeStruct((2, SHARE_IN, CHUNK * CHUNKS), bf16)
    share_out = jax.ShapeDtypeStruct((2, CHUNK, WIDTH), bf16)
    results = pl.pallas_call(
        block_kernel,
        out_shape=(
            jax.ShapeDtypeStruct((788, WIDTH), bf16),
            jax.ShapeDtypeStruct((788, WIDTH), f32),
            jax.ShapeDtypeStruct((4 * WIDTH, WIDTH), bf16),
            jax.ShapeDtypeStruct((16, WIDTH), f32),
            share_in, share_in, share_out, share_out,
        ),
        in_specs=[anywhere] * 2 + [vmem] * 2 + [anywhere] * 2 + [vmem] * 4 + [anywhere] * 2,
        out_specs=(anywhere, anywhere, anywhere, vmem) + (anywhere,) * 4,
        scratch_shapes=scratch,
        compiler_params=pltpu.CompilerParams(
            collective_id=0, has_side_effects=True, vmem_limit_bytes=61 << 20
        ),
        name="block",
    )(
        tokens, cotangent, ln1_gain[None, :], ln2_gain[None, :], w_qkv, w_proj, w_router.T,
        noise.T, choices.T, slots.T, w_in, w_out
    )
    ended = pl.pallas_call(
        finish_kernel,
        out_shape=(
            jax.ShapeDtypeStruct((788, WIDTH), bf16),
            jax.ShapeDtypeStruct((788, WIDTH), f32),
            jax.ShapeDtypeStruct((WIDTH,), f32),
            jax.ShapeDtypeStruct((WIDTH, 3 * WIDTH), f32),
            jax.ShapeDtypeStruct((WIDTH, WIDTH), f32),
            jax.ShapeDtypeStruct((WIDTH,), f32),
            jax.ShapeDtypeStruct((8, WIDTH), f32),
            jax.ShapeDtypeStruct((2, SHARE_IN, CHUNK * CHUNKS), f32),
            jax.ShapeDtypeStruct((2, CHUNK, WIDTH), f32),
        ),
        in_specs=[anywhere] * 8,
        out_specs=(anywhere, anywhere, vmem, anywhere, anywhere, vmem, vmem, anywhere, anywhere),
        scratch_shapes=[
            v((4 * WIDTH, WIDTH), bf16), v((16, WIDTH), f32),
            v((2, SHARE_IN, CHUNK * CHUNKS), bf16), v((2, SHARE_IN, CHUNK * CHUNKS), bf16),
            v((2, CHUNK, WIDTH), bf16), v((2, CHUNK, WIDTH), bf16),
            v((WIDTH, 3 * WIDTH), f32), v((WIDTH, WIDTH), f32),
            v((2, SHARE_IN, CHUNK * CHUNKS), f32), v((2, CHUNK, WIDTH), f32),
            v((788, WIDTH), f32), v((788, WIDTH), bf16), dma((11,)), dma((6,)),
        ],
        compiler_params=pltpu.CompilerParams(vmem_limit_bytes=60 << 20),
        name="finish",
    )(*results)
    return (*ended[:6], ended[6].T, *ended[7:])


def solution(mesh):
    in_specs = (
        P(("rep", "ep"), None),
        P(),
        P(),
        P(),
        P(),
        P(),
        P("ep", None, None),
        P("ep", None, None),
        P(("rep", "ep"), None),
        P(("rep", "ep"), None),
        P(("rep", "ep"), None),
        P(("rep", "ep"), None),
    )
    out_specs = (
        P(("rep", "ep"), None),
        P(("rep", "ep"), None),
        P(),
        P(),
        P(),
        P(),
        P(),
        P("ep", "rep", None),
        P("ep", "rep", None),
    )
    whole = fused if dict(mesh.shape) == {"rep": 8, "ep": 4} else local
    return jax.shard_map(whole, mesh=mesh, in_specs=in_specs, out_specs=out_specs, check_vma=False)
```

```python
import functools

import jax
import jax.numpy as jnp
from jax import lax
from jax.experimental import pallas as pl
from jax.experimental.pallas import tpu as pltpu
from jax.sharding import PartitionSpec as P

HEADS = 8
HEAD_DIM = 64
SEQ = 197
CAP = 246


epsilon = 1e-06


def layer_norm(source, gain_row):
    row_mean = jnp.mean(source, -1, keepdims=True)
    centered = source - row_mean
    spread = jnp.mean(centered * centered, -1, keepdims=True)
    return centered * lax.rsqrt(spread + epsilon) * gain_row


def expert_hidden(arrived, w_in):
    hidden_pre = jnp.einsum("jrd,jdf->jrf", arrived, w_in, preferred_element_type=jnp.float32)
    return (hidden_pre, jax.nn.gelu(hidden_pre).astype(jnp.bfloat16))


def local(
    tokens,
    ln1_gain,
    w_qkv,
    w_proj,
    ln2_gain,
    w_router,
    w_in,
    w_out,
    noise,
    choices,
    slots,
    cotangent,
):
    row_count, model_width = tokens.shape
    experts_all = w_router.shape[1]
    images = row_count // SEQ
    score_scale = HEAD_DIM ** (-0.5)
    source = tokens.astype(jnp.float32)
    normed, norm1_back = jax.vjp(layer_norm, source, ln1_gain)
    normed_low = normed.astype(jnp.bfloat16)
    projected = jnp.dot(normed_low, w_qkv, preferred_element_type=jnp.float32).astype(jnp.bfloat16)

    def heads_of(columns):
        return columns.reshape(images, SEQ, HEADS, HEAD_DIM)

    queries = heads_of(projected[:, :model_width])
    keys_all = heads_of(projected[:, model_width : 2 * model_width])
    values_all = heads_of(projected[:, 2 * model_width :])
    scores = (
        jnp.einsum("ishd,ithd->ihst", queries, keys_all, preferred_element_type=jnp.float32)
        * score_scale
    )
    logsum = jax.nn.logsumexp(scores, -1, keepdims=True)
    attention = jnp.exp(scores - logsum).astype(jnp.bfloat16)
    attended = jnp.einsum(
        "ihst,ithd->ishd", attention, values_all, preferred_element_type=jnp.float32
    )
    attended = attended.reshape(row_count, model_width).astype(jnp.bfloat16)
    residual = source + jnp.dot(attended, w_proj, preferred_element_type=jnp.float32)
    normed2, norm2_back = jax.vjp(layer_norm, residual, ln2_gain)
    hidden = normed2.astype(jnp.bfloat16)
    logits = jnp.dot(hidden, w_router, preferred_element_type=jnp.float32)

    def routing(logit_rows):
        return jnp.take_along_axis(jax.nn.softmax(logit_rows + noise, -1), choices, 1)

    picked_gate, routing_back = jax.vjp(routing, logits)
    kept_pair = slots < CAP
    kept_float = kept_pair.astype(jnp.float32)
    slot_index = jnp.where(kept_pair, choices * CAP + slots, experts_all * CAP)
    read_index = jnp.minimum(slot_index, experts_all * CAP - 1)
    pair_gate = picked_gate * kept_float

    def place(pair_rows):
        flat_rows = pair_rows.reshape(row_count * 2, model_width)
        filled = (
            jnp.zeros((experts_all * CAP, model_width), jnp.bfloat16)
            .at[slot_index.reshape(-1)]
            .set(flat_rows, mode="drop")
        )
        return filled.reshape(experts_all, CAP, model_width)

    hidden_pairs = jnp.broadcast_to(hidden[:, None, :], (row_count, 2, model_width))
    arrived = lax.all_to_all(place(hidden_pairs), "ep", split_axis=0, concat_axis=1, tiled=True)
    hidden_pre, hidden_act = expert_hidden(arrived, w_in)
    expert_out = jnp.einsum(
        "jrf,jfd->jrd", hidden_act, w_out, preferred_element_type=jnp.float32
    ).astype(jnp.bfloat16)
    returned = lax.all_to_all(expert_out, "ep", split_axis=1, concat_axis=0, tiled=True).reshape(
        experts_all * CAP, model_width
    )
    gathered = returned[read_index].astype(jnp.float32)
    output = residual + jnp.sum(pair_gate[..., None] * gathered, 1)
    upstream = cotangent.astype(jnp.float32)
    d_gate = jnp.sum(upstream[:, None, :] * gathered, -1) * kept_float
    d_pairs = (pair_gate[..., None] * upstream[:, None, :]).astype(jnp.bfloat16)
    grad_rows = lax.all_to_all(place(d_pairs), "ep", split_axis=0, concat_axis=1, tiled=True)
    again_rows, again_pre, again_act = (arrived, hidden_pre, hidden_act)
    d_act = jnp.einsum("jrd,jfd->jrf", grad_rows, w_out, preferred_element_type=jnp.float32)
    gelu_back = jax.vjp(jax.nn.gelu, again_pre)[1]
    d_pre = gelu_back(d_act)[0].astype(jnp.bfloat16)
    d_w_out = jnp.einsum("jrf,jrd->jfd", again_act, grad_rows, preferred_element_type=jnp.float32)
    d_w_in = jnp.einsum("jrd,jrf->jdf", again_rows, d_pre, preferred_element_type=jnp.float32)
    in_share, out_share = (
        lax.psum_scatter(d_w_in, "rep", scatter_dimension=1, tiled=True),
        lax.psum_scatter(d_w_out, "rep", scatter_dimension=1, tiled=True),
    )
    d_rows = jnp.einsum("jrf,jdf->jrd", d_pre, w_in, preferred_element_type=jnp.float32).astype(
        jnp.bfloat16
    )
    d_back = lax.all_to_all(d_rows, "ep", split_axis=1, concat_axis=0, tiled=True).reshape(
        experts_all * CAP, model_width
    )
    d_hidden = jnp.sum(d_back[read_index].astype(jnp.float32) * kept_float[..., None], 1)
    d_logits = routing_back(d_gate)[0].astype(jnp.bfloat16)
    d_w_router = jnp.einsum("td,te->de", hidden, d_logits, preferred_element_type=jnp.float32)
    d_hidden = d_hidden + jnp.einsum(
        "te,de->td", d_logits, w_router, preferred_element_type=jnp.float32
    )
    d_resid_part, d_gain2 = norm2_back(d_hidden)
    d_residual = upstream + d_resid_part
    d_branch = d_residual.astype(jnp.bfloat16)
    d_w_proj = jnp.einsum("td,te->de", attended, d_branch, preferred_element_type=jnp.float32)
    d_attended = jnp.einsum("te,de->td", d_branch, w_proj, preferred_element_type=jnp.float32)
    d_attended = heads_of(d_attended.astype(jnp.bfloat16))
    rescored = (
        jnp.einsum("ishd,ithd->ihst", queries, keys_all, preferred_element_type=jnp.float32)
        * score_scale
    )
    probability = jnp.exp(rescored - logsum)
    d_prob = jnp.einsum(
        "ishd,ithd->ihst", d_attended, values_all, preferred_element_type=jnp.float32
    )
    d_values = jnp.einsum(
        "ihst,ishd->ithd",
        probability.astype(jnp.bfloat16),
        d_attended,
        preferred_element_type=jnp.float32,
    )
    d_scores = (probability * (d_prob - jnp.sum(probability * d_prob, -1, keepdims=True))).astype(
        jnp.bfloat16
    )
    d_queries = (
        jnp.einsum("ihst,ithd->ishd", d_scores, keys_all, preferred_element_type=jnp.float32)
        * score_scale
    )
    d_keys = (
        jnp.einsum("ihst,ishd->ithd", d_scores, queries, preferred_element_type=jnp.float32)
        * score_scale
    )
    d_projected = jnp.concatenate(
        [
            d_queries.reshape(row_count, model_width),
            d_keys.reshape(row_count, model_width),
            d_values.reshape(row_count, model_width),
        ],
        1,
    ).astype(jnp.bfloat16)
    d_w_qkv = jnp.einsum("td,te->de", normed_low, d_projected, preferred_element_type=jnp.float32)
    d_normed = jnp.einsum("te,de->td", d_projected, w_qkv, preferred_element_type=jnp.float32)
    d_source_part, d_gain1 = norm1_back(d_normed)
    input_grad = d_residual + d_source_part
    dense_sums = lax.psum((d_gain1, d_w_qkv, d_w_proj, d_gain2, d_w_router), ("rep", "ep"))
    return (
        output.astype(jnp.bfloat16),
        input_grad,
        dense_sums[0],
        dense_sums[1],
        dense_sums[2],
        dense_sums[3],
        dense_sums[4],
        in_share,
        out_share,
    )


IMAGES = 4
PAD = 208
ROWS = IMAGES * PAD
WIDTH = 512
PAIRS = 4
SLOT_PAD = 256
PLACES = 4 * SLOT_PAD
CHUNK = 256
CHUNKS = 8
WIDE = 2 * CHUNK
STEPS = CHUNKS // 2
UNITS = 8
SHARE_IN = 64
PARTS = 2
MESH = pl.DeviceIdType.MESH
bf16 = jnp.bfloat16
f32 = jnp.float32


def dot(a, b):
    return jnp.dot(a, b, preferred_element_type=f32)


def dot_nt(a, b):
    return lax.dot_general(a, b, (((1,), (1,)), ((), ())), preferred_element_type=f32)


def dot_tn(a, b):
    return lax.dot_general(a, b, (((0,), (0,)), ((), ())), preferred_element_type=f32)


def normalized(source):
    centered = source - jnp.mean(source, -1, keepdims=True)
    scale = lax.rsqrt(jnp.mean(centered * centered, -1, keepdims=True) + epsilon)
    return centered * scale, scale


def norm_back(unit, scale, gain_row, grad):
    d_unit = grad * gain_row
    return scale * (
        d_unit
        - jnp.mean(d_unit, -1, keepdims=True)
        - unit * jnp.mean(d_unit * unit, -1, keepdims=True)
    )


def remote(src, dst, send, recv, device):
    return pltpu.make_async_remote_copy(
        src_ref=src, dst_ref=dst, send_sem=send, recv_sem=recv, device_id=device, device_id_type=MESH
    )


def block_kernel(
    tok, cot, gain1, gain2, w_qkv, w_proj, wrt, noise, choices, slots, w_in, w_out,
    out_g, ig_g, dense_g, small_g, win_a, win_b, wout_a, wout_b,
    wqkv, wproj, table, meta_in, out, ig, padf, tok_p, dy_own, hid_own, proj, att, resid, da_temp, gates, meta, hid_all, dy_all,
    buf_x, buf_g, buf_y, wi_buf, wo_buf, act_s, dpre_s, acc, turned_x,
    dwi, dwo, ri1, ri2, ri3, ro1, ro2, ro3,
    rret1, rret2, dgp, rdg1, rdg2, rg_c, rg_y, rg_d, rg_w, sm, rsm,
    f_sem, w_sem, o_sem, li_sem, lo_sem, ag_s, ag_r, near_r, far_r, m_s, m_r, p1_s, p1_r, p2_s, p2_r, q1_s, q1_r, q2_s, q2_r,
    rs_s, di_r, i3_r, do1_r, do2_r, do3_r, ar_s, ar_r, ad_s, ad_r, sr_s, sr_r,
):
    rep = lax.axis_index("rep")
    ep = lax.axis_index("ep")
    core = lax.rem(ep, 2)
    yy = ep // 2
    bx = lax.rem(rep, 2)
    bz = lax.rem(rep // 2, 2)
    bw = rep // 4
    mate_e = ep + 1 - 2 * core
    mirror_e = ep + 2 - 4 * yy
    diag_e = mate_e + 2 - 4 * yy
    mate = (rep, mate_e)
    mirror = (rep, mirror_e)
    dev_x = (rep + 1 - 2 * bx, ep)
    dev_z = (rep + 2 - 4 * bz, ep)
    dev_w = (rep + 4 - 8 * bw, ep)

    barrier = pltpu.get_barrier_semaphore()
    dev_xz = (rep + 1 - 2 * bx + 2 - 4 * bz, ep)
    for device in (mate, mirror, dev_x, dev_z, dev_xz, dev_w):
        pl.semaphore_signal(barrier, inc=1, device_id=device, device_id_type=MESH)
    fetches = [
        pltpu.make_async_copy(a, b, f_sem.at[n])
        for n, (a, b) in enumerate(((cot, out), (w_qkv, wqkv), (w_proj, wproj), (tok, out)))
    ]
    for fetch in fetches[:3]:
        fetch.start()

    def image_rows(i):
        return pl.ds(pl.multiple_of(i * PAD, 16), PAD)

    row_id = lax.broadcasted_iota(jnp.int32, (PAD, WIDTH), 0)

    def pad_rows(put):
        padf[784:800, :] = jnp.zeros((16, WIDTH), f32)
        padf[0:788, :] = out[...].astype(f32)
        for i in range(IMAGES):
            value = padf[SEQ * i : SEQ * i + PAD, :]
            put(i, jnp.where(row_id < SEQ, value, 0.0).astype(bf16))

    def put_tok(i, value):
        tok_p[i * PAD : (i + 1) * PAD, :] = value

    def put_dy(i, value):
        dy_own[i * PAD : (i + 1) * PAD, :] = value

    fetches[0].wait()
    pad_rows(put_dy)
    fetches[3].start()
    pl.semaphore_wait(barrier, 6)

    stores = (dy_own, hid_own)
    gathered = (dy_all, hid_all)

    def gather_send(kind, i):
        rows = image_rows(i)
        for route, device in ((0, mate), (1, mirror)):
            remote(
                stores[kind].at[rows], gathered[kind].at[ep, rows],
                ag_s.at[kind], near_r.at[kind] if route == 0 else ag_r.at[kind, i], device,
            ).start()

    def gather_forward(kind, i):
        rows = image_rows(i)
        here = gathered[kind].at[mirror_e, rows]
        remote(here, here, ag_s.at[kind], ag_r.at[kind, i], mirror).wait_recv()
        remote(here, here, ag_s.at[kind], far_r.at[kind], mate).start()

    def gather_near(kind):
        here = gathered[kind].at[mate_e]
        remote(here, here, ag_s.at[kind], near_r.at[kind], mate).wait_recv()

    def gather_far(kind):
        here = gathered[kind].at[diag_e]
        remote(here, here, ag_s.at[kind], far_r.at[kind], mate).wait_recv()
        here = gathered[kind].at[0:3]
        remote(here, here, ag_s.at[kind], far_r.at[kind], mate).wait_send()

    def sent(like, semaphore):
        remote(like, like, semaphore, q2_r, mate).wait_send()

    for i in range(IMAGES):
        gather_send(0, i)
    table[...] = jnp.zeros((16, 896), f32)
    table[0:8, 0:788] = noise[...]
    table[8:10, 0:788] = choices[...].astype(f32)
    table[10:12, 0:788] = slots[...].astype(f32)
    lanes = lax.broadcasted_iota(jnp.int32, (16, 896), 1)
    kinds = lax.broadcasted_iota(jnp.int32, (16, 896), 0)
    spaced = jnp.where(kinds < 8, 0.0, jnp.where(kinds < 10, -1.0, float(CAP)))
    flat = table[...]
    for i in range(IMAGES):
        shifted = flat if i == 0 else pltpu.roll(flat, i * (PAD - SEQ), 1)
        spaced = jnp.where((lanes >= i * PAD) & (lanes < i * PAD + SEQ), shifted, spaced)
    meta_in[...] = spaced[:, 0:ROWS]
    fetches[3].wait()
    pad_rows(put_tok)

    def weights(step):
        el = lax.rem(step // STEPS, 2)
        start = pl.multiple_of(lax.rem(step, STEPS) * WIDE, WIDE)
        slot = lax.rem(step, 2)
        return (
            pltpu.make_async_copy(w_in.at[el, :, pl.ds(start, WIDE)], wi_buf.at[slot], w_sem.at[0, slot]),
            pltpu.make_async_copy(w_out.at[el, pl.ds(start, WIDE), :], wo_buf.at[slot], w_sem.at[1, slot]),
        )

    for copy in weights(0):
        copy.start()

    fetches[1].wait()
    fetches[2].wait()
    lane = lax.broadcasted_iota(jnp.int32, (1, 128), 1)
    masks = ((lane < HEAD_DIM).astype(f32).astype(bf16), (lane >= HEAD_DIM).astype(f32).astype(bf16))
    key_col = lax.broadcasted_iota(jnp.int32, (PAD, PAD), 1)
    score_scale = HEAD_DIM ** (-0.5)

    def softmax_of(queries, keys):
        scores = jnp.where(key_col < SEQ, dot_nt(queries, keys), -1e30)
        weight = jnp.exp(scores - jnp.max(scores, -1, keepdims=True))
        return weight / jnp.sum(weight, -1, keepdims=True)

    def columns(part, pair):
        start = part * WIDTH + pair * 128
        return slice(start, start + 128)

    def forward_image(i, carry):
        rows = image_rows(i)
        source = tok_p[rows, :].astype(f32)
        unit, _ = normalized(source)
        normed = (unit * gain1[...]).astype(bf16)
        for part in range(3):
            cols = slice(part * WIDTH, (part + 1) * WIDTH)
            proj[rows, cols] = dot(normed, wqkv[:, cols]).astype(bf16)
        for pair in range(PAIRS):
            queries = proj[rows, columns(0, pair)] * jnp.array(score_scale, bf16)
            keys = proj[rows, columns(1, pair)]
            values = proj[rows, columns(2, pair)]
            total = None
            for mask in masks:
                attention = softmax_of(queries, keys * mask).astype(bf16)
                term = dot(attention, values * mask)
                total = term if total is None else total + term
            att[rows, columns(0, pair)] = total.astype(bf16)
        residual = source + dot(att[rows, :], wproj[...])
        resid[rows, :] = residual
        unit2, _ = normalized(residual)
        hid_own[rows, :] = (unit2 * gain2[...]).astype(bf16)
        gather_send(1, i)

        return carry

    lax.fori_loop(0, IMAGES, forward_image, 0)

    expert_id = lax.broadcasted_iota(jnp.int32, (8, ROWS), 0).astype(f32)

    def picks():
        return [(expert_id == meta_in[8 + c : 9 + c, :]).astype(f32) for c in range(2)]

    logits = dot_nt(wrt[...], hid_own[...]) + meta_in[0:8, :]
    gate_top = jnp.exp(logits - jnp.max(logits, 0, keepdims=True))
    gate_rows = gate_top / jnp.sum(gate_top, 0, keepdims=True)
    gates[...] = gate_rows
    meta[ep] = jnp.zeros((8, ROWS), f32)
    for c, hot in enumerate(picks()):
        slot = meta_in[10 + c : 11 + c, :]
        kept = slot < CAP
        chosen = meta_in[8 + c : 9 + c, :]
        meta[ep, c : c + 1, :] = jnp.where(kept, chosen * SLOT_PAD + slot, -1.0)
        meta[ep, 2 + c : 3 + c, :] = jnp.where(kept, jnp.sum(gate_rows * hot, 0, keepdims=True), 0.0)
    for route, device in ((0, mate), (1, mirror)):
        remote(meta.at[ep], meta.at[ep], m_s.at[route], m_r.at[route], device).start()
    dy_all[ep] = dy_own[...]
    hid_all[ep] = hid_own[...]
    gather_forward(0, 0)
    for kind in range(2):
        gather_near(kind)
    remote(meta.at[mate_e], meta.at[mate_e], m_s.at[0], m_r.at[0], mate).wait_recv()

    slot_id = lax.broadcasted_iota(jnp.int32, (SLOT_PAD, ROWS), 0)

    def hits(s, el):
        first = (2 * ep + el) * SLOT_PAD
        place = (slot_id + first).astype(f32)
        return place == meta[s, 0:1, :], place == meta[s, 1:2, :]

    def hot_of(hit):
        return jnp.where(hit[0] | hit[1], 1.0, 0.0).astype(bf16)

    def slot_gate(s, hit):
        weight = jnp.where(hit[0], meta[s, 2:3, :], 0.0) + jnp.where(hit[1], meta[s, 3:4, :], 0.0)
        return jnp.sum(weight, -1, keepdims=True)

    sources = ((ep, mate_e), (mirror_e, diag_e))

    def slot_rows(pass_id, el, index):
        start = pass_id * PLACES + el * 2 * SLOT_PAD + index * SLOT_PAD
        return pl.ds(pl.multiple_of(start, SLOT_PAD), SLOT_PAD)

    def place_one(pass_id, index, el):
        s = sources[pass_id][index]
        hit = hits(s, el)
        hot = hot_of(hit)
        rows = slot_rows(pass_id, el, index)
        buf_x[rows, :] = dot(hot, hid_all[s]).astype(bf16)
        placed = dot(hot, dy_all[s])
        buf_y[rows, :] = placed.astype(bf16)
        buf_g[rows, :] = (slot_gate(s, hit) * placed).astype(bf16)

    for el in range(2):
        for index in range(2):
            place_one(0, index, el)

    def unit_parts(u):
        el = u // 4
        j = u % 4
        even = el * CHUNKS + 2 * j
        return el, j, even

    def copy_o1(u):
        el, j, even = unit_parts(u)
        return remote(dwo.at[el, j // 2, j % 2, 1 - bx], ro1.at[u], rs_s.at[5], do1_r.at[u], dev_x)

    def copy_o2(el, hi):
        return remote(
            dwo.at[el, hi, 1 - bz, bx], ro2.at[el, hi], rs_s.at[6], do2_r.at[el, hi], dev_z
        )

    def copy_o3(el, part):
        rows = slice(part * 64, (part + 1) * 64)
        return remote(
            dwo.at[el, 1 - bw, bz, bx, rows], ro3.at[el, rows], rs_s.at[7], do3_r.at[el], dev_w
        )

    def copy_e1(u):
        el, j, even = unit_parts(u)
        return remote(dwi.at[even, :, :, 1 - bx], ri1.at[even], rs_s.at[0], di_r.at[0, u], dev_x)

    def copy_e2(u):
        el, j, even = unit_parts(u)
        return remote(dwi.at[even, :, 1 - bz, bx], ri2.at[even], rs_s.at[1], di_r.at[1, u], dev_z)

    def copy_d1(u):
        el, j, even = unit_parts(u)
        return remote(dwi.at[even + 1, :, 1 - bz, :], ri1.at[even + 1], rs_s.at[2], di_r.at[2, u], dev_z)

    def copy_d2(u):
        el, j, even = unit_parts(u)
        return remote(dwi.at[even + 1, :, bz, 1 - bx], ri2.at[even + 1], rs_s.at[3], di_r.at[3, u], dev_x)

    def copy_i3(u, odd):
        el, j, even = unit_parts(u)
        return remote(
            dwi.at[even + odd, 1 - bw, bz, bx], ri3.at[even + odd],
            rs_s.at[4], i3_r.at[odd, el], dev_w,
        )

    def leave_in(u, odd):
        el, j, even = unit_parts(u)
        cols = slice((2 * j + odd) * CHUNK, (2 * j + odd + 1) * CHUNK)
        return [
            pltpu.make_async_copy(dwi.at[even + odd, bw, bz, bx], win_a.at[el, :, cols], li_sem.at[0]),
            pltpu.make_async_copy(ri3.at[even + odd], win_b.at[el, :, cols], li_sem.at[1]),
        ]

    def leave_out(el):
        return [
            pltpu.make_async_copy(dwo.at[el, bw, bz, bx], wout_a.at[el], lo_sem.at[0]),
            pltpu.make_async_copy(ro3.at[el], wout_b.at[el], lo_sem.at[1]),
        ]

    def plus(a, b):
        return (a.astype(f32) + b.astype(f32)).astype(bf16)

    def send_o(u):
        copy_o1(u).start()

    def send_e(u):
        copy_e1(u).start()

    def send_d(u):
        copy_d1(u).start()

    def took_o1(u):
        el, j, even = unit_parts(u)
        copy_o1(u).wait_recv()
        if u + 3 < UNITS:
            send_o(u + 3)
        dwo[el, j // 2, j % 2, bx] = plus(dwo[el, j // 2, j % 2, bx], ro1[u])
        if j % 2 == 1:
            copy_o2(el, j // 2).start()

    def took_o2(el, hi):
        copy_o2(el, hi).wait_recv()
        dwo[el, hi, bz, bx] = plus(dwo[el, hi, bz, bx], ro2[el, hi])

    def took_o3(el):
        remote(ro3.at[el], ro3.at[el], rs_s.at[7], do3_r.at[el], dev_w).wait_recv()
        for copy in leave_out(el):
            copy.start()

    def took_e1(u):
        el, j, even = unit_parts(u)
        copy_e1(u).wait_recv()
        dwi[even, :, :, bx] = plus(dwi[even, :, :, bx], ri1[even])
        copy_e2(u).start()

    def took_e2(u):
        el, j, even = unit_parts(u)
        copy_e2(u).wait_recv()
        dwi[even, :, bz, bx] = plus(dwi[even, :, bz, bx], ri2[even])
        copy_i3(u, 0).start()

    def took_d1(u):
        el, j, even = unit_parts(u)
        copy_d1(u).wait_recv()
        dwi[even + 1, :, bz] = plus(dwi[even + 1, :, bz], ri1[even + 1])

    def took_d2(u):
        el, j, even = unit_parts(u)
        copy_d2(u).wait_recv()
        dwi[even + 1, :, bz, bx] = plus(dwi[even + 1, :, bz, bx], ri2[even + 1])
        copy_i3(u, 1).start()

    def took_i3(el, odd):
        group = ri3.at[0:4]
        remote(group, group, rs_s.at[4], i3_r.at[odd, el], dev_w).wait_recv()
        for j in range(4):
            for copy in leave_in(4 * el + j, odd):
                copy.start()

    moves = {
        "O": send_o, "E": send_e, "D": send_d, "o": took_o1, "e": took_e1, "d": took_d1,
        "f": took_e2, "c": took_d2, "K": lambda n: copy_d2(n).start(),
        "p": lambda n: took_o2(n // 2, n % 2), "q": took_o3, "r": lambda n: copy_o3(n // 4, n % 4).start(),
        "g": lambda n: took_i3(n, 0), "h": lambda n: took_i3(n, 1),
    }

    def go(*words):
        for word in words:
            moves[word[:-1]](int(word[-1]))

    gelu_a = 0.7978845608028654
    gelu_b = gelu_a * 0.044715

    half_places = 2 * SLOT_PAD

    def expert_pass(pass_id, extra):
        def expert_step(step, carry):
            turn = pass_id * 2 * STEPS + step
            el = step // STEPS
            k = lax.rem(step, STEPS)
            slot = lax.rem(step, 2)
            first = pl.multiple_of(pass_id * PLACES + el * half_places, half_places)
            whole = pl.ds(first, half_places)
            for copy in weights(turn):
                copy.wait()

            @pl.when(turn + 1 < 4 * STEPS)
            def _():
                for copy in weights(turn + 1):
                    copy.start()

            @pl.when(k == 0)
            def _():
                acc[...] = jnp.zeros((PLACES, WIDTH), f32)
                turned_x[...] = buf_x[whole, :].T

            wi = wi_buf[slot]
            wo = wo_buf[slot]
            for part in range(PARTS):
                size = half_places // PARTS
                rows = slice(part * size, (part + 1) * size)
                rows_r = slice(half_places + part * size, half_places + (part + 1) * size)
                far = pl.ds(pl.multiple_of(first + part * size, size), size)
                pre = dot(buf_x[far, :], wi)
                square = pre * pre
                level = jnp.tanh(pre * (gelu_a + gelu_b * square))
                half = 0.5 + 0.5 * level
                act = (pre * half).astype(bf16)
                slope = half + (0.5 * pre) * (1.0 - level * level) * (gelu_a + 3.0 * gelu_b * square)
                d_act = dot_nt(buf_g[far, :], wo)
                d_pre = (d_act * slope).astype(bf16)
                act_s[rows, :] = act
                dpre_s[rows, :] = d_pre
                acc[rows, :] += dot(act, wo)
                acc[rows_r, :] += dot_nt(d_pre, wi)
            for odd in range(2):
                cols = slice(odd * CHUNK, (odd + 1) * CHUNK)
                grad_out = dot_tn(act_s[0:half_places, cols], buf_g[whole, :])
                grad_in = dot(turned_x[...], dpre_s[0:half_places, cols]).reshape(2, 2, 2, SHARE_IN, CHUNK)
                out_at = (el, k // 2, lax.rem(k, 2), odd)
                in_at = 2 * step + odd
                if pass_id == 1:
                    grad_out = grad_out + dwo[out_at].astype(f32)
                    grad_in = grad_in + dwi[in_at].astype(f32)
                dwo[out_at] = grad_out.astype(bf16)
                dwi[in_at] = grad_in.astype(bf16)
            for when, what in extra:

                @pl.when(step == when)
                def _(what=what):
                    what()

            @pl.when(k == STEPS - 1)
            def _():
                buf_x[whole, :] = acc[0:half_places, :].astype(bf16)
                buf_g[whole, :] = acc[half_places:, :].astype(bf16)

            return carry

        lax.fori_loop(0, 2 * STEPS, expert_step, 0)

    expert_pass(
        0,
        [
            (0, lambda: gather_forward(0, 1)),
            (2, lambda: gather_forward(0, 2)),
            (4, lambda: gather_forward(0, 3)),
            (5, lambda: gather_forward(1, 0)),
            (7, lambda: gather_forward(1, 1)),
        ],
    )

    partial = (dy_all, hid_all)

    def ret_one(kind, which, who):
        return remote(partial[kind].at[who], rret1.at[kind, which], p1_s, p1_r.at[kind, which], mate)

    def ret_two(kind, i):
        rows = image_rows(i)
        return remote(partial[kind].at[mirror_e, rows], rret2.at[kind, rows], p2_s, p2_r.at[kind, i], mirror)

    def gate_one(which, who):
        return remote(dgp.at[who], rdg1.at[which], q1_s, q1_r.at[which], mate)

    def gate_two():
        return remote(dgp.at[mirror_e], rdg2, q2_s, q2_r, mirror)

    turned = (act_s, dpre_s)

    def turn(pass_id, index):
        cols = slice(index * CHUNK, (index + 1) * CHUNK)
        for el in range(2):
            turned[el][:, cols] = hot_of(hits(sources[pass_id][index], el)).T

    def to_rows(pass_id, index, source, target):
        cols = slice(index * CHUNK, (index + 1) * CHUNK)
        s = sources[pass_id][index]

        def rows_of_image(i, carry):
            rows = image_rows(i)
            value = dot(act_s[rows, cols], source[slot_rows(pass_id, 0, index), :])
            value = value + dot(dpre_s[rows, cols], source[slot_rows(pass_id, 1, index), :])
            target[s, rows, :] = value.astype(bf16)
            return carry

        lax.fori_loop(0, IMAGES, rows_of_image, 0)

    def return_source(pass_id, index):
        s = sources[pass_id][index]
        turn(pass_id, index)
        gate_total = [None, None]
        for el in range(2):
            hit = hits(s, el)
            rows = slot_rows(pass_id, el, index)
            result = buf_x[rows, :].astype(f32)
            d_slot = jnp.sum(result * buf_y[rows, :].astype(f32), -1, keepdims=True)
            buf_x[rows, :] = (slot_gate(s, hit) * result).astype(bf16)
            for c in range(2):
                term = jnp.sum(jnp.where(hit[c], d_slot, 0.0), 0, keepdims=True)
                gate_total[c] = term if el == 0 else gate_total[c] + term
        dgp[s] = jnp.zeros((8, ROWS), f32)
        for c in range(2):
            dgp[s, c : c + 1, :] = gate_total[c]
        to_rows(pass_id, index, buf_g, dy_all)

    return_source(0, 1)
    gate_one(0, mate_e).start()
    ret_one(0, 0, mate_e).start()
    gather_forward(1, 2)
    return_source(0, 0)
    gather_forward(1, 3)
    here = meta.at[mirror_e]
    remote(here, here, m_s.at[1], m_r.at[1], mirror).wait_recv()
    remote(here, here, m_s.at[2], m_r.at[2], mate).start()
    place_one(1, 0, 0)
    for kind in range(2):
        gather_far(kind)
    remote(meta.at[diag_e], meta.at[diag_e], m_s.at[2], m_r.at[2], mate).wait_recv()
    for route in range(3):
        remote(meta.at[ep], meta.at[ep], m_s.at[route], m_r.at[route], mate).wait_send()
    place_one(1, 1, 0)
    expert_pass(
        1,
        [
            (0, lambda: go("O0", "D0")),
            (1, lambda: go("O1", "D1")),
            (2, lambda: go("O2", "D2")),
            (3, lambda: (go("D3"), place_one(1, 0, 1), place_one(1, 1, 1))),
            (4, lambda: go("D4", "o0")),
            (5, lambda: go("D5")),
            (6, lambda: go("D6", "o1")),
            (7, lambda: go("D7")),
        ],
    )
    return_source(1, 1)
    gate_one(1, diag_e).start()
    ret_one(0, 1, diag_e).start()
    go("d0", "d1", "o2")
    return_source(1, 0)
    gate_one(1, diag_e).wait_recv()
    dgp[mirror_e] = dgp[mirror_e] + rdg1[1]
    gate_two().start()

    def cross(kind, i):
        rows = slice(i * PAD, (i + 1) * PAD)
        partial[kind][mirror_e, rows, :] = plus(partial[kind][mirror_e, rows, :], rret1[kind, 1, rows, :])
        ret_two(kind, i).start()

    ret_one(0, 1, diag_e).wait_recv()
    for i in range(IMAGES):
        cross(0, i)
    to_rows(1, 1, buf_x, hid_all)
    ret_one(1, 1, diag_e).start()
    turn(0, 1)
    to_rows(0, 1, buf_x, hid_all)
    ret_one(1, 0, mate_e).start()
    to_rows(1, 0, buf_x, hid_all)
    turn(0, 0)
    to_rows(0, 0, buf_x, hid_all)
    go("d2", "d3", "o3", "K0")

    gate_one(0, mate_e).wait_recv()
    gate_two().wait_recv()
    d_gate = dgp[ep] + rdg1[0] + rdg2[...]
    spread = None
    for c, hot in enumerate(picks()):
        term = hot * jnp.where(meta_in[10 + c : 11 + c, :] < CAP, d_gate[c : c + 1, :], 0.0)
        spread = term if spread is None else spread + term
    gate_rows = gates[...]
    d_logits = (gate_rows * (spread - jnp.sum(gate_rows * spread, 0, keepdims=True))).astype(bf16)
    padf[...] = dot_tn(d_logits, wrt[...])
    sm[0, 0:8, :] = jnp.zeros((8, WIDTH), f32)
    sm[0, 8:16, :] = dot(d_logits, hid_own[...])
    for kind in range(2):
        ret_one(kind, 0, mate_e).wait_recv()

    def backward_image(i, carry):
        rows = image_rows(i)
        ret_two(0, i).wait_recv()
        d_hidden = (
            padf[rows, :]
            + dy_all[ep, rows, :].astype(f32)
            + rret1[0, 0, rows, :].astype(f32)
            + rret2[0, rows, :].astype(f32)
        )
        unit2, scale2 = normalized(resid[rows, :])
        sm[0, 1:2, :] += jnp.sum(d_hidden * unit2, 0, keepdims=True)
        d_residual = dy_own[rows, :].astype(f32) + norm_back(unit2, scale2, gain2[...], d_hidden)
        padf[rows, :] = d_residual
        d_branch = d_residual.astype(bf16)
        hid_own[rows, :] = d_branch
        da_temp[...] = dot_nt(d_branch, wproj[...]).astype(bf16)
        for pair in range(PAIRS):
            queries = proj[rows, columns(0, pair)] * jnp.array(score_scale, bf16)
            keys = proj[rows, columns(1, pair)]
            values = proj[rows, columns(2, pair)]
            d_att = da_temp[:, columns(0, pair)]
            d_q = d_k = d_v = None
            for mask in masks:
                own_keys = keys * mask
                chance = softmax_of(queries, own_keys)
                d_chance = dot_nt(d_att, values * mask)
                both = chance * d_chance
                d_scores = (both - chance * jnp.sum(both, -1, keepdims=True)).astype(bf16)
                t_q = dot(d_scores, own_keys)
                t_k = dot_tn(d_scores, queries * mask)
                t_v = dot_tn(chance.astype(bf16), d_att * mask)
                d_q = t_q if d_q is None else d_q + t_q
                d_k = t_k if d_k is None else d_k + t_k
                d_v = t_v if d_v is None else d_v + t_v
            proj[rows, columns(0, pair)] = (d_q * score_scale).astype(bf16)
            proj[rows, columns(1, pair)] = d_k.astype(bf16)
            proj[rows, columns(2, pair)] = d_v.astype(bf16)
        d_normed = dot_nt(proj[rows, :], wqkv[...])
        unit, scale = normalized(tok_p[rows, :].astype(f32))
        sm[0, 0:1, :] += jnp.sum(d_normed * unit, 0, keepdims=True)
        padf[rows, :] += norm_back(unit, scale, gain1[...], d_normed)
        tok_p[rows, :] = (unit * gain1[...]).astype(bf16)
        for when, what in (
            (0, lambda: (go("d4", "d5", "d6", "d7", "o4", "p0", "K1"),)),
            (1, lambda: (go("o5", "p1", "r0", "r1", "r2", "r3", "E0"), ret_one(1, 1, diag_e).wait_recv(), cross(1, 0), go("K2"),)),
            (2, lambda: (go("o6", "E1", "K3", "E2"),)),
            (3, lambda: (go("c0", "o7"),)),
        ):

            @pl.when(i == when)
            def _(what=what):
                what()

        return carry

    lax.fori_loop(0, IMAGES, backward_image, 0)

    for part in range(3):
        for half in range(2):
            cols = slice(part * WIDTH + half * 256, part * WIDTH + (half + 1) * 256)
            buf_x[part * WIDTH : (part + 1) * WIDTH, half * 256 : (half + 1) * 256] = dot_tn(
                tok_p[...], proj[:, cols]
            ).astype(bf16)
    for half in range(2):
        cols = slice(half * 256, (half + 1) * 256)
        buf_x[3 * WIDTH : 4 * WIDTH, cols] = dot_tn(att[...], hid_own[:, cols]).astype(bf16)

    plane = ((1 - bx, bz, dev_x), (bx, 1 - bz, dev_z), (1 - bx, 1 - bz, dev_xz))

    def half_at(chunk, bit):
        return pl.ds(pl.multiple_of(chunk * WIDTH + bit * 256, 256), 256)

    def quarter_at(chunk, bit):
        return pl.ds(pl.multiple_of(chunk * WIDTH + core * 256 + bit * 128, 128), 128)

    def plane_at(chunk, x, z):
        return pl.ds(pl.multiple_of(chunk * WIDTH + core * 256 + yy * 128 + z * 64 + x * 32, 32), 32)

    def piece_at(chunk, bit):
        start = chunk * WIDTH + core * 256 + yy * 128 + bz * 64 + bx * 32 + bit * 16
        return pl.ds(pl.multiple_of(start, 16), 16)

    def sum_core(chunk):
        return remote(buf_x.at[half_at(chunk, 1 - core)], rg_c.at[chunk], ar_s.at[0], ar_r.at[chunk, 0], mate)

    def sum_y(chunk):
        return remote(buf_x.at[quarter_at(chunk, 1 - yy)], rg_y.at[chunk], ar_s.at[1], ar_r.at[chunk, 1], mirror)

    def sum_plane(chunk):
        return [
            remote(buf_x.at[plane_at(chunk, x, z)], rg_d.at[chunk, n], ad_s.at[0], ad_r.at[chunk, 0], device)
            for n, (x, z, device) in enumerate(plane)
        ]

    def sum_w(chunk):
        return remote(buf_x.at[piece_at(chunk, 1 - bw)], rg_w.at[chunk], ar_s.at[2], ar_r.at[chunk, 2], dev_w)

    def spread_w(chunk, bit):
        here = buf_g.at[piece_at(chunk, bit)]
        return remote(here, here, ar_s.at[3], ar_r.at[chunk, 3], dev_w)

    def spread_plane(chunk):
        copies = []
        here = buf_g.at[plane_at(chunk, bx, bz)]
        for _, _, device in plane:
            copies.append(remote(here, here, ad_s.at[1], ad_r.at[chunk, 1], device))
        return copies

    def spread_y(chunk, bit):
        here = buf_g.at[quarter_at(chunk, bit)]
        return remote(here, here, ar_s.at[4], ar_r.at[chunk, 4], mirror)

    def spread_core(chunk, bit):
        here = buf_g.at[half_at(chunk, bit)]
        return remote(here, here, ar_s.at[5], ar_r.at[chunk, 5], mate)

    def dense_out(chunk):
        rows = slice(chunk * WIDTH, (chunk + 1) * WIDTH)
        return pltpu.make_async_copy(buf_g.at[rows], dense_g.at[rows], o_sem.at[chunk])

    def do_c(chunk):
        sum_core(chunk).wait_recv()
        keep = half_at(chunk, core)
        buf_x[keep, :] = plus(buf_x[keep, :], rg_c[chunk])
        sum_y(chunk).start()

    def do_y(chunk):
        sum_y(chunk).wait_recv()
        keep = quarter_at(chunk, yy)
        buf_x[keep, :] = plus(buf_x[keep, :], rg_y[chunk])
        for copy in sum_plane(chunk):
            copy.start()

    def do_plane(chunk):
        remote(rg_d.at[chunk], rg_d.at[chunk], ad_s.at[0], ad_r.at[chunk, 0], dev_x).wait_recv()
        keep = plane_at(chunk, bx, bz)
        total = buf_x[keep, :].astype(f32)
        for n in range(3):
            total = total + rg_d[chunk, n].astype(f32)
        buf_x[keep, :] = total.astype(bf16)
        sum_w(chunk).start()

    def do_w(chunk):
        sum_w(chunk).wait_recv()
        keep = piece_at(chunk, bw)
        buf_g[keep, :] = plus(buf_x[keep, :], rg_w[chunk])
        spread_w(chunk, bw).start()

    def do_aw(chunk):
        spread_w(chunk, 1 - bw).wait_recv()
        for copy in spread_plane(chunk):
            copy.start()

    def do_aplane(chunk):
        remote(rg_d.at[chunk], rg_d.at[chunk], ad_s.at[1], ad_r.at[chunk, 1], dev_x).wait_recv()
        spread_y(chunk, yy).start()

    def do_ay(chunk):
        spread_y(chunk, 1 - yy).wait_recv()
        spread_core(chunk, core).start()

    def do_ac(chunk):
        spread_core(chunk, 1 - core).wait_recv()
        dense_out(chunk).start()

    little_way = (mate, mirror, dev_x, dev_z, dev_w)

    def little_copy(level):
        return remote(sm.at[level], rsm.at[level], sr_s, sr_r.at[level], little_way[level])

    def little(level):
        little_copy(level).wait_recv()
        sm[level + 1] = sm[level] + rsm[level]
        if level < 4:
            little_copy(level + 1).start()

    def unpad_grad():
        for i in range(IMAGES):
            ig[SEQ * i : SEQ * i + SEQ, :] = padf[i * PAD : i * PAD + SEQ, :]

    def finish_rows():
        sent(rret1, p1_s)
        sent(rret2, p2_s)
        sent(rdg1, q1_s)
        sent(rdg2, q2_s)
        for n, like in enumerate((ri1.at[0:8], ri2.at[0:8], ri1.at[0:8], ri2.at[0:8])):
            sent(like, rs_s.at[n])
        sent(ro1, rs_s.at[5])
        sent(ro2, rs_s.at[6])
        sent(rsm, sr_s)
        for n, like in enumerate((rg_c, rg_y, rg_w, rg_w)):
            sent(like, ar_s.at[n])
        for n in range(2):
            sent(rg_d, ad_s.at[n])
        for i in range(IMAGES):
            rows = slice(i * PAD, (i + 1) * PAD)
            ret_two(1, i).wait_recv()
            value = (
                resid[rows, :]
                + hid_all[ep, rows, :].astype(f32)
                + rret1[1, 0, rows, :].astype(f32)
                + rret2[1, rows, :].astype(f32)
            )
            acc[SEQ * i : SEQ * i + SEQ, :] = value[0:SEQ, :]
        out[...] = acc[0:788, :].astype(bf16)

    for chunk in range(4):
        sum_core(chunk).start()
    little_copy(0).start()
    unpad_grad()
    pltpu.make_async_copy(ig, ig_g, f_sem.at[0]).start()
    moves.update({
        "Y": do_y, "P": do_plane, "W": do_w, "A": do_aw, "B": do_aplane, "G": do_ay, "C": do_ac,
        "S": do_c, "L": little, "X": lambda n: cross(1, n),
    })
    go("S0", "S1", "S2", "S3", "E3", "c1", "L0", "e0", "p2", "Y0", "e1", "E4", "Y1", "p3")
    go("r4", "r5", "P0", "X1", "e2", "E5", "f0", "c2", "Y2", "P1", "W0", "L1", "f1", "X2")
    go("Y3", "r6", "e3", "E6", "P2", "W1", "A0", "f2", "X3", "P3", "r7", "W2", "A1", "L2")
    go("e4", "E7", "B0", "W3", "A2", "e5", "f3", "c3", "K4", "A3", "B1", "L3", "G0", "e6")
    go("K5", "f4", "c4", "B2", "G1", "C0", "e7", "K6", "f5", "c5", "L4", "h0", "K7", "f6")
    go("g0", "B3", "C1", "G2", "f7", "c6", "C2", "G3", "c7", "C3")
    finish_rows()
    pltpu.make_async_copy(out, out_g, f_sem.at[1]).start()
    go("q0", "q1", "g1", "h1")
    small_g[...] = sm[5]
    pltpu.make_async_copy(ig, ig_g, f_sem.at[0]).wait()
    pltpu.make_async_copy(out, out_g, f_sem.at[1]).wait()

    sent(ri3, rs_s.at[4])
    sent(ro3, rs_s.at[7])
    sent(rg_y, ar_s.at[4])
    sent(rg_c, ar_s.at[5])
    for chunk in range(4):
        dense_out(chunk).wait()
    for n in range(2):
        pltpu.make_async_copy(ri3, ri3, li_sem.at[n]).wait()
        pltpu.make_async_copy(ro3, ro3, lo_sem.at[n]).wait()


def finish_kernel(
    out_in, ig_in, dense_in, small_in, win_a, win_b, wout_a, wout_b,
    out, ig, gain1_g, qkv_g, proj_g, gain2_g, router_g, win_g, wout_g,
    dense, small, in_a, in_b, out_a, out_b, qkv, projected, in_sum, out_sum, rows_f, rows_b, sems, leave,
):
    parts = [slice(part * WIDTH, (part + 1) * WIDTH) for part in range(4)]
    pairs = [(small_in, small)] + [(dense_in.at[rows], dense.at[rows]) for rows in parts]
    pairs += [(win_a, in_a), (win_b, in_b), (wout_a, out_a), (wout_b, out_b), (ig_in, rows_f), (out_in, rows_b)]
    fetch = [pltpu.make_async_copy(a, b, sems.at[n]) for n, (a, b) in enumerate(pairs)]
    for copy in fetch:
        copy.start()
    put = [
        pltpu.make_async_copy(a, b, leave.at[n])
        for n, (a, b) in enumerate(
            (
                (in_sum, win_g), (out_sum, wout_g), (projected, proj_g), (rows_f, ig), (rows_b, out), (qkv, qkv_g),
            )
        )
    ]
    fetch[0].wait()
    gain1_g[...] = small[0, :]
    gain2_g[...] = small[1, :]
    router_g[...] = small[8:16, :]
    for part, rows in enumerate(parts[:3]):
        fetch[1 + part].wait()
        qkv[:, rows] = dense[rows, :].astype(f32)
    put[5].start()
    fetch[4].wait()
    projected[...] = dense[3 * WIDTH :, :].astype(f32)
    put[2].start()
    fetch[5].wait()
    fetch[6].wait()
    in_sum[...] = in_a[...].astype(f32) + in_b[...].astype(f32)
    put[0].start()
    fetch[7].wait()
    fetch[8].wait()
    out_sum[...] = out_a[...].astype(f32) + out_b[...].astype(f32)
    put[1].start()
    fetch[9].wait()
    put[3].start()
    fetch[10].wait()
    put[4].start()
    for copy in put:
        copy.wait()


def fused(
    tokens, ln1_gain, w_qkv, w_proj, ln2_gain, w_router, w_in, w_out, noise, choices, slots, cotangent
):
    vmem = pl.BlockSpec(memory_space=pltpu.VMEM)
    anywhere = pl.BlockSpec(memory_space=pl.ANY)
    dma = pltpu.SemaphoreType.DMA
    v = pltpu.VMEM
    rows = (ROWS, WIDTH)
    scratch = [
        v((WIDTH, 3 * WIDTH), bf16), v((WIDTH, WIDTH), bf16), v((16, 896), f32), v((16, ROWS), f32),
        v((788, WIDTH), bf16), v((788, WIDTH), f32),
        v(rows, f32), v(rows, bf16), v(rows, bf16), v(rows, bf16), v((ROWS, 3 * WIDTH), bf16), v(rows, bf16),
        v(rows, f32), v((PAD, WIDTH), bf16), v((8, ROWS), f32), v((4, 8, ROWS), f32),
        v((4, *rows), bf16), v((4, *rows), bf16),
        v((2 * PLACES, WIDTH), bf16), v((2 * PLACES, WIDTH), bf16), v((2 * PLACES, WIDTH), bf16),
        v((2, WIDTH, WIDE), bf16), v((2, WIDE, WIDTH), bf16),
        v((ROWS, WIDE), bf16), v((ROWS, WIDE), bf16), v((PLACES, WIDTH), f32), v((WIDTH, 2 * SLOT_PAD), bf16),
        v((2 * CHUNKS, 2, 2, 2, SHARE_IN, CHUNK), bf16), v((2, 2, 2, 2, CHUNK, WIDTH), bf16),
        v((2 * CHUNKS, 2, 2, SHARE_IN, CHUNK), bf16), v((2 * CHUNKS, 2, SHARE_IN, CHUNK), bf16),
        v((2 * CHUNKS, SHARE_IN, CHUNK), bf16),
        v((UNITS, CHUNK, WIDTH), bf16), v((2, 2, CHUNK, WIDTH), bf16), v((2, CHUNK, WIDTH), bf16),
        v((2, 2, *rows), bf16), v((2, *rows), bf16),
        v((4, 8, ROWS), f32), v((2, 8, ROWS), f32), v((8, ROWS), f32),
        v((4, 256, WIDTH), bf16), v((4, 128, WIDTH), bf16), v((4, 3, 32, WIDTH), bf16), v((4, 16, WIDTH), bf16), v((6, 16, WIDTH), f32), v((5, 16, WIDTH), f32),
        dma((4,)), dma((2, 2)), dma((4,)), dma((2,)), dma((2,)),
        dma((2,)), dma((2, IMAGES)), dma((2,)), dma((2,)), dma((3,)), dma((3,)),
        dma, dma((2, 2)), dma, dma((2, IMAGES)), dma, dma((2,)), dma, dma,
        dma((8,)), dma((4, UNITS)), dma((2, 2)), dma((UNITS,)), dma((2, 2)), dma((2,)),
        dma((6,)), dma((4, 6)), dma((2,)), dma((4, 2)), dma, dma((5,)),
    ]
    share_in = jax.ShapeDtypeStruct((2, SHARE_IN, CHUNK * CHUNKS), bf16)
    share_out = jax.ShapeDtypeStruct((2, CHUNK, WIDTH), bf16)
    results = pl.pallas_call(
        block_kernel,
        out_shape=(
            jax.ShapeDtypeStruct((788, WIDTH), bf16),
            jax.ShapeDtypeStruct((788, WIDTH), f32),
            jax.ShapeDtypeStruct((4 * WIDTH, WIDTH), bf16),
            jax.ShapeDtypeStruct((16, WIDTH), f32),
            share_in, share_in, share_out, share_out,
        ),
        in_specs=[anywhere] * 2 + [vmem] * 2 + [anywhere] * 2 + [vmem] * 4 + [anywhere] * 2,
        out_specs=(anywhere, anywhere, anywhere, vmem) + (anywhere,) * 4,
        scratch_shapes=scratch,
        compiler_params=pltpu.CompilerParams(
            collective_id=0, has_side_effects=True, vmem_limit_bytes=61 << 20
        ),
        name="block",
    )(
        tokens, cotangent, ln1_gain[None, :], ln2_gain[None, :], w_qkv, w_proj, w_router.T,
        noise.T, choices.T, slots.T, w_in, w_out
    )
    ended = pl.pallas_call(
        finish_kernel,
        out_shape=(
            jax.ShapeDtypeStruct((788, WIDTH), bf16),
            jax.ShapeDtypeStruct((788, WIDTH), f32),
            jax.ShapeDtypeStruct((WIDTH,), f32),
            jax.ShapeDtypeStruct((WIDTH, 3 * WIDTH), f32),
            jax.ShapeDtypeStruct((WIDTH, WIDTH), f32),
            jax.ShapeDtypeStruct((WIDTH,), f32),
            jax.ShapeDtypeStruct((8, WIDTH), f32),
            jax.ShapeDtypeStruct((2, SHARE_IN, CHUNK * CHUNKS), f32),
            jax.ShapeDtypeStruct((2, CHUNK, WIDTH), f32),
        ),
        in_specs=[anywhere] * 8,
        out_specs=(anywhere, anywhere, vmem, anywhere, anywhere, vmem, vmem, anywhere, anywhere),
        scratch_shapes=[
            v((4 * WIDTH, WIDTH), bf16), v((16, WIDTH), f32),
            v((2, SHARE_IN, CHUNK * CHUNKS), bf16), v((2, SHARE_IN, CHUNK * CHUNKS), bf16),
            v((2, CHUNK, WIDTH), bf16), v((2, CHUNK, WIDTH), bf16),
            v((WIDTH, 3 * WIDTH), f32), v((WIDTH, WIDTH), f32),
            v((2, SHARE_IN, CHUNK * CHUNKS), f32), v((2, CHUNK, WIDTH), f32),
            v((788, WIDTH), f32), v((788, WIDTH), bf16), dma((11,)), dma((6,)),
        ],
        compiler_params=pltpu.CompilerParams(vmem_limit_bytes=60 << 20),
        name="finish",
    )(*results)
    return (*ended[:6], ended[6].T, *ended[7:])


def solution(mesh):
    in_specs = (
        P(("rep", "ep"), None),
        P(),
        P(),
        P(),
        P(),
        P(),
        P("ep", None, None),
        P("ep", None, None),
        P(("rep", "ep"), None),
        P(("rep", "ep"), None),
        P(("rep", "ep"), None),
        P(("rep", "ep"), None),
    )
    out_specs = (
        P(("rep", "ep"), None),
        P(("rep", "ep"), None),
        P(),
        P(),
        P(),
        P(),
        P(),
        P("ep", "rep", None),
        P("ep", "rep", None),
    )
    whole = fused if dict(mesh.shape) == {"rep": 8, "ep": 4} else local
    return jax.shard_map(whole, mesh=mesh, in_specs=in_specs, out_specs=out_specs, check_vma=False)
```

```python
import functools

import jax
import jax.numpy as jnp
from jax import lax
from jax.experimental import pallas as pl
from jax.experimental.pallas import tpu as pltpu
from jax.sharding import PartitionSpec as P

HEADS = 8
HEAD_DIM = 64
SEQ = 197
CAP = 246


epsilon = 1e-06


def layer_norm(source, gain_row):
    row_mean = jnp.mean(source, -1, keepdims=True)
    centered = source - row_mean
    spread = jnp.mean(centered * centered, -1, keepdims=True)
    return centered * lax.rsqrt(spread + epsilon) * gain_row


def expert_hidden(arrived, w_in):
    hidden_pre = jnp.einsum("jrd,jdf->jrf", arrived, w_in, preferred_element_type=jnp.float32)
    return (hidden_pre, jax.nn.gelu(hidden_pre).astype(jnp.bfloat16))


def local(
    tokens,
    ln1_gain,
    w_qkv,
    w_proj,
    ln2_gain,
    w_router,
    w_in,
    w_out,
    noise,
    choices,
    slots,
    cotangent,
):
    row_count, model_width = tokens.shape
    experts_all = w_router.shape[1]
    images = row_count // SEQ
    score_scale = HEAD_DIM ** (-0.5)
    source = tokens.astype(jnp.float32)
    normed, norm1_back = jax.vjp(layer_norm, source, ln1_gain)
    normed_low = normed.astype(jnp.bfloat16)
    projected = jnp.dot(normed_low, w_qkv, preferred_element_type=jnp.float32).astype(jnp.bfloat16)

    def heads_of(columns):
        return columns.reshape(images, SEQ, HEADS, HEAD_DIM)

    queries = heads_of(projected[:, :model_width])
    keys_all = heads_of(projected[:, model_width : 2 * model_width])
    values_all = heads_of(projected[:, 2 * model_width :])
    scores = (
        jnp.einsum("ishd,ithd->ihst", queries, keys_all, preferred_element_type=jnp.float32)
        * score_scale
    )
    logsum = jax.nn.logsumexp(scores, -1, keepdims=True)
    attention = jnp.exp(scores - logsum).astype(jnp.bfloat16)
    attended = jnp.einsum(
        "ihst,ithd->ishd", attention, values_all, preferred_element_type=jnp.float32
    )
    attended = attended.reshape(row_count, model_width).astype(jnp.bfloat16)
    residual = source + jnp.dot(attended, w_proj, preferred_element_type=jnp.float32)
    normed2, norm2_back = jax.vjp(layer_norm, residual, ln2_gain)
    hidden = normed2.astype(jnp.bfloat16)
    logits = jnp.dot(hidden, w_router, preferred_element_type=jnp.float32)

    def routing(logit_rows):
        return jnp.take_along_axis(jax.nn.softmax(logit_rows + noise, -1), choices, 1)

    picked_gate, routing_back = jax.vjp(routing, logits)
    kept_pair = slots < CAP
    kept_float = kept_pair.astype(jnp.float32)
    slot_index = jnp.where(kept_pair, choices * CAP + slots, experts_all * CAP)
    read_index = jnp.minimum(slot_index, experts_all * CAP - 1)
    pair_gate = picked_gate * kept_float

    def place(pair_rows):
        flat_rows = pair_rows.reshape(row_count * 2, model_width)
        filled = (
            jnp.zeros((experts_all * CAP, model_width), jnp.bfloat16)
            .at[slot_index.reshape(-1)]
            .set(flat_rows, mode="drop")
        )
        return filled.reshape(experts_all, CAP, model_width)

    hidden_pairs = jnp.broadcast_to(hidden[:, None, :], (row_count, 2, model_width))
    arrived = lax.all_to_all(place(hidden_pairs), "ep", split_axis=0, concat_axis=1, tiled=True)
    hidden_pre, hidden_act = expert_hidden(arrived, w_in)
    expert_out = jnp.einsum(
        "jrf,jfd->jrd", hidden_act, w_out, preferred_element_type=jnp.float32
    ).astype(jnp.bfloat16)
    returned = lax.all_to_all(expert_out, "ep", split_axis=1, concat_axis=0, tiled=True).reshape(
        experts_all * CAP, model_width
    )
    gathered = returned[read_index].astype(jnp.float32)
    output = residual + jnp.sum(pair_gate[..., None] * gathered, 1)
    upstream = cotangent.astype(jnp.float32)
    d_gate = jnp.sum(upstream[:, None, :] * gathered, -1) * kept_float
    d_pairs = (pair_gate[..., None] * upstream[:, None, :]).astype(jnp.bfloat16)
    grad_rows = lax.all_to_all(place(d_pairs), "ep", split_axis=0, concat_axis=1, tiled=True)
    again_rows, again_pre, again_act = (arrived, hidden_pre, hidden_act)
    d_act = jnp.einsum("jrd,jfd->jrf", grad_rows, w_out, preferred_element_type=jnp.float32)
    gelu_back = jax.vjp(jax.nn.gelu, again_pre)[1]
    d_pre = gelu_back(d_act)[0].astype(jnp.bfloat16)
    d_w_out = jnp.einsum("jrf,jrd->jfd", again_act, grad_rows, preferred_element_type=jnp.float32)
    d_w_in = jnp.einsum("jrd,jrf->jdf", again_rows, d_pre, preferred_element_type=jnp.float32)
    in_share, out_share = (
        lax.psum_scatter(d_w_in, "rep", scatter_dimension=1, tiled=True),
        lax.psum_scatter(d_w_out, "rep", scatter_dimension=1, tiled=True),
    )
    d_rows = jnp.einsum("jrf,jdf->jrd", d_pre, w_in, preferred_element_type=jnp.float32).astype(
        jnp.bfloat16
    )
    d_back = lax.all_to_all(d_rows, "ep", split_axis=1, concat_axis=0, tiled=True).reshape(
        experts_all * CAP, model_width
    )
    d_hidden = jnp.sum(d_back[read_index].astype(jnp.float32) * kept_float[..., None], 1)
    d_logits = routing_back(d_gate)[0].astype(jnp.bfloat16)
    d_w_router = jnp.einsum("td,te->de", hidden, d_logits, preferred_element_type=jnp.float32)
    d_hidden = d_hidden + jnp.einsum(
        "te,de->td", d_logits, w_router, preferred_element_type=jnp.float32
    )
    d_resid_part, d_gain2 = norm2_back(d_hidden)
    d_residual = upstream + d_resid_part
    d_branch = d_residual.astype(jnp.bfloat16)
    d_w_proj = jnp.einsum("td,te->de", attended, d_branch, preferred_element_type=jnp.float32)
    d_attended = jnp.einsum("te,de->td", d_branch, w_proj, preferred_element_type=jnp.float32)
    d_attended = heads_of(d_attended.astype(jnp.bfloat16))
    rescored = (
        jnp.einsum("ishd,ithd->ihst", queries, keys_all, preferred_element_type=jnp.float32)
        * score_scale
    )
    probability = jnp.exp(rescored - logsum)
    d_prob = jnp.einsum(
        "ishd,ithd->ihst", d_attended, values_all, preferred_element_type=jnp.float32
    )
    d_values = jnp.einsum(
        "ihst,ishd->ithd",
        probability.astype(jnp.bfloat16),
        d_attended,
        preferred_element_type=jnp.float32,
    )
    d_scores = (probability * (d_prob - jnp.sum(probability * d_prob, -1, keepdims=True))).astype(
        jnp.bfloat16
    )
    d_queries = (
        jnp.einsum("ihst,ithd->ishd", d_scores, keys_all, preferred_element_type=jnp.float32)
        * score_scale
    )
    d_keys = (
        jnp.einsum("ihst,ishd->ithd", d_scores, queries, preferred_element_type=jnp.float32)
        * score_scale
    )
    d_projected = jnp.concatenate(
        [
            d_queries.reshape(row_count, model_width),
            d_keys.reshape(row_count, model_width),
            d_values.reshape(row_count, model_width),
        ],
        1,
    ).astype(jnp.bfloat16)
    d_w_qkv = jnp.einsum("td,te->de", normed_low, d_projected, preferred_element_type=jnp.float32)
    d_normed = jnp.einsum("te,de->td", d_projected, w_qkv, preferred_element_type=jnp.float32)
    d_source_part, d_gain1 = norm1_back(d_normed)
    input_grad = d_residual + d_source_part
    dense_sums = lax.psum((d_gain1, d_w_qkv, d_w_proj, d_gain2, d_w_router), ("rep", "ep"))
    return (
        output.astype(jnp.bfloat16),
        input_grad,
        dense_sums[0],
        dense_sums[1],
        dense_sums[2],
        dense_sums[3],
        dense_sums[4],
        in_share,
        out_share,
    )


IMAGES = 4
PAD = 208
ROWS = IMAGES * PAD
WIDTH = 512
PAIRS = 4
SLOT_PAD = 256
PLACES = 4 * SLOT_PAD
CHUNK = 256
CHUNKS = 8
WIDE = 2 * CHUNK
STEPS = CHUNKS // 2
UNITS = 8
SHARE_IN = 64
PARTS = 2
MESH = pl.DeviceIdType.MESH
bf16 = jnp.bfloat16
f32 = jnp.float32


def dot(a, b):
    return jnp.dot(a, b, preferred_element_type=f32)


def dot_nt(a, b):
    return lax.dot_general(a, b, (((1,), (1,)), ((), ())), preferred_element_type=f32)


def dot_tn(a, b):
    return lax.dot_general(a, b, (((0,), (0,)), ((), ())), preferred_element_type=f32)


def normalized(source):
    centered = source - jnp.mean(source, -1, keepdims=True)
    scale = lax.rsqrt(jnp.mean(centered * centered, -1, keepdims=True) + epsilon)
    return centered * scale, scale


def norm_back(unit, scale, gain_row, grad):
    d_unit = grad * gain_row
    return scale * (
        d_unit
        - jnp.mean(d_unit, -1, keepdims=True)
        - unit * jnp.mean(d_unit * unit, -1, keepdims=True)
    )


def remote(src, dst, send, recv, device):
    return pltpu.make_async_remote_copy(
        src_ref=src, dst_ref=dst, send_sem=send, recv_sem=recv, device_id=device, device_id_type=MESH
    )


def block_kernel(
    tok, cot, gain1, gain2, w_qkv, w_proj, wrt, noise, choices, slots, w_in, w_out,
    out_g, ig_g, dense_g, small_g, win_a, win_b, wout_a, wout_b,
    wqkv, wproj, table, meta_in, out, ig, padf, tok_p, dy_own, hid_own, proj, att, resid, da_temp, gates, meta, hid_all, dy_all,
    buf_x, buf_g, buf_y, wi_buf, wo_buf, act_s, dpre_s, acc, turned_x,
    dwi, dwo, ri1, ri2, ri3, ro1, ro2, ro3,
    rret1, rret2, dgp, rdg1, rdg2, rg_c, rg_y, rg_d, rg_w, sm, rsm,
    f_sem, w_sem, o_sem, li_sem, lo_sem, ag_s, ag_r, near_r, far_r, m_s, m_r, p1_s, p1_r, p2_s, p2_r, q1_s, q1_r, q2_s, q2_r,
    rs_s, di_r, i3_r, do1_r, do2_r, do3_r, ar_s, ar_r, ad_s, ad_r, sr_s, sr_r,
):
    rep = lax.axis_index("rep")
    ep = lax.axis_index("ep")
    core = lax.rem(ep, 2)
    yy = ep // 2
    bx = lax.rem(rep, 2)
    bz = lax.rem(rep // 2, 2)
    bw = rep // 4
    mate_e = ep + 1 - 2 * core
    mirror_e = ep + 2 - 4 * yy
    diag_e = mate_e + 2 - 4 * yy
    mate = (rep, mate_e)
    mirror = (rep, mirror_e)
    dev_x = (rep + 1 - 2 * bx, ep)
    dev_z = (rep + 2 - 4 * bz, ep)
    dev_w = (rep + 4 - 8 * bw, ep)

    barrier = pltpu.get_barrier_semaphore()
    dev_xz = (rep + 1 - 2 * bx + 2 - 4 * bz, ep)
    for device in (mate, mirror, dev_x, dev_z, dev_xz, dev_w):
        pl.semaphore_signal(barrier, inc=1, device_id=device, device_id_type=MESH)
    fetches = [
        pltpu.make_async_copy(a, b, f_sem.at[n])
        for n, (a, b) in enumerate(((cot, out), (w_qkv, wqkv), (w_proj, wproj), (tok, out)))
    ]
    for fetch in fetches[:3]:
        fetch.start()

    def image_rows(i):
        return pl.ds(pl.multiple_of(i * PAD, 16), PAD)

    row_id = lax.broadcasted_iota(jnp.int32, (PAD, WIDTH), 0)

    def pad_rows(put):
        padf[784:800, :] = jnp.zeros((16, WIDTH), f32)
        padf[0:788, :] = out[...].astype(f32)
        for i in range(IMAGES):
            value = padf[SEQ * i : SEQ * i + PAD, :]
            put(i, jnp.where(row_id < SEQ, value, 0.0).astype(bf16))

    def put_tok(i, value):
        tok_p[i * PAD : (i + 1) * PAD, :] = value

    def put_dy(i, value):
        dy_own[i * PAD : (i + 1) * PAD, :] = value

    fetches[0].wait()
    pad_rows(put_dy)
    fetches[3].start()
    pl.semaphore_wait(barrier, 6)

    stores = (dy_own, hid_own)
    gathered = (dy_all, hid_all)

    def gather_send(kind, i):
        rows = image_rows(i)
        for route, device in ((0, mate), (1, mirror)):
            remote(
                stores[kind].at[rows], gathered[kind].at[ep, rows],
                ag_s.at[kind], near_r.at[kind] if route == 0 else ag_r.at[kind, i], device,
            ).start()

    def gather_forward(kind, i):
        rows = image_rows(i)
        here = gathered[kind].at[mirror_e, rows]
        remote(here, here, ag_s.at[kind], ag_r.at[kind, i], mirror).wait_recv()
        remote(here, here, ag_s.at[kind], far_r.at[kind], mate).start()

    def gather_near(kind):
        here = gathered[kind].at[mate_e]
        remote(here, here, ag_s.at[kind], near_r.at[kind], mate).wait_recv()

    def gather_far(kind):
        here = gathered[kind].at[diag_e]
        remote(here, here, ag_s.at[kind], far_r.at[kind], mate).wait_recv()
        here = gathered[kind].at[0:3]
        remote(here, here, ag_s.at[kind], far_r.at[kind], mate).wait_send()

    def sent(like, semaphore):
        remote(like, like, semaphore, q2_r, mate).wait_send()

    for i in range(IMAGES):
        gather_send(0, i)
    table[...] = jnp.zeros((16, 896), f32)
    table[0:8, 0:788] = noise[...]
    table[8:10, 0:788] = choices[...].astype(f32)
    table[10:12, 0:788] = slots[...].astype(f32)
    lanes = lax.broadcasted_iota(jnp.int32, (16, 896), 1)
    kinds = lax.broadcasted_iota(jnp.int32, (16, 896), 0)
    spaced = jnp.where(kinds < 8, 0.0, jnp.where(kinds < 10, -1.0, float(CAP)))
    flat = table[...]
    for i in range(IMAGES):
        shifted = flat if i == 0 else pltpu.roll(flat, i * (PAD - SEQ), 1)
        spaced = jnp.where((lanes >= i * PAD) & (lanes < i * PAD + SEQ), shifted, spaced)
    meta_in[...] = spaced[:, 0:ROWS]
    fetches[3].wait()
    pad_rows(put_tok)

    def weights(step):
        el = lax.rem(step // STEPS, 2)
        start = pl.multiple_of(lax.rem(step, STEPS) * WIDE, WIDE)
        slot = lax.rem(step, 2)
        return (
            pltpu.make_async_copy(w_in.at[el, :, pl.ds(start, WIDE)], wi_buf.at[slot], w_sem.at[0, slot]),
            pltpu.make_async_copy(w_out.at[el, pl.ds(start, WIDE), :], wo_buf.at[slot], w_sem.at[1, slot]),
        )

    for copy in weights(0):
        copy.start()

    fetches[1].wait()
    fetches[2].wait()
    lane = lax.broadcasted_iota(jnp.int32, (1, 128), 1)
    masks = ((lane < HEAD_DIM).astype(f32).astype(bf16), (lane >= HEAD_DIM).astype(f32).astype(bf16))
    key_col = lax.broadcasted_iota(jnp.int32, (PAD, PAD), 1)
    score_scale = HEAD_DIM ** (-0.5)

    def softmax_of(queries, keys):
        scores = jnp.where(key_col < SEQ, dot_nt(queries, keys), -1e30)
        weight = jnp.exp(scores - jnp.max(scores, -1, keepdims=True))
        return weight / jnp.sum(weight, -1, keepdims=True)

    def columns(part, pair):
        start = part * WIDTH + pair * 128
        return slice(start, start + 128)

    def forward_image(i, carry):
        rows = image_rows(i)
        source = tok_p[rows, :].astype(f32)
        unit, _ = normalized(source)
        normed = (unit * gain1[...]).astype(bf16)
        for part in range(3):
            cols = slice(part * WIDTH, (part + 1) * WIDTH)
            proj[rows, cols] = dot(normed, wqkv[:, cols]).astype(bf16)
        for pair in range(PAIRS):
            queries = proj[rows, columns(0, pair)] * jnp.array(score_scale, bf16)
            keys = proj[rows, columns(1, pair)]
            values = proj[rows, columns(2, pair)]
            total = None
            for mask in masks:
                attention = softmax_of(queries, keys * mask).astype(bf16)
                term = dot(attention, values * mask)
                total = term if total is None else total + term
            att[rows, columns(0, pair)] = total.astype(bf16)
        residual = source + dot(att[rows, :], wproj[...])
        resid[rows, :] = residual
        unit2, _ = normalized(residual)
        hid_own[rows, :] = (unit2 * gain2[...]).astype(bf16)
        gather_send(1, i)

        return carry

    lax.fori_loop(0, IMAGES, forward_image, 0)

    expert_id = lax.broadcasted_iota(jnp.int32, (8, ROWS), 0).astype(f32)

    def picks():
        return [(expert_id == meta_in[8 + c : 9 + c, :]).astype(f32) for c in range(2)]

    logits = dot_nt(wrt[...], hid_own[...]) + meta_in[0:8, :]
    gate_top = jnp.exp(logits - jnp.max(logits, 0, keepdims=True))
    gate_rows = gate_top / jnp.sum(gate_top, 0, keepdims=True)
    gates[...] = gate_rows
    meta[ep] = jnp.zeros((8, ROWS), f32)
    for c, hot in enumerate(picks()):
        slot = meta_in[10 + c : 11 + c, :]
        kept = slot < CAP
        chosen = meta_in[8 + c : 9 + c, :]
        meta[ep, c : c + 1, :] = jnp.where(kept, chosen * SLOT_PAD + slot, -1.0)
        meta[ep, 2 + c : 3 + c, :] = jnp.where(kept, jnp.sum(gate_rows * hot, 0, keepdims=True), 0.0)
    for route, device in ((0, mate), (1, mirror)):
        remote(meta.at[ep], meta.at[ep], m_s.at[route], m_r.at[route], device).start()
    dy_all[ep] = dy_own[...]
    hid_all[ep] = hid_own[...]
    gather_forward(0, 0)
    for kind in range(2):
        gather_near(kind)
    remote(meta.at[mate_e], meta.at[mate_e], m_s.at[0], m_r.at[0], mate).wait_recv()

    slot_id = lax.broadcasted_iota(jnp.int32, (SLOT_PAD, ROWS), 0)

    def hits(s, el):
        first = (2 * ep + el) * SLOT_PAD
        place = (slot_id + first).astype(f32)
        return place == meta[s, 0:1, :], place == meta[s, 1:2, :]

    def hot_of(hit):
        return jnp.where(hit[0] | hit[1], 1.0, 0.0).astype(bf16)

    def slot_gate(s, hit):
        weight = jnp.where(hit[0], meta[s, 2:3, :], 0.0) + jnp.where(hit[1], meta[s, 3:4, :], 0.0)
        return jnp.sum(weight, -1, keepdims=True)

    sources = ((ep, mate_e), (mirror_e, diag_e))

    def slot_rows(pass_id, el, index):
        start = pass_id * PLACES + el * 2 * SLOT_PAD + index * SLOT_PAD
        return pl.ds(pl.multiple_of(start, SLOT_PAD), SLOT_PAD)

    def place_one(pass_id, index, el):
        s = sources[pass_id][index]
        hit = hits(s, el)
        hot = hot_of(hit)
        rows = slot_rows(pass_id, el, index)
        buf_x[rows, :] = dot(hot, hid_all[s]).astype(bf16)
        placed = dot(hot, dy_all[s])
        buf_y[rows, :] = placed.astype(bf16)
        buf_g[rows, :] = (slot_gate(s, hit) * placed).astype(bf16)

    for el in range(2):
        for index in range(2):
            place_one(0, index, el)

    def unit_parts(u):
        el = u // 4
        j = u % 4
        even = el * CHUNKS + 2 * j
        return el, j, even

    def copy_o1(u):
        el, j, even = unit_parts(u)
        return remote(dwo.at[el, j // 2, j % 2, 1 - bx], ro1.at[u], rs_s.at[5], do1_r.at[u], dev_x)

    def copy_o2(el, hi):
        return remote(
            dwo.at[el, hi, 1 - bz, bx], ro2.at[el, hi], rs_s.at[6], do2_r.at[el, hi], dev_z
        )

    def copy_o3(el, part):
        rows = slice(part * 64, (part + 1) * 64)
        return remote(
            dwo.at[el, 1 - bw, bz, bx, rows], ro3.at[el, rows], rs_s.at[7], do3_r.at[el], dev_w
        )

    def copy_e1(u):
        el, j, even = unit_parts(u)
        return remote(dwi.at[even, :, :, 1 - bx], ri1.at[even], rs_s.at[0], di_r.at[0, u], dev_x)

    def copy_e2(u):
        el, j, even = unit_parts(u)
        return remote(dwi.at[even, :, 1 - bz, bx], ri2.at[even], rs_s.at[1], di_r.at[1, u], dev_z)

    def copy_d1(u):
        el, j, even = unit_parts(u)
        return remote(dwi.at[even + 1, :, 1 - bz, :], ri1.at[even + 1], rs_s.at[2], di_r.at[2, u], dev_z)

    def copy_d2(u):
        el, j, even = unit_parts(u)
        return remote(dwi.at[even + 1, :, bz, 1 - bx], ri2.at[even + 1], rs_s.at[3], di_r.at[3, u], dev_x)

    def copy_i3(u, odd):
        el, j, even = unit_parts(u)
        return remote(
            dwi.at[even + odd, 1 - bw, bz, bx], ri3.at[even + odd],
            rs_s.at[4], i3_r.at[odd, el], dev_w,
        )

    def leave_in(u, odd):
        el, j, even = unit_parts(u)
        cols = slice((2 * j + odd) * CHUNK, (2 * j + odd + 1) * CHUNK)
        return [
            pltpu.make_async_copy(dwi.at[even + odd, bw, bz, bx], win_a.at[el, :, cols], li_sem.at[0]),
            pltpu.make_async_copy(ri3.at[even + odd], win_b.at[el, :, cols], li_sem.at[1]),
        ]

    def leave_out(el):
        return [
            pltpu.make_async_copy(dwo.at[el, bw, bz, bx], wout_a.at[el], lo_sem.at[0]),
            pltpu.make_async_copy(ro3.at[el], wout_b.at[el], lo_sem.at[1]),
        ]

    def plus(a, b):
        return (a.astype(f32) + b.astype(f32)).astype(bf16)

    def send_o(u):
        copy_o1(u).start()

    def send_e(u):
        copy_e1(u).start()

    def send_d(u):
        copy_d1(u).start()

    def took_o1(u):
        el, j, even = unit_parts(u)
        copy_o1(u).wait_recv()
        if u + 3 < UNITS:
            send_o(u + 3)
        dwo[el, j // 2, j % 2, bx] = plus(dwo[el, j // 2, j % 2, bx], ro1[u])
        if j % 2 == 1:
            copy_o2(el, j // 2).start()

    def took_o2(el, hi):
        copy_o2(el, hi).wait_recv()
        dwo[el, hi, bz, bx] = plus(dwo[el, hi, bz, bx], ro2[el, hi])

    def took_o3(el):
        remote(ro3.at[el], ro3.at[el], rs_s.at[7], do3_r.at[el], dev_w).wait_recv()
        for copy in leave_out(el):
            copy.start()

    def took_e1(u):
        el, j, even = unit_parts(u)
        copy_e1(u).wait_recv()
        dwi[even, :, :, bx] = plus(dwi[even, :, :, bx], ri1[even])
        copy_e2(u).start()

    def took_e2(u):
        el, j, even = unit_parts(u)
        copy_e2(u).wait_recv()
        dwi[even, :, bz, bx] = plus(dwi[even, :, bz, bx], ri2[even])
        copy_i3(u, 0).start()

    def took_d1(u):
        el, j, even = unit_parts(u)
        copy_d1(u).wait_recv()
        dwi[even + 1, :, bz] = plus(dwi[even + 1, :, bz], ri1[even + 1])

    def took_d2(u):
        el, j, even = unit_parts(u)
        copy_d2(u).wait_recv()
        dwi[even + 1, :, bz, bx] = plus(dwi[even + 1, :, bz, bx], ri2[even + 1])
        copy_i3(u, 1).start()

    def took_i3(el, odd):
        group = ri3.at[0:4]
        remote(group, group, rs_s.at[4], i3_r.at[odd, el], dev_w).wait_recv()
        for j in range(4):
            for copy in leave_in(4 * el + j, odd):
                copy.start()

    moves = {
        "O": send_o, "E": send_e, "D": send_d, "o": took_o1, "e": took_e1, "d": took_d1,
        "f": took_e2, "c": took_d2, "K": lambda n: copy_d2(n).start(),
        "p": lambda n: took_o2(n // 2, n % 2), "q": took_o3, "r": lambda n: copy_o3(n // 4, n % 4).start(),
        "g": lambda n: took_i3(n, 0), "h": lambda n: took_i3(n, 1),
    }

    def go(*words):
        for word in words:
            moves[word[:-1]](int(word[-1]))

    gelu_a = 0.7978845608028654
    gelu_b = gelu_a * 0.044715

    half_places = 2 * SLOT_PAD

    def expert_pass(pass_id, extra):
        def expert_step(step, carry):
            turn = pass_id * 2 * STEPS + step
            el = step // STEPS
            k = lax.rem(step, STEPS)
            slot = lax.rem(step, 2)
            first = pl.multiple_of(pass_id * PLACES + el * half_places, half_places)
            whole = pl.ds(first, half_places)
            for copy in weights(turn):
                copy.wait()

            @pl.when(turn + 1 < 4 * STEPS)
            def _():
                for copy in weights(turn + 1):
                    copy.start()

            @pl.when(k == 0)
            def _():
                acc[...] = jnp.zeros((PLACES, WIDTH), f32)
                turned_x[...] = buf_x[whole, :].T

            wi = wi_buf[slot]
            wo = wo_buf[slot]
            for part in range(PARTS):
                size = half_places // PARTS
                rows = slice(part * size, (part + 1) * size)
                rows_r = slice(half_places + part * size, half_places + (part + 1) * size)
                far = pl.ds(pl.multiple_of(first + part * size, size), size)
                pre = dot(buf_x[far, :], wi)
                square = pre * pre
                level = jnp.tanh(pre * (gelu_a + gelu_b * square))
                half = 0.5 + 0.5 * level
                act = (pre * half).astype(bf16)
                slope = half + (0.5 * pre) * (1.0 - level * level) * (gelu_a + 3.0 * gelu_b * square)
                d_act = dot_nt(buf_g[far, :], wo)
                d_pre = (d_act * slope).astype(bf16)
                act_s[rows, :] = act
                dpre_s[rows, :] = d_pre
                acc[rows, :] += dot(act, wo)
                acc[rows_r, :] += dot_nt(d_pre, wi)
            for odd in range(2):
                cols = slice(odd * CHUNK, (odd + 1) * CHUNK)
                grad_out = dot_tn(act_s[0:half_places, cols], buf_g[whole, :])
                grad_in = dot(turned_x[...], dpre_s[0:half_places, cols]).reshape(2, 2, 2, SHARE_IN, CHUNK)
                out_at = (el, k // 2, lax.rem(k, 2), odd)
                in_at = 2 * step + odd
                if pass_id == 1:
                    grad_out = grad_out + dwo[out_at].astype(f32)
                    grad_in = grad_in + dwi[in_at].astype(f32)
                dwo[out_at] = grad_out.astype(bf16)
                dwi[in_at] = grad_in.astype(bf16)
            for when, what in extra:

                @pl.when(step == when)
                def _(what=what):
                    what()

            @pl.when(k == STEPS - 1)
            def _():
                buf_x[whole, :] = acc[0:half_places, :].astype(bf16)
                buf_g[whole, :] = acc[half_places:, :].astype(bf16)

            return carry

        lax.fori_loop(0, 2 * STEPS, expert_step, 0)

    expert_pass(
        0,
        [
            (0, lambda: gather_forward(0, 1)),
            (2, lambda: gather_forward(0, 2)),
            (4, lambda: gather_forward(0, 3)),
            (5, lambda: gather_forward(1, 0)),
            (7, lambda: gather_forward(1, 1)),
        ],
    )

    partial = (dy_all, hid_all)

    def ret_one(kind, which, who):
        return remote(partial[kind].at[who], rret1.at[kind, which], p1_s, p1_r.at[kind, which], mate)

    def ret_two(kind, i):
        rows = image_rows(i)
        return remote(partial[kind].at[mirror_e, rows], rret2.at[kind, rows], p2_s, p2_r.at[kind, i], mirror)

    def gate_one(which, who):
        return remote(dgp.at[who], rdg1.at[which], q1_s, q1_r.at[which], mate)

    def gate_two():
        return remote(dgp.at[mirror_e], rdg2, q2_s, q2_r, mirror)

    turned = (act_s, dpre_s)

    def turn(pass_id, index):
        cols = slice(index * CHUNK, (index + 1) * CHUNK)
        for el in range(2):
            turned[el][:, cols] = hot_of(hits(sources[pass_id][index], el)).T

    def to_rows(pass_id, index, source, target):
        cols = slice(index * CHUNK, (index + 1) * CHUNK)
        s = sources[pass_id][index]

        def rows_of_image(i, carry):
            rows = image_rows(i)
            value = dot(act_s[rows, cols], source[slot_rows(pass_id, 0, index), :])
            value = value + dot(dpre_s[rows, cols], source[slot_rows(pass_id, 1, index), :])
            target[s, rows, :] = value.astype(bf16)
            return carry

        lax.fori_loop(0, IMAGES, rows_of_image, 0)

    def return_source(pass_id, index):
        s = sources[pass_id][index]
        turn(pass_id, index)
        gate_total = [None, None]
        for el in range(2):
            hit = hits(s, el)
            rows = slot_rows(pass_id, el, index)
            result = buf_x[rows, :].astype(f32)
            d_slot = jnp.sum(result * buf_y[rows, :].astype(f32), -1, keepdims=True)
            buf_x[rows, :] = (slot_gate(s, hit) * result).astype(bf16)
            for c in range(2):
                term = jnp.sum(jnp.where(hit[c], d_slot, 0.0), 0, keepdims=True)
                gate_total[c] = term if el == 0 else gate_total[c] + term
        dgp[s] = jnp.zeros((8, ROWS), f32)
        for c in range(2):
            dgp[s, c : c + 1, :] = gate_total[c]
        to_rows(pass_id, index, buf_g, dy_all)

    return_source(0, 1)
    gate_one(0, mate_e).start()
    ret_one(0, 0, mate_e).start()
    gather_forward(1, 2)
    return_source(0, 0)
    gather_forward(1, 3)
    here = meta.at[mirror_e]
    remote(here, here, m_s.at[1], m_r.at[1], mirror).wait_recv()
    remote(here, here, m_s.at[2], m_r.at[2], mate).start()
    place_one(1, 0, 0)
    for kind in range(2):
        gather_far(kind)
    remote(meta.at[diag_e], meta.at[diag_e], m_s.at[2], m_r.at[2], mate).wait_recv()
    for route in range(3):
        remote(meta.at[ep], meta.at[ep], m_s.at[route], m_r.at[route], mate).wait_send()
    place_one(1, 1, 0)
    expert_pass(
        1,
        [
            (0, lambda: go("O0", "D0")),
            (1, lambda: go("O1", "D1")),
            (2, lambda: go("O2", "D2")),
            (3, lambda: (go("D3"), place_one(1, 0, 1), place_one(1, 1, 1))),
            (4, lambda: go("D4", "o0")),
            (5, lambda: go("D5")),
            (6, lambda: go("D6", "o1")),
            (7, lambda: go("D7")),
        ],
    )
    return_source(1, 1)
    gate_one(1, diag_e).start()
    ret_one(0, 1, diag_e).start()
    go("d0", "d1", "o2")
    return_source(1, 0)
    gate_one(1, diag_e).wait_recv()
    dgp[mirror_e] = dgp[mirror_e] + rdg1[1]
    gate_two().start()

    def cross(kind, i):
        rows = slice(i * PAD, (i + 1) * PAD)
        partial[kind][mirror_e, rows, :] = plus(partial[kind][mirror_e, rows, :], rret1[kind, 1, rows, :])
        ret_two(kind, i).start()

    ret_one(0, 1, diag_e).wait_recv()
    for i in range(IMAGES):
        cross(0, i)
    to_rows(1, 1, buf_x, hid_all)
    ret_one(1, 1, diag_e).start()
    turn(0, 1)
    to_rows(0, 1, buf_x, hid_all)
    ret_one(1, 0, mate_e).start()
    to_rows(1, 0, buf_x, hid_all)
    turn(0, 0)
    to_rows(0, 0, buf_x, hid_all)
    go("d2", "d3", "o3", "K0")

    gate_one(0, mate_e).wait_recv()
    gate_two().wait_recv()
    d_gate = dgp[ep] + rdg1[0] + rdg2[...]
    spread = None
    for c, hot in enumerate(picks()):
        term = hot * jnp.where(meta_in[10 + c : 11 + c, :] < CAP, d_gate[c : c + 1, :], 0.0)
        spread = term if spread is None else spread + term
    gate_rows = gates[...]
    d_logits = (gate_rows * (spread - jnp.sum(gate_rows * spread, 0, keepdims=True))).astype(bf16)
    padf[...] = dot_tn(d_logits, wrt[...])
    sm[0, 0:8, :] = jnp.zeros((8, WIDTH), f32)
    sm[0, 8:16, :] = dot(d_logits, hid_own[...])
    for kind in range(2):
        ret_one(kind, 0, mate_e).wait_recv()

    def backward_image(i, carry):
        rows = image_rows(i)
        ret_two(0, i).wait_recv()
        d_hidden = (
            padf[rows, :]
            + dy_all[ep, rows, :].astype(f32)
            + rret1[0, 0, rows, :].astype(f32)
            + rret2[0, rows, :].astype(f32)
        )
        unit2, scale2 = normalized(resid[rows, :])
        sm[0, 1:2, :] += jnp.sum(d_hidden * unit2, 0, keepdims=True)
        d_residual = dy_own[rows, :].astype(f32) + norm_back(unit2, scale2, gain2[...], d_hidden)
        padf[rows, :] = d_residual
        d_branch = d_residual.astype(bf16)
        hid_own[rows, :] = d_branch
        da_temp[...] = dot_nt(d_branch, wproj[...]).astype(bf16)
        for pair in range(PAIRS):
            queries = proj[rows, columns(0, pair)] * jnp.array(score_scale, bf16)
            keys = proj[rows, columns(1, pair)]
            values = proj[rows, columns(2, pair)]
            d_att = da_temp[:, columns(0, pair)]
            d_q = d_k = d_v = None
            for mask in masks:
                own_keys = keys * mask
                chance = softmax_of(queries, own_keys)
                d_chance = dot_nt(d_att, values * mask)
                both = chance * d_chance
                d_scores = (both - chance * jnp.sum(both, -1, keepdims=True)).astype(bf16)
                t_q = dot(d_scores, own_keys)
                t_k = dot_tn(d_scores, queries * mask)
                t_v = dot_tn(chance.astype(bf16), d_att * mask)
                d_q = t_q if d_q is None else d_q + t_q
                d_k = t_k if d_k is None else d_k + t_k
                d_v = t_v if d_v is None else d_v + t_v
            proj[rows, columns(0, pair)] = (d_q * score_scale).astype(bf16)
            proj[rows, columns(1, pair)] = d_k.astype(bf16)
            proj[rows, columns(2, pair)] = d_v.astype(bf16)
        d_normed = dot_nt(proj[rows, :], wqkv[...])
        unit, scale = normalized(tok_p[rows, :].astype(f32))
        sm[0, 0:1, :] += jnp.sum(d_normed * unit, 0, keepdims=True)
        padf[rows, :] += norm_back(unit, scale, gain1[...], d_normed)
        tok_p[rows, :] = (unit * gain1[...]).astype(bf16)
        for when, what in (
            (0, lambda: (go("d4", "d5", "d6", "d7", "o4", "p0", "K1"),)),
            (1, lambda: (go("o5", "p1", "r0", "r1", "r2", "r3", "E0"), ret_one(1, 1, diag_e).wait_recv(), cross(1, 0), go("K2"),)),
            (2, lambda: (go("o6", "E1", "K3", "E2"),)),
            (3, lambda: (go("c0", "o7"),)),
        ):

            @pl.when(i == when)
            def _(what=what):
                what()

        return carry

    lax.fori_loop(0, IMAGES, backward_image, 0)

    for part in range(3):
        for half in range(2):
            cols = slice(part * WIDTH + half * 256, part * WIDTH + (half + 1) * 256)
            buf_x[part * WIDTH : (part + 1) * WIDTH, half * 256 : (half + 1) * 256] = dot_tn(
                tok_p[...], proj[:, cols]
            ).astype(bf16)
    for half in range(2):
        cols = slice(half * 256, (half + 1) * 256)
        buf_x[3 * WIDTH : 4 * WIDTH, cols] = dot_tn(att[...], hid_own[:, cols]).astype(bf16)

    plane = ((1 - bx, bz, dev_x), (bx, 1 - bz, dev_z), (1 - bx, 1 - bz, dev_xz))

    def half_at(chunk, bit):
        return pl.ds(pl.multiple_of(chunk * WIDTH + bit * 256, 256), 256)

    def quarter_at(chunk, bit):
        return pl.ds(pl.multiple_of(chunk * WIDTH + core * 256 + bit * 128, 128), 128)

    def plane_at(chunk, x, z):
        return pl.ds(pl.multiple_of(chunk * WIDTH + core * 256 + yy * 128 + z * 64 + x * 32, 32), 32)

    def piece_at(chunk, bit):
        start = chunk * WIDTH + core * 256 + yy * 128 + bz * 64 + bx * 32 + bit * 16
        return pl.ds(pl.multiple_of(start, 16), 16)

    def sum_core(chunk):
        return remote(buf_x.at[half_at(chunk, 1 - core)], rg_c.at[chunk], ar_s.at[0], ar_r.at[chunk, 0], mate)

    def sum_y(chunk):
        return remote(buf_x.at[quarter_at(chunk, 1 - yy)], rg_y.at[chunk], ar_s.at[1], ar_r.at[chunk, 1], mirror)

    def sum_plane(chunk):
        return [
            remote(buf_x.at[plane_at(chunk, x, z)], rg_d.at[chunk, n], ad_s.at[0], ad_r.at[chunk, 0], device)
            for n, (x, z, device) in enumerate(plane)
        ]

    def sum_w(chunk):
        return remote(buf_x.at[piece_at(chunk, 1 - bw)], rg_w.at[chunk], ar_s.at[2], ar_r.at[chunk, 2], dev_w)

    def spread_w(chunk, bit):
        here = buf_g.at[piece_at(chunk, bit)]
        return remote(here, here, ar_s.at[3], ar_r.at[chunk, 3], dev_w)

    def spread_plane(chunk):
        copies = []
        here = buf_g.at[plane_at(chunk, bx, bz)]
        for _, _, device in plane:
            copies.append(remote(here, here, ad_s.at[1], ad_r.at[chunk, 1], device))
        return copies

    def spread_y(chunk, bit):
        here = buf_g.at[quarter_at(chunk, bit)]
        return remote(here, here, ar_s.at[4], ar_r.at[chunk, 4], mirror)

    def spread_core(chunk, bit):
        here = buf_g.at[half_at(chunk, bit)]
        return remote(here, here, ar_s.at[5], ar_r.at[chunk, 5], mate)

    def dense_out(chunk):
        rows = slice(chunk * WIDTH, (chunk + 1) * WIDTH)
        return pltpu.make_async_copy(buf_g.at[rows], dense_g.at[rows], o_sem.at[chunk])

    def do_c(chunk):
        sum_core(chunk).wait_recv()
        keep = half_at(chunk, core)
        buf_x[keep, :] = plus(buf_x[keep, :], rg_c[chunk])
        sum_y(chunk).start()

    def do_y(chunk):
        sum_y(chunk).wait_recv()
        keep = quarter_at(chunk, yy)
        buf_x[keep, :] = plus(buf_x[keep, :], rg_y[chunk])
        for copy in sum_plane(chunk):
            copy.start()

    def do_plane(chunk):
        remote(rg_d.at[chunk], rg_d.at[chunk], ad_s.at[0], ad_r.at[chunk, 0], dev_x).wait_recv()
        keep = plane_at(chunk, bx, bz)
        total = buf_x[keep, :].astype(f32)
        for n in range(3):
            total = total + rg_d[chunk, n].astype(f32)
        buf_x[keep, :] = total.astype(bf16)
        sum_w(chunk).start()

    def do_w(chunk):
        sum_w(chunk).wait_recv()
        keep = piece_at(chunk, bw)
        buf_g[keep, :] = plus(buf_x[keep, :], rg_w[chunk])
        spread_w(chunk, bw).start()

    def do_aw(chunk):
        spread_w(chunk, 1 - bw).wait_recv()
        for copy in spread_plane(chunk):
            copy.start()

    def do_aplane(chunk):
        remote(rg_d.at[chunk], rg_d.at[chunk], ad_s.at[1], ad_r.at[chunk, 1], dev_x).wait_recv()
        spread_y(chunk, yy).start()

    def do_ay(chunk):
        spread_y(chunk, 1 - yy).wait_recv()
        spread_core(chunk, core).start()

    def do_ac(chunk):
        spread_core(chunk, 1 - core).wait_recv()
        dense_out(chunk).start()

    little_way = (mate, mirror, dev_x, dev_z, dev_w)

    def little_copy(level):
        return remote(sm.at[level], rsm.at[level], sr_s, sr_r.at[level], little_way[level])

    def little(level):
        little_copy(level).wait_recv()
        sm[level + 1] = sm[level] + rsm[level]
        if level < 4:
            little_copy(level + 1).start()

    def unpad_grad():
        for i in range(IMAGES):
            ig[SEQ * i : SEQ * i + SEQ, :] = padf[i * PAD : i * PAD + SEQ, :]

    def finish_rows():
        sent(rret1, p1_s)
        sent(rret2, p2_s)
        sent(rdg1, q1_s)
        sent(rdg2, q2_s)
        for n, like in enumerate((ri1.at[0:8], ri2.at[0:8], ri1.at[0:8], ri2.at[0:8])):
            sent(like, rs_s.at[n])
        sent(ro1, rs_s.at[5])
        sent(ro2, rs_s.at[6])
        sent(rsm, sr_s)
        for n, like in enumerate((rg_c, rg_y, rg_w, rg_w)):
            sent(like, ar_s.at[n])
        for n in range(2):
            sent(rg_d, ad_s.at[n])
        for i in range(IMAGES):
            rows = slice(i * PAD, (i + 1) * PAD)
            ret_two(1, i).wait_recv()
            value = (
                resid[rows, :]
                + hid_all[ep, rows, :].astype(f32)
                + rret1[1, 0, rows, :].astype(f32)
                + rret2[1, rows, :].astype(f32)
            )
            acc[SEQ * i : SEQ * i + SEQ, :] = value[0:SEQ, :]
        out[...] = acc[0:788, :].astype(bf16)

    for chunk in range(4):
        sum_core(chunk).start()
    little_copy(0).start()
    unpad_grad()
    pltpu.make_async_copy(ig, ig_g, f_sem.at[0]).start()
    moves.update({
        "Y": do_y, "P": do_plane, "W": do_w, "A": do_aw, "B": do_aplane, "G": do_ay, "C": do_ac,
        "S": do_c, "L": little, "X": lambda n: cross(1, n),
    })
    go("S0", "S1", "S2", "S3", "E3", "c1", "L0", "e0", "p2", "Y0", "e1", "E4", "Y1", "p3")
    go("r4", "P0", "X1", "e2", "E5", "f0", "c2", "Y2", "P1", "W0", "L1", "f1", "X2", "Y3")
    go("r5", "e3", "E6", "P2", "W1", "A0", "f2", "X3", "P3", "W2", "A1", "L2", "e4", "E7")
    go("B0", "W3", "A2", "r6", "e5", "f3", "c3", "K4", "A3", "L3", "B1", "G0", "e6", "K5")
    go("f4", "c4", "r7", "B2", "G1", "C0", "e7", "K6", "f5", "c5", "L4", "h0", "K7", "f6")
    go("g0", "B3", "C1", "G2", "f7", "c6", "C2", "G3", "c7", "C3")
    finish_rows()
    pltpu.make_async_copy(out, out_g, f_sem.at[1]).start()
    go("q0", "q1", "g1", "h1")
    small_g[...] = sm[5]
    pltpu.make_async_copy(ig, ig_g, f_sem.at[0]).wait()
    pltpu.make_async_copy(out, out_g, f_sem.at[1]).wait()

    sent(ri3, rs_s.at[4])
    sent(ro3, rs_s.at[7])
    sent(rg_y, ar_s.at[4])
    sent(rg_c, ar_s.at[5])
    for chunk in range(4):
        dense_out(chunk).wait()
    for n in range(2):
        pltpu.make_async_copy(ri3, ri3, li_sem.at[n]).wait()
        pltpu.make_async_copy(ro3, ro3, lo_sem.at[n]).wait()


def finish_kernel(
    out_in, ig_in, dense_in, small_in, win_a, win_b, wout_a, wout_b,
    out, ig, gain1_g, qkv_g, proj_g, gain2_g, router_g, win_g, wout_g,
    dense, small, in_a, in_b, out_a, out_b, qkv, projected, in_sum, out_sum, rows_f, rows_b, sems, leave,
):
    parts = [slice(part * WIDTH, (part + 1) * WIDTH) for part in range(4)]
    pairs = [(small_in, small)] + [(dense_in.at[rows], dense.at[rows]) for rows in parts]
    pairs += [(win_a, in_a), (win_b, in_b), (wout_a, out_a), (wout_b, out_b), (ig_in, rows_f), (out_in, rows_b)]
    fetch = [pltpu.make_async_copy(a, b, sems.at[n]) for n, (a, b) in enumerate(pairs)]
    for copy in fetch:
        copy.start()
    put = [
        pltpu.make_async_copy(a, b, leave.at[n])
        for n, (a, b) in enumerate(
            (
                (in_sum, win_g), (out_sum, wout_g), (projected, proj_g), (rows_f, ig), (rows_b, out), (qkv, qkv_g),
            )
        )
    ]
    fetch[0].wait()
    gain1_g[...] = small[0, :]
    gain2_g[...] = small[1, :]
    router_g[...] = small[8:16, :]
    for part, rows in enumerate(parts[:3]):
        fetch[1 + part].wait()
        qkv[:, rows] = dense[rows, :].astype(f32)
    put[5].start()
    fetch[4].wait()
    projected[...] = dense[3 * WIDTH :, :].astype(f32)
    put[2].start()
    fetch[5].wait()
    fetch[6].wait()
    in_sum[...] = in_a[...].astype(f32) + in_b[...].astype(f32)
    put[0].start()
    fetch[7].wait()
    fetch[8].wait()
    out_sum[...] = out_a[...].astype(f32) + out_b[...].astype(f32)
    put[1].start()
    fetch[9].wait()
    put[3].start()
    fetch[10].wait()
    put[4].start()
    for copy in put:
        copy.wait()


def fused(
    tokens, ln1_gain, w_qkv, w_proj, ln2_gain, w_router, w_in, w_out, noise, choices, slots, cotangent
):
    vmem = pl.BlockSpec(memory_space=pltpu.VMEM)
    anywhere = pl.BlockSpec(memory_space=pl.ANY)
    dma = pltpu.SemaphoreType.DMA
    v = pltpu.VMEM
    rows = (ROWS, WIDTH)
    scratch = [
        v((WIDTH, 3 * WIDTH), bf16), v((WIDTH, WIDTH), bf16), v((16, 896), f32), v((16, ROWS), f32),
        v((788, WIDTH), bf16), v((788, WIDTH), f32),
        v(rows, f32), v(rows, bf16), v(rows, bf16), v(rows, bf16), v((ROWS, 3 * WIDTH), bf16), v(rows, bf16),
        v(rows, f32), v((PAD, WIDTH), bf16), v((8, ROWS), f32), v((4, 8, ROWS), f32),
        v((4, *rows), bf16), v((4, *rows), bf16),
        v((2 * PLACES, WIDTH), bf16), v((2 * PLACES, WIDTH), bf16), v((2 * PLACES, WIDTH), bf16),
        v((2, WIDTH, WIDE), bf16), v((2, WIDE, WIDTH), bf16),
        v((ROWS, WIDE), bf16), v((ROWS, WIDE), bf16), v((PLACES, WIDTH), f32), v((WIDTH, 2 * SLOT_PAD), bf16),
        v((2 * CHUNKS, 2, 2, 2, SHARE_IN, CHUNK), bf16), v((2, 2, 2, 2, CHUNK, WIDTH), bf16),
        v((2 * CHUNKS, 2, 2, SHARE_IN, CHUNK), bf16), v((2 * CHUNKS, 2, SHARE_IN, CHUNK), bf16),
        v((2 * CHUNKS, SHARE_IN, CHUNK), bf16),
        v((UNITS, CHUNK, WIDTH), bf16), v((2, 2, CHUNK, WIDTH), bf16), v((2, CHUNK, WIDTH), bf16),
        v((2, 2, *rows), bf16), v((2, *rows), bf16),
        v((4, 8, ROWS), f32), v((2, 8, ROWS), f32), v((8, ROWS), f32),
        v((4, 256, WIDTH), bf16), v((4, 128, WIDTH), bf16), v((4, 3, 32, WIDTH), bf16), v((4, 16, WIDTH), bf16), v((6, 16, WIDTH), f32), v((5, 16, WIDTH), f32),
        dma((4,)), dma((2, 2)), dma((4,)), dma((2,)), dma((2,)),
        dma((2,)), dma((2, IMAGES)), dma((2,)), dma((2,)), dma((3,)), dma((3,)),
        dma, dma((2, 2)), dma, dma((2, IMAGES)), dma, dma((2,)), dma, dma,
        dma((8,)), dma((4, UNITS)), dma((2, 2)), dma((UNITS,)), dma((2, 2)), dma((2,)),
        dma((6,)), dma((4, 6)), dma((2,)), dma((4, 2)), dma, dma((5,)),
    ]
    share_in = jax.ShapeDtypeStruct((2, SHARE_IN, CHUNK * CHUNKS), bf16)
    share_out = jax.ShapeDtypeStruct((2, CHUNK, WIDTH), bf16)
    results = pl.pallas_call(
        block_kernel,
        out_shape=(
            jax.ShapeDtypeStruct((788, WIDTH), bf16),
            jax.ShapeDtypeStruct((788, WIDTH), f32),
            jax.ShapeDtypeStruct((4 * WIDTH, WIDTH), bf16),
            jax.ShapeDtypeStruct((16, WIDTH), f32),
            share_in, share_in, share_out, share_out,
        ),
        in_specs=[anywhere] * 2 + [vmem] * 2 + [anywhere] * 2 + [vmem] * 4 + [anywhere] * 2,
        out_specs=(anywhere, anywhere, anywhere, vmem) + (anywhere,) * 4,
        scratch_shapes=scratch,
        compiler_params=pltpu.CompilerParams(
            collective_id=0, has_side_effects=True, vmem_limit_bytes=61 << 20
        ),
        name="block",
    )(
        tokens, cotangent, ln1_gain[None, :], ln2_gain[None, :], w_qkv, w_proj, w_router.T,
        noise.T, choices.T, slots.T, w_in, w_out
    )
    ended = pl.pallas_call(
        finish_kernel,
        out_shape=(
            jax.ShapeDtypeStruct((788, WIDTH), bf16),
            jax.ShapeDtypeStruct((788, WIDTH), f32),
            jax.ShapeDtypeStruct((WIDTH,), f32),
            jax.ShapeDtypeStruct((WIDTH, 3 * WIDTH), f32),
            jax.ShapeDtypeStruct((WIDTH, WIDTH), f32),
            jax.ShapeDtypeStruct((WIDTH,), f32),
            jax.ShapeDtypeStruct((8, WIDTH), f32),
            jax.ShapeDtypeStruct((2, SHARE_IN, CHUNK * CHUNKS), f32),
            jax.ShapeDtypeStruct((2, CHUNK, WIDTH), f32),
        ),
        in_specs=[anywhere] * 8,
        out_specs=(anywhere, anywhere, vmem, anywhere, anywhere, vmem, vmem, anywhere, anywhere),
        scratch_shapes=[
            v((4 * WIDTH, WIDTH), bf16), v((16, WIDTH), f32),
            v((2, SHARE_IN, CHUNK * CHUNKS), bf16), v((2, SHARE_IN, CHUNK * CHUNKS), bf16),
            v((2, CHUNK, WIDTH), bf16), v((2, CHUNK, WIDTH), bf16),
            v((WIDTH, 3 * WIDTH), f32), v((WIDTH, WIDTH), f32),
            v((2, SHARE_IN, CHUNK * CHUNKS), f32), v((2, CHUNK, WIDTH), f32),
            v((788, WIDTH), f32), v((788, WIDTH), bf16), dma((11,)), dma((6,)),
        ],
        compiler_params=pltpu.CompilerParams(vmem_limit_bytes=60 << 20),
        name="finish",
    )(*results)
    return (*ended[:6], ended[6].T, *ended[7:])


def solution(mesh):
    in_specs = (
        P(("rep", "ep"), None),
        P(),
        P(),
        P(),
        P(),
        P(),
        P("ep", None, None),
        P("ep", None, None),
        P(("rep", "ep"), None),
        P(("rep", "ep"), None),
        P(("rep", "ep"), None),
        P(("rep", "ep"), None),
    )
    out_specs = (
        P(("rep", "ep"), None),
        P(("rep", "ep"), None),
        P(),
        P(),
        P(),
        P(),
        P(),
        P("ep", "rep", None),
        P("ep", "rep", None),
    )
    whole = fused if dict(mesh.shape) == {"rep": 8, "ep": 4} else local
    return jax.shard_map(whole, mesh=mesh, in_specs=in_specs, out_specs=out_specs, check_vma=False)
```
